32 devices in a mesh: dp: 4 (over y, x), fsdp: 8 (over z, core).
Axes of the slice: x: 2, y: 2, z: 4, core: 2. Of those that a mesh axis runs over, the one named last changes fastest.
Arguments:
- full_input: bfloat16 [32, 256, 1152], P(('dp', 'fsdp')), may hold values from -6 to 6
- masked_input: bfloat16 [32, 256, 1152], P(('dp', 'fsdp')), may hold values from -6 to 6
- keep_index: int32 [32, 128], P(('dp', 'fsdp')), may hold values from 0 to 255, as said below
- cond_full: bfloat16 [32, 1152], P(('dp', 'fsdp')), may hold values from -6 to 6
- cond_masked: bfloat16 [32, 1152], P(('dp', 'fsdp')), may hold values from -6 to 6
- w_ada: bfloat16 [1152, 6912], P('dp', 'fsdp'), may hold values from -0.1875 to 0.1875
- b_ada: bfloat16 [6912], P('fsdp'), may hold values from -4 to 4
- w_qkv: bfloat16 [1152, 3456], P('dp', 'fsdp'), may hold values from -0.1875 to 0.1875
- b_q: bfloat16 [1152], P('fsdp'), may hold values from -6 to 6
- b_v: bfloat16 [1152], P('fsdp'), may hold values from -6 to 6
- w_out: bfloat16 [1152, 1152], P('dp', 'fsdp'), may hold values from -0.75 to 0.75
- b_out: bfloat16 [1152], P('fsdp'), may hold values from -4 to 4
- w_fc1: bfloat16 [1152, 4608], P('dp', 'fsdp'), may hold values from -0.1875 to 0.1875
- b_fc1: bfloat16 [4608], P('fsdp'), may hold values from -4 to 4
- w_fc2: bfloat16 [4608, 1152], P('dp', 'fsdp'), may hold values from -0.09375 to 0.09375
- b_fc2: bfloat16 [1152], P('fsdp'), may hold values from -4 to 4
- cot_full: bfloat16 [32, 256, 1152], P(('dp', 'fsdp')), may hold values from -6 to 6
- cot_masked: bfloat16 [32, 128, 1152], P(('dp', 'fsdp')), may hold values from -6 to 6
Outputs:
- out_full: bfloat16 [32, 256, 1152], P(('dp', 'fsdp'))
- out_masked: bfloat16 [32, 128, 1152], P(('dp', 'fsdp'))
- grad_full: float32 [32, 256, 1152], P(('dp', 'fsdp'))
- grad_masked: float32 [32, 256, 1152], P(('dp', 'fsdp'))
- grad_cond_full: float32 [32, 1152], P(('dp', 'fsdp'))
- grad_cond_masked: float32 [32, 1152], P(('dp', 'fsdp'))
- grad_w_ada: float32 [1152, 6912], P('dp', 'fsdp')
- grad_b_ada: float32 [6912], P('fsdp')
- grad_w_qkv: float32 [1152, 3456], P('dp', 'fsdp')
- grad_b_q: float32 [1152], P('fsdp')
- grad_b_v: float32 [1152], P('fsdp')
- grad_w_out: float32 [1152, 1152], P('dp', 'fsdp')
- grad_b_out: float32 [1152], P('fsdp')
- grad_w_fc1: float32 [1152, 4608], P('dp', 'fsdp')
- grad_b_fc1: float32 [4608], P('fsdp')
- grad_w_fc2: float32 [4608, 1152], P('dp', 'fsdp')
- grad_b_fc2: float32 [1152], P('fsdp')
The draws below stay inside these ranges and needn't reach their ends.
Inputs may be any that keep to these rules, and one draw needn't show every extreme that they name: `keep_index`: each row holds 128 distinct positions of one image in increasing order.
All inputs are finite; a program needn't handle non-finite values.
Results may differ from the reference program's by a relative error of at most 0.02.
Values may be sent and summed in bfloat16 or wider, within the bound.
A program may use at most 256 MiB of HBM per device.

```python
import math
import jax
import jax.numpy as jnp
from jax import lax

D = 1152
HEADS = 16
HEAD_DIM = 72
FF = 4608
SEQ = 256
KEEP = 128
HALF = 32


def draw_keep_index(key, part):
    key = jax.random.fold_in(key, 11)
    row_keys = jax.random.split(key, HALF)
    picks = jax.vmap(lambda single: jax.random.permutation(single, SEQ)[:KEEP])(row_keys)
    return jnp.sort(picks, axis=1).astype(jnp.int32)


def raised(entries, own_key, source, target, shards_of, factor):
    owner, partner = [(jnp.arange(entries.shape[axis_at]) // (entries.shape[axis_at] // shards_of)).reshape([-1 if axis == axis_at else 1 for axis in range(entries.ndim)]) for axis_at in (source, target)]
    chosen = jax.random.permutation(own_key, shards_of)[partner]
    strong = (owner == chosen) | (owner == (partner + shards_of // 2) % shards_of)
    return jnp.where(strong, factor * entries, entries)


def block_scale(rng, extent, cuts, smallest, high):
    def one(axis_at, parts):
        heights = jax.random.uniform(jax.random.fold_in(jax.random.fold_in(rng, 6), axis_at), (parts,), jnp.float32, smallest / len(cuts), high / len(cuts))
        return jnp.repeat(jnp.exp(heights), extent[axis_at] // parts).reshape((-1,) + (1,) * (len(extent) - axis_at - 1))

    loudness = one(*cuts[0])
    for cut in cuts[1:]:
        loudness = loudness * one(*cut)
    return loudness


def bell_draw(rng, extent, deviation, bound, shards=(), held_as=jnp.bfloat16):
    drawn = jax.random.normal(rng, extent, jnp.float32) * deviation
    if len(shards) > 0:
        drawn = block_scale(rng, extent, shards, -0.22, 0.18) * drawn
    return jnp.clip(drawn, min=-bound, max=bound).astype(held_as)


def heavy_noise(rng, dims, spread, limit, cuts, heavy, dtype=jnp.bfloat16):
    values = spread * jax.random.normal(rng, dims, jnp.float32)
    if cuts:
        values = values * block_scale(rng, dims, cuts, -0.22, 0.18)
    return jnp.clip(raised(values, jax.random.fold_in(rng, 3), *heavy), -limit, limit).astype(dtype)


def setup_inputs(seed: int = 0) -> dict:
    key_of = jax.random.split(jax.random.key(seed), 19)
    return {
        "full_input": bell_draw(key_of[0], (HALF, SEQ, D), 1.0, 6.0, ((0, 32),)),
        "masked_input": bell_draw(key_of[1], (HALF, SEQ, D), 1.0, 6.0, ((0, 32),)),
        "keep_index": draw_keep_index(jax.random.fold_in(key_of[18], 71), 0),
        "cond_full": bell_draw(key_of[3], (HALF, D), 1.0, 6.0, ((0, 32),)),
        "cond_masked": bell_draw(key_of[4], (HALF, D), 1.0, 6.0, ((0, 32),)),
        "w_ada": bell_draw(key_of[5], (D, 6 * D), D ** -0.5, 0.1875, ((0, 4), (1, 8))),
        "b_ada": bell_draw(key_of[6], (6 * D,), 0.3, 4.0, ((0, 8),)),
        "w_qkv": bell_draw(key_of[7], (D, 3 * D), D ** -0.5, 0.1875, ((0, 4), (1, 8))),
        "b_q": bell_draw(key_of[8], (D,), 0.5, 6.0, ((0, 8),)),
        "b_v": bell_draw(key_of[9], (D,), 0.5, 6.0, ((0, 8),)),
        "w_out": bell_draw(key_of[10], (D, D), HEAD_DIM ** -0.5, 0.75, ((0, 4), (1, 8))),
        "b_out": bell_draw(key_of[11], (D,), 0.3, 4.0, ((0, 8),)),
        "w_fc1": bell_draw(key_of[12], (D, FF), D ** -0.5, 0.1875, ((0, 4), (1, 8))),
        "b_fc1": bell_draw(key_of[13], (FF,), 0.3, 4.0, ((0, 8),)),
        "w_fc2": bell_draw(key_of[14], (FF, D), FF ** -0.5, 0.09375, ((0, 4), (1, 8))),
        "b_fc2": bell_draw(key_of[15], (D,), 0.3, 4.0, ((0, 8),)),
        "cot_full": heavy_noise(key_of[16], (HALF, SEQ, D), 1.0, 6.0, ((0, 32),), (0, 2, 32, 2.75)),
        "cot_masked": heavy_noise(key_of[17], (HALF, KEEP, D), 1.0, 6.0, ((0, 32),), (0, 2, 32, 2.75)),
    }


@jax.custom_vjp
def low(v):
    return lax.optimization_barrier(v.astype(jnp.bfloat16)).astype(jnp.float32)

@jax.custom_vjp
def low_back(v):
    return v

def low_keep(v):
    return (low(v), None)

def low_pass(kept, grad):
    return (grad,)

def back_keep(v):
    return (v, None)

def back_low(kept, grad):
    return (low(grad),)
low.defvjp(low_keep, low_pass)
low_back.defvjp(back_keep, back_low)

def product(spec, left, right):
    return jnp.einsum(spec, left, right, precision=lax.Precision.HIGHEST)

def layer_norm(values):
    centered = values - lax.optimization_barrier(jnp.mean(values, axis=-1, keepdims=True))
    return centered * lax.rsqrt(lax.optimization_barrier(jnp.mean(centered * centered, axis=-1, keepdims=True)) + 1e-06)

def spread_mods(piece):
    groups = piece.shape[0]
    head_part = jnp.broadcast_to(piece[:, 0:1], (groups, SEQ, D))
    tail_part = jnp.broadcast_to(piece[:, 1:2], (groups, KEEP, D))
    return jnp.concatenate([head_part, tail_part], axis=1)

def block_group(bundle, params):
    full_rows, masked_rows, kept_rows, cond_pair = bundle
    w_ada, b_ada, w_qkv, b_q, b_v, w_out, b_out, w_fc1, b_fc1, w_fc2, b_fc2 = params
    picked = jnp.take_along_axis(masked_rows, kept_rows[:, :, None], axis=1)
    tokens = jnp.concatenate([full_rows, picked], axis=1)
    groups = tokens.shape[0]
    length = SEQ + KEEP
    mods = low_back(product('gid,de->gie', low(jax.nn.silu(cond_pair)), w_ada) + b_ada)
    pieces = [spread_mods(mods[:, :, column * D:(column + 1) * D]) for column in range(6)]
    shift_one, scale_one, gate_one, shift_two, scale_two, gate_two = pieces
    hidden_one = low(layer_norm(tokens) * (1.0 + scale_one) + shift_one)
    bias_all = jnp.concatenate([b_q, jnp.zeros((D,), jnp.float32), b_v])
    projected = low(low_back(product('gtd,de->gte', hidden_one, w_qkv) + bias_all))
    projected = projected.reshape(groups, length, 3, HEADS, HEAD_DIM)
    scale_factor = 1.0 / math.sqrt(HEAD_DIM)
    scores = low_back(product('gqhc,gkhc->ghqk', projected[:, :, 0], projected[:, :, 1]) * scale_factor)
    marker = jnp.arange(length) >= SEQ
    same_image = marker[:, None] == marker[None, :]
    scores = jnp.where(same_image, scores, -1e+30)
    row_max = lax.optimization_barrier(jnp.max(scores, axis=-1, keepdims=True))
    exponent = jnp.exp(scores - row_max)
    attention = exponent / lax.optimization_barrier(jnp.sum(exponent, axis=-1, keepdims=True))
    mixed = low(low_back(product('ghqk,gkhc->gqhc', low(attention), projected[:, :, 2])))
    mixed = mixed.reshape(groups, length, D)
    attn_out = low_back(product('gtd,de->gte', mixed, w_out) + b_out)
    residual = tokens + gate_one * attn_out
    hidden_two = low(layer_norm(residual) * (1.0 + scale_two) + shift_two)
    upper = low_back(product('gtd,df->gtf', hidden_two, w_fc1) + b_fc1)
    activated = low(jax.nn.gelu(upper, approximate=True))
    branch = low_back(product('gtf,fd->gtd', activated, w_fc2) + b_fc2)
    result = residual + gate_two * branch
    return (result[:, :SEQ], result[:, SEQ:])

def reference(full_input, masked_input, keep_index, cond_full, cond_masked, w_ada, b_ada, w_qkv, b_q, b_v, w_out, b_out, w_fc1, b_fc1, w_fc2, b_fc2, cot_full, cot_masked):
    groups = HALF // 8

    def forward(full_rows, masked_rows, cond_one, cond_two, *params):
        conds = jnp.stack([cond_one, cond_two], axis=1)
        bundles = (full_rows.reshape(groups, 8, SEQ, D), masked_rows.reshape(groups, 8, SEQ, D), keep_index.reshape(groups, 8, KEEP).astype(jnp.int32), conds.reshape(groups, 8, 2, D))
        head_out, tail_out = lax.map(jax.checkpoint(lambda bundle: block_group(bundle, params)), bundles)
        return (head_out.reshape(HALF, SEQ, D), tail_out.reshape(HALF, KEEP, D))
    floats = [operand.astype(jnp.float32) for operand in (full_input, masked_input, cond_full, cond_masked, w_ada, b_ada, w_qkv, b_q, b_v, w_out, b_out, w_fc1, b_fc1, w_fc2, b_fc2)]
    outputs, pullback = jax.vjp(forward, *floats)
    grads = pullback((cot_full.astype(jnp.float32), cot_masked.astype(jnp.float32)))
    return (outputs[0].astype(jnp.bfloat16), outputs[1].astype(jnp.bfloat16), grads[0], grads[1], grads[2], grads[3], grads[4], grads[5], grads[6], grads[7], grads[8], grads[9], grads[10], grads[11], grads[12], grads[13], grads[14])
```

```python
import math
import functools

import jax
import jax.numpy as jnp
from jax import lax
from jax.experimental import pallas as pl
from jax.experimental.pallas import tpu as pltpu
from jax.sharding import PartitionSpec as P

MESH = pl.DeviceIdType.MESH

HEAD_DIM = 72


def layer_stats(values):
    centered = values - jnp.mean(values, axis=-1, keepdims=True)
    inverse = lax.rsqrt(jnp.mean(centered * centered, axis=-1, keepdims=True) + 1e-06)
    return (centered * inverse, inverse)


def layer_back(upstream, normed, inverse):
    return inverse * (
        upstream
        - jnp.mean(upstream, axis=-1, keepdims=True)
        - normed * jnp.mean(upstream * normed, axis=-1, keepdims=True)
    )


def gelu_tanh(values):
    return jax.nn.gelu(values, approximate=True)


def expand_mods(piece, full_length, kept_length):
    head_part = jnp.broadcast_to(piece[:, 0:1], (piece.shape[0], full_length, piece.shape[2]))
    tail_part = jnp.broadcast_to(piece[:, 1:2], (piece.shape[0], kept_length, piece.shape[2]))
    return jnp.concatenate([head_part, tail_part], axis=1)


def image_sums(values, full_length):
    return jnp.stack(
        [jnp.sum(values[:, :full_length], axis=1), jnp.sum(values[:, full_length:], axis=1)], axis=1
    )


def forward_pass(tokens, mods, weights, biases, full_length):
    images, length, features = tokens.shape
    head_count = features // HEAD_DIM
    pieces = [
        expand_mods(
            mods[:, :, column * features : (column + 1) * features],
            full_length,
            length - full_length,
        )
        for column in range(6)
    ]
    norm_one, inverse_one = layer_stats(tokens)
    hidden_one = (norm_one * (1.0 + pieces[1]) + pieces[0]).astype(jnp.bfloat16)
    bias_all = jnp.concatenate([biases[1], jnp.zeros((features,), jnp.bfloat16), biases[2]]).astype(
        jnp.float32
    )
    projected = (
        jnp.einsum("itd,de->ite", hidden_one, weights[1], preferred_element_type=jnp.float32)
        + bias_all
    )
    projected = projected.astype(jnp.bfloat16).reshape(images, length, 3, head_count, HEAD_DIM)
    query_rows = projected[:, :, 0]
    key_rows = projected[:, :, 1]
    value_rows = projected[:, :, 2]
    scale_factor = 1.0 / math.sqrt(HEAD_DIM)
    scores = (
        jnp.einsum("iqhc,ikhc->ihqk", query_rows, key_rows, preferred_element_type=jnp.float32)
        * scale_factor
    )
    marker = jnp.arange(length) >= full_length
    same_image = marker[:, None] == marker[None, :]
    scores = jnp.where(same_image, scores, -1e30)
    row_max = jnp.max(scores, axis=-1, keepdims=True)
    exponent = jnp.exp(scores - row_max)
    attention = exponent / jnp.sum(exponent, axis=-1, keepdims=True)
    attention_low = attention.astype(jnp.bfloat16)
    mixed = jnp.einsum(
        "ihqk,ikhc->iqhc", attention_low, value_rows, preferred_element_type=jnp.float32
    )
    mixed = mixed.astype(jnp.bfloat16).reshape(images, length, features)
    attn_out = jnp.einsum(
        "itd,de->ite", mixed, weights[2], preferred_element_type=jnp.float32
    ) + biases[3].astype(jnp.float32)
    residual = tokens + pieces[2] * attn_out
    norm_two, inverse_two = layer_stats(residual)
    hidden_two = (norm_two * (1.0 + pieces[4]) + pieces[3]).astype(jnp.bfloat16)
    upper = jnp.einsum(
        "itd,df->itf", hidden_two, weights[3], preferred_element_type=jnp.float32
    ) + biases[4].astype(jnp.float32)
    activated = gelu_tanh(upper).astype(jnp.bfloat16)
    branch = jnp.einsum(
        "itf,fd->itd", activated, weights[4], preferred_element_type=jnp.float32
    ) + biases[5].astype(jnp.float32)
    result = residual + pieces[5] * branch
    return (
        result,
        pieces,
        norm_one,
        inverse_one,
        hidden_one,
        query_rows,
        key_rows,
        value_rows,
        attention,
        attention_low,
        mixed,
        attn_out,
        norm_two,
        inverse_two,
        hidden_two,
        upper,
        activated,
        branch,
    )


MATS = (("qkv", 864, True), ("out", 288, False), ("fc1", 1152, True), ("fc2", 1152, False))
SPLIT = ((80, 64), (64, 80))


class Place:
    def __init__(self):
        self.dp = lax.axis_index("dp")
        self.f = lax.axis_index("fsdp")
        self.z = self.f // 2
        self.c = self.f % 2
        dp, f = self.dp, self.f
        self.xn = dp + 1 - 2 * (dp % 2)
        self.yn = (dp + 2) % 4
        self.dg = 3 - dp
        self.sib_f = f + 1 - 2 * self.c
        self.middle = (self.z == 1) | (self.z == 2)
        z = self.z
        low = z < 2
        self.order = (
            z,
            z + 1 - 2 * (z % 2),
            jnp.where(low, 2, 1),
            jnp.where(low, 3, 0),
        )


def barrier_all(p):
    sem = pltpu.get_barrier_semaphore()
    for dev in ((p.xn, p.f), (p.yn, p.f), (p.dp, p.sib_f)):
        pl.semaphore_signal(sem, inc=1, device_id=dev, device_id_type=MESH)

    @pl.when(p.z < 3)
    def _():
        pl.semaphore_signal(sem, inc=1, device_id=(p.dp, p.f + 2), device_id_type=MESH)

    @pl.when(p.z > 0)
    def _():
        pl.semaphore_signal(sem, inc=1, device_id=(p.dp, p.f - 2), device_id_type=MESH)

    pl.semaphore_wait(sem, jnp.where(p.middle, 5, 4))


class Gather:
    def __init__(self, p, bufs, sems):
        self.p, self.bufs = p, bufs
        (self.rz, self.rx, self.ry, self.rd, self.rs, self.so, self.sf, self.sx, self.sy, self.sd, self.ss, self.loc) = sems

    def slot(self, m, dp, zs):
        t = self.bufs[m]
        return t.at[zs, dp, self.p.c] if MATS[m][2] else t.at[dp, zs, self.p.c]

    def plane(self, m, zs):
        t = self.bufs[m]
        return t.at[zs, :, self.p.c] if MATS[m][2] else t.at[:, zs, self.p.c]

    def cp(self, src, dst, send, recv, dev):
        return pltpu.make_async_remote_copy(src_ref=src, dst_ref=dst, send_sem=send, recv_sem=recv, device_id=dev, device_id_type=MESH)

    def z_copy(self, m, src, zs, send, step):
        p = self.p
        return self.cp(src, self.slot(m, p.dp, zs), send, self.rz.at[m, zs], (p.dp, p.f + step))

    def x_copy(self, m, src, zs):
        p = self.p
        return self.cp(src, self.slot(m, p.dp, zs), self.sx.at[m, zs], self.rx.at[m, zs], (p.xn, p.f))

    def y_copy(self, m, src, zs):
        p = self.p
        return self.cp(src, self.slot(m, p.dp, zs), self.sy.at[m, zs], self.ry.at[m, zs], (p.yn, p.f))

    def d_copy(self, m, j, zs, half):
        p = self.p
        a, b = SPLIT[j % 2]
        rows = pl.ds(0, a) if half == 0 else pl.ds(a, b)
        src = self.slot(m, p.xn if half == 0 else p.yn, zs).at[rows]
        dev = (p.yn, p.f) if half == 0 else (p.xn, p.f)
        return self.cp(src, src, self.sd.at[m, zs, half], self.rd.at[m, zs, half], dev)

    def d_wait(self, m, j, zs, half):
        p = self.p
        a, b = SPLIT[j % 2]
        rows = pl.ds(0, a) if half == 0 else pl.ds(a, b)
        dst = self.slot(m, p.dg, zs).at[rows]
        self.cp(dst, dst, self.sd.at[m, zs, half], self.rd.at[m, zs, half], (p.xn, p.f)).wait_recv()

    def s_copy(self, m, zs):
        p = self.p
        src = self.plane(m, zs)
        return self.cp(src, src, self.ss.at[m, zs], self.rs.at[m, zs], (p.dp, p.sib_f))

    def own(self, m, blk):
        p = self.p

        @pl.when(p.z < 3)
        def _():
            self.z_copy(m, blk, p.z, self.so.at[m, 0], 2).start()

        @pl.when(p.z > 0)
        def _():
            self.z_copy(m, blk, p.z, self.so.at[m, 1], -2).start()

        self.x_copy(m, blk, p.z).start()
        self.y_copy(m, blk, p.z).start()
        pltpu.make_async_copy(blk, self.slot(m, p.dp, p.z), self.loc.at[m]).start()

    def arrive(self, m, j):
        p = self.p
        zs = p.order[j]
        slot = self.slot(m, p.dp, zs)
        self.cp(slot, slot, self.sf.at[m, zs], self.rz.at[m, zs], (p.xn, p.f)).wait_recv()

        @pl.when(p.middle)
        def _():
            step = jnp.where(zs < p.z, 2, -2)
            self.z_copy(m, slot, zs, self.sf.at[m, zs], step).start()

        self.x_copy(m, slot, zs).start()
        self.y_copy(m, slot, zs).start()

    def cross(self, m, j):
        p = self.p
        zs = p.order[j]
        sx, sy = self.slot(m, p.xn, zs), self.slot(m, p.yn, zs)
        self.cp(sx, sx, self.sx.at[m, zs], self.rx.at[m, zs], (p.xn, p.f)).wait_recv()
        self.d_copy(m, j, zs, 0).start()
        self.cp(sy, sy, self.sy.at[m, zs], self.ry.at[m, zs], (p.yn, p.f)).wait_recv()
        self.d_copy(m, j, zs, 1).start()

    def finish(self, m, j):
        p = self.p
        zs = p.order[j]
        self.d_wait(m, j, zs, 0)
        self.d_wait(m, j, zs, 1)
        if j == 0:
            pltpu.make_async_copy(self.slot(m, p.dp, p.z), self.slot(m, p.dp, p.z), self.loc.at[m]).wait()
        self.s_copy(m, zs).start()

    def arrived(self, m, j):
        p = self.p
        dst = self.plane(m, p.order[j])
        other = self.bufs[m].at[p.order[j], :, 1 - p.c] if MATS[m][2] else self.bufs[m].at[:, p.order[j], 1 - p.c]
        self.cp(dst, other, self.ss.at[m, p.order[j]], self.rs.at[m, p.order[j]], (p.dp, p.sib_f)).wait_recv()

    def drain(self, m, blk):
        p = self.p

        @pl.when(p.z < 3)
        def _():
            self.z_copy(m, blk, p.z, self.so.at[m, 0], 2).wait_send()

        @pl.when(p.z > 0)
        def _():
            self.z_copy(m, blk, p.z, self.so.at[m, 1], -2).wait_send()

        for j in range(4):
            zs = p.order[j]
            src = self.slot(m, p.dp, zs)
            if j:
                @pl.when(p.middle)
                def _():
                    step = jnp.where(zs < p.z, 2, -2)
                    self.z_copy(m, src, zs, self.sf.at[m, zs], step).wait_send()
            self.x_copy(m, src, zs).wait_send()
            self.y_copy(m, src, zs).wait_send()
            self.d_copy(m, j, zs, 0).wait_send()
            self.d_copy(m, j, zs, 1).wait_send()
            self.s_copy(m, zs).wait_send()


def gather_sems():
    D = pltpu.SemaphoreType.DMA
    return [D((4, 4)), D((4, 4)), D((4, 4)), D((4, 4, 2)), D((4, 4)), D((4, 2)), D((4, 4)), D((4, 4)), D((4, 4)), D((4, 4, 2)), D((4, 4)), D((4,))]


N_SEMS = 12


def stage(p, shard, got, width, send, recv):
    rows = shard.shape[0] // 2
    return pltpu.make_async_remote_copy(
        src_ref=shard.at[pl.ds((1 - p.c) * rows, rows)], dst_ref=got, send_sem=send, recv_sem=recv,
        device_id=(p.dp, p.sib_f), device_id_type=MESH)


def join(p, shard, got, blk):
    rows, width = got.shape
    own = shard[pl.ds(pl.multiple_of(p.c * rows, 16), rows), :]
    other = got[...]
    first = p.c == 0
    blk[:, 0:width] = jnp.where(first, own, other)
    blk[:, width:2 * width] = jnp.where(first, other, own)


def ag_kernel(wq, wo, w1, w2, tq, to, t1, t2, gq, g1, bq, b1, ssem, rsem, *sems):
    p = Place()
    g = Gather(p, (tq, to, t1, t2), sems)
    blks = (bq, wo, b1, w2)
    barrier_all(p)
    cq = stage(p, wq, gq, 432, ssem.at[0], rsem.at[0])
    cq.start()
    c1 = stage(p, w1, g1, 576, ssem.at[1], rsem.at[1])
    c1.start()
    g.own(1, wo)
    cq.wait_recv()
    join(p, wq, gq, bq)
    g.own(0, bq)
    c1.wait_recv()
    join(p, w1, g1, b1)
    for m in range(4):
        if m + 1 < 4 and m + 1 >= 2:
            g.own(m + 1, blks[m + 1])
        for j in range(5):
            if 1 <= j <= 3:
                g.arrive(m, j)
            if j >= 1:
                g.cross(m, j - 1)
            if j >= 2:
                g.finish(m, j - 2)
        g.finish(m, 3)
        for j in range(4):
            g.arrived(m, j)
    cq.wait_send()
    c1.wait_send()
    for m in range(4):
        g.drain(m, blks[m])


def all_gather(w_qkv, w_out, w_fc1, w_fc2):
    B = jnp.bfloat16
    shapes = [jax.ShapeDtypeStruct((4, 4, 2, 144, n), B) for _, n, _ in MATS]
    V = pl.BlockSpec(memory_space=pltpu.VMEM)
    outs = pl.pallas_call(
        ag_kernel,
        out_shape=shapes,
        in_specs=[V] * 4,
        out_specs=[pl.BlockSpec(memory_space=pl.ANY)] * 4,
        scratch_shapes=[pltpu.VMEM((144, 432), B), pltpu.VMEM((144, 576), B), pltpu.VMEM((144, 864), B), pltpu.VMEM((144, 1152), B),
                        pltpu.SemaphoreType.DMA((2,)), pltpu.SemaphoreType.DMA((2,))] + gather_sems(),
        compiler_params=pltpu.CompilerParams(collective_id=0, has_side_effects=True, vmem_limit_bytes=32 * 2**20),
        name="gather_weights",
    )(w_qkv, w_out.T, w_fc1, w_fc2.T)
    return outs


def on_device(
    special,
    full_input,
    masked_input,
    keep_index,
    cond_full,
    cond_masked,
    w_ada,
    b_ada,
    w_qkv,
    b_q,
    b_v,
    w_out,
    b_out,
    w_fc1,
    b_fc1,
    w_fc2,
    b_fc2,
    cot_full,
    cot_masked,
):
    def columns(shard):
        return lax.all_gather(lax.all_gather(shard, "dp", axis=0, tiled=True), "fsdp", axis=1, tiled=True)

    if special:
        bufs = all_gather(w_qkv, w_out, w_fc1, w_fc2)
        flat = [t.reshape(4, 1152, -1) for t in bufs]
        qkv, out_t, fc1, fc2_t = [jnp.concatenate(list(t), axis=1) for t in flat]
        weights = (None, qkv, out_t.T, fc1, fc2_t.T)
    else:
        weights = (None, columns(w_qkv), columns(w_out), columns(w_fc1), columns(w_fc2))
    widths = [b.shape[0] for b in (b_q, b_v, b_out, b_fc1, b_fc2)]
    packed = lax.all_gather(jnp.concatenate([b_q, b_v, b_out, b_fc1, b_fc2]), "fsdp", axis=0, tiled=False)
    biases, at = [None], 0
    for width in widths:
        biases.append(packed[:, at : at + width].reshape(-1))
        at += width
    full_length = full_input.shape[1]
    images = full_input.shape[0]
    features = full_input.shape[2]
    picked = jnp.take_along_axis(masked_input, keep_index[:, :, None], axis=1)
    tokens = jnp.concatenate([full_input, picked], axis=1).astype(jnp.float32)
    conds = jnp.stack([cond_full, cond_masked], axis=1).astype(jnp.float32)
    silu_low = jax.nn.silu(conds).astype(jnp.bfloat16)
    n_dp, n_fsdp = lax.axis_size("dp"), lax.axis_size("fsdp")
    rows_ada, cols_ada = w_ada.shape
    every_silu = lax.all_gather(silu_low, ("dp", "fsdp"), axis=0, tiled=True)
    my_silu = lax.dynamic_slice_in_dim(every_silu, lax.axis_index("dp") * rows_ada, rows_ada, axis=2)
    part = jnp.einsum("ijd,de->ije", my_silu, w_ada, preferred_element_type=jnp.float32)
    part = lax.psum_scatter(part, "dp", scatter_dimension=0, tiled=True)
    part = part + b_ada.astype(jnp.float32)
    mods = lax.all_to_all(part, "fsdp", split_axis=0, concat_axis=2, tiled=True)
    (
        result,
        pieces,
        norm_one,
        inverse_one,
        hidden_one,
        query_rows,
        key_rows,
        value_rows,
        attention,
        attention_low,
        mixed,
        attn_out,
        norm_two,
        inverse_two,
        hidden_two,
        upper,
        activated,
        branch,
    ) = forward_pass(tokens, mods, weights, biases, full_length)
    length = tokens.shape[1]
    head_count = features // HEAD_DIM
    scale_factor = 1.0 / math.sqrt(HEAD_DIM)
    grad_result = jnp.concatenate([cot_full, cot_masked], axis=1).astype(jnp.float32)
    grad_gate_two = image_sums(grad_result * branch, full_length)
    grad_branch = (pieces[5] * grad_result).astype(jnp.bfloat16)
    grad_b_fc2 = jnp.sum(grad_branch.astype(jnp.float32), axis=(0, 1))
    grad_w_fc2 = jnp.einsum(
        "itf,itd->fd", activated, grad_branch, preferred_element_type=jnp.float32
    )
    grad_act = jnp.einsum(
        "itd,fd->itf", grad_branch, weights[4], preferred_element_type=jnp.float32
    )
    grad_upper = jax.vjp(gelu_tanh, upper)[1](grad_act)[0].astype(jnp.bfloat16)
    grad_b_fc1 = jnp.sum(grad_upper.astype(jnp.float32), axis=(0, 1))
    grad_w_fc1 = jnp.einsum(
        "itd,itf->df", hidden_two, grad_upper, preferred_element_type=jnp.float32
    )
    grad_hidden_two = jnp.einsum(
        "itf,df->itd", grad_upper, weights[3], preferred_element_type=jnp.float32
    )
    grad_scale_two = image_sums(grad_hidden_two * norm_two, full_length)
    grad_shift_two = image_sums(grad_hidden_two, full_length)
    grad_residual = grad_result + layer_back(
        grad_hidden_two * (1.0 + pieces[4]), norm_two, inverse_two
    )
    grad_gate_one = image_sums(grad_residual * attn_out, full_length)
    grad_attn = (pieces[2] * grad_residual).astype(jnp.bfloat16)
    grad_b_out = jnp.sum(grad_attn.astype(jnp.float32), axis=(0, 1))
    grad_w_out = jnp.einsum("itd,ite->de", mixed, grad_attn, preferred_element_type=jnp.float32)
    grad_mixed = jnp.einsum(
        "ite,de->itd", grad_attn, weights[2], preferred_element_type=jnp.float32
    )
    grad_mixed = grad_mixed.astype(jnp.bfloat16).reshape(images, length, head_count, HEAD_DIM)
    grad_attention = jnp.einsum(
        "iqhc,ikhc->ihqk", grad_mixed, value_rows, preferred_element_type=jnp.float32
    )
    grad_values = jnp.einsum(
        "ihqk,iqhc->ikhc", attention_low, grad_mixed, preferred_element_type=jnp.float32
    )
    grad_scores = attention * (
        grad_attention - jnp.sum(attention * grad_attention, axis=-1, keepdims=True)
    )
    grad_scores = grad_scores.astype(jnp.bfloat16)
    grad_queries = (
        jnp.einsum("ihqk,ikhc->iqhc", grad_scores, key_rows, preferred_element_type=jnp.float32)
        * scale_factor
    )
    grad_keys = (
        jnp.einsum("ihqk,iqhc->ikhc", grad_scores, query_rows, preferred_element_type=jnp.float32)
        * scale_factor
    )
    grad_projected = jnp.stack([grad_queries, grad_keys, grad_values], axis=2)
    grad_projected = grad_projected.reshape(images, length, 3 * features).astype(jnp.bfloat16)
    grad_b_q = jnp.sum(grad_projected[:, :, :features].astype(jnp.float32), axis=(0, 1))
    grad_b_v = jnp.sum(grad_projected[:, :, 2 * features :].astype(jnp.float32), axis=(0, 1))
    grad_w_qkv = jnp.einsum(
        "itd,ite->de", hidden_one, grad_projected, preferred_element_type=jnp.float32
    )
    grad_hidden_one = jnp.einsum(
        "ite,de->itd", grad_projected, weights[1], preferred_element_type=jnp.float32
    )
    grad_scale_one = image_sums(grad_hidden_one * norm_one, full_length)
    grad_shift_one = image_sums(grad_hidden_one, full_length)
    grad_tokens = grad_residual + layer_back(
        grad_hidden_one * (1.0 + pieces[1]), norm_one, inverse_one
    )
    grad_mods = jnp.concatenate(
        [
            grad_shift_one,
            grad_scale_one,
            grad_gate_one,
            grad_shift_two,
            grad_scale_two,
            grad_gate_two,
        ],
        axis=-1,
    ).astype(jnp.bfloat16)
    cut = grad_mods.reshape(images, 2, n_fsdp, cols_ada)
    mine = lax.all_to_all(cut, "fsdp", split_axis=2, concat_axis=0, tiled=False)
    mine = lax.all_gather(mine.reshape(n_fsdp * images, 2, cols_ada), "dp", axis=0, tiled=True)
    grad_b_ada = jnp.sum(mine.astype(jnp.float32), axis=(0, 1))
    grad_w_ada = jnp.einsum("ijd,ije->de", my_silu, mine, preferred_element_type=jnp.float32)
    back = jnp.einsum("ije,de->ijd", mine, w_ada, preferred_element_type=jnp.float32)
    back = lax.psum_scatter(back.reshape(n_dp, n_fsdp * images, 2, rows_ada), "fsdp", scatter_dimension=1, tiled=True)
    grad_silu = lax.all_to_all(back, "dp", split_axis=0, concat_axis=3, tiled=True).reshape(images, 2, features)
    grad_cond = jax.vjp(jax.nn.silu, conds)[1](grad_silu)[0]
    image_rows = jnp.arange(images)[:, None]
    grad_masked = (
        jnp.zeros((images, full_length, features), jnp.float32)
        .at[image_rows, keep_index]
        .set(grad_tokens[:, full_length:])
    )
    def owned(grad):
        inner = lax.psum_scatter(grad.astype(jnp.bfloat16), "dp", scatter_dimension=0, tiled=True)
        return lax.psum_scatter(inner, "fsdp", scatter_dimension=1, tiled=True).astype(jnp.float32)

    matrices = (grad_w_ada, owned(grad_w_qkv), owned(grad_w_out), owned(grad_w_fc1), owned(grad_w_fc2))
    sums = (grad_b_q, grad_b_v, grad_b_out, grad_b_fc1, grad_b_fc2)
    line = jnp.concatenate([g.reshape(n_fsdp, -1) for g in sums], axis=1)
    line = lax.psum(lax.psum_scatter(line, "fsdp", scatter_dimension=0, tiled=True), "dp")[0]
    vectors, at = [grad_b_ada], 0
    for width in widths:
        vectors.append(line[at : at + width])
        at += width
    return (
        result[:, :full_length].astype(jnp.bfloat16),
        result[:, full_length:].astype(jnp.bfloat16),
        grad_tokens[:, :full_length],
        grad_masked,
        grad_cond[:, 0],
        grad_cond[:, 1],
        matrices[0],
        vectors[0],
        matrices[1],
        vectors[1],
        vectors[2],
        matrices[2],
        vectors[3],
        matrices[3],
        vectors[4],
        matrices[4],
        vectors[5],
    )


def solution(mesh):
    special = dict(mesh.shape) == {"dp": 4, "fsdp": 8}
    return jax.shard_map(
        functools.partial(on_device, special),
        mesh=mesh,
        in_specs=(
            P(("dp", "fsdp"), None, None),
            P(("dp", "fsdp"), None, None),
            P(("dp", "fsdp"), None),
            P(("dp", "fsdp"), None),
            P(("dp", "fsdp"), None),
            P("dp", "fsdp"),
            P("fsdp"),
            P("dp", "fsdp"),
            P("fsdp"),
            P("fsdp"),
            P("dp", "fsdp"),
            P("fsdp"),
            P("dp", "fsdp"),
            P("fsdp"),
            P("dp", "fsdp"),
            P("fsdp"),
            P(("dp", "fsdp"), None, None),
            P(("dp", "fsdp"), None, None),
        ),
        out_specs=(
            P(("dp", "fsdp"), None, None),
            P(("dp", "fsdp"), None, None),
            P(("dp", "fsdp"), None, None),
            P(("dp", "fsdp"), None, None),
            P(("dp", "fsdp"), None),
            P(("dp", "fsdp"), None),
            P("dp", "fsdp"),
            P("fsdp"),
            P("dp", "fsdp"),
            P("fsdp"),
            P("fsdp"),
            P("dp", "fsdp"),
            P("fsdp"),
            P("dp", "fsdp"),
            P("fsdp"),
            P("dp", "fsdp"),
            P("fsdp"),
        ),
        check_vma=False,
    )
```

```python
import functools
import math
import jax
import jax.numpy as jnp
from jax import lax
from jax.experimental import pallas as pl
from jax.experimental.pallas import tpu as pltpu
from jax.sharding import PartitionSpec as P


MESH = pl.DeviceIdType.MESH
ROWS, COLS = "dp", "fsdp"
F32, B16 = jnp.float32, jnp.bfloat16
D, HEADS, HEAD_DIM, SEQ, KEEP, TOK = 1152, 16, 72, 256, 128, 384
SCALE = 1.0 / math.sqrt(HEAD_DIM)
GELU_A, GELU_B = math.sqrt(2.0 / math.pi), 0.044715
MATS = ((864, True, 0), (288, False, 0), (1152, True, 48), (1152, False, 48))
QKV, OUT, FC1, FC2 = range(4)


def nn(a, b):
    return lax.dot_general(a, b, (((1,), (0,)), ((), ())), preferred_element_type=F32)


def nt(a, b):
    return lax.dot_general(a, b, (((1,), (1,)), ((), ())), preferred_element_type=F32)


def tn(a, b):
    return lax.dot_general(a, b, (((0,), (0,)), ((), ())), preferred_element_type=F32)


class Script:
    def __init__(self):
        self.steps = []

    def __getattr__(self, name):
        return lambda *args: self.steps.append((name, args))


class Place:
    def __init__(self):
        self.dp = dp = lax.axis_index(ROWS)
        self.f = f = lax.axis_index(COLS)
        self.z, self.c = f // 2, f % 2
        self.xn = dp + 1 - 2 * (dp % 2)
        self.yn = (dp + 2) % 4
        self.dg = 3 - dp
        self.sf = f + 1 - 2 * self.c
        z = self.z
        self.middle = (z == 1) | (z == 2)
        low = z < 2
        self.order = (z, z + 1 - 2 * (z % 2), jnp.where(low, 2, 1), jnp.where(low, 3, 0))
        self.x_dev, self.y_dev, self.d_dev, self.s_dev = (self.xn, f), (self.yn, f), (self.dg, f), (dp, self.sf)
        self.rows = [(self.dp + k) % 4 for k in (1, 2, 3)]
        self.cols = [(self.f + k) % 8 for k in range(1, 8)]

    def barrier(self):
        sem = pltpu.get_barrier_semaphore()
        for dev in [(r, self.f) for r in self.rows] + [(self.dp, c) for c in self.cols]:
            pl.semaphore_signal(sem, inc=1, device_id=dev, device_id_type=MESH)
        pl.semaphore_wait(sem, 10)


def remote(src, dst, send, recv, dev):
    return pltpu.make_async_remote_copy(src_ref=src, dst_ref=dst, send_sem=send, recv_sem=recv, device_id=dev, device_id_type=MESH)


def cut(ref, lo, n):
    return ref.at[pl.ds(lo, n)]


class Gather:
    SEMS = dict(rz=(4, 4), rx=(4, 4), ry=(4, 4), rd=(4, 4, 2), rs=(4, 4), so=(4, 2), sf=(4, 4), sx=(4, 4), sy=(4, 4), sd=(4, 4, 2),
                ss=(4, 4), loc=(4,), bx=(4,), by=(4,), bd=(4, 2), bz=(4, 4), cx=(4,), cy=(4,), cd=(4, 2), co=(4, 2), cf=(4, 4))

    def __init__(self, p, bufs, blks, sems):
        self.p, self.bufs, self.blks = p, bufs, blks
        for name, sem in zip(self.SEMS, sems, strict=True):
            setattr(self, name, sem)

    @classmethod
    def scratch(cls):
        return [pltpu.SemaphoreType.DMA(s) for s in cls.SEMS.values()]

    def a(self, m):
        return 144 - MATS[m][2]

    def split(self, m, j):
        a = self.a(m)
        h = (a // 32) * 16
        return (a - h, h) if j % 2 == 0 else (h, a - h)

    def slot(self, m, dp, zs):
        t = self.bufs[m]
        return t.at[zs, dp, self.p.c] if MATS[m][1] else t.at[dp, zs, self.p.c]

    def top(self, m, dp, zs):
        return cut(self.slot(m, dp, zs), 0, self.a(m))

    def low(self, m, dp, zs):
        return cut(self.slot(m, dp, zs), self.a(m), MATS[m][2])

    def low4(self, m, zs):
        t, rows = self.bufs[m], pl.ds(self.a(m), MATS[m][2])
        return t.at[zs, :, self.p.c, rows] if MATS[m][1] else t.at[:, zs, self.p.c, rows]

    def plane(self, m, zs, c):
        t = self.bufs[m]
        return t.at[zs, :, c] if MATS[m][1] else t.at[:, zs, c]

    def z_copies(self, m):
        p = self.p
        blk = cut(self.blks[m], 0, self.a(m))
        dst = self.top(m, p.dp, p.z)
        up = remote(blk, dst, self.so.at[m, 0], self.rz.at[m, p.z], (p.dp, p.f + 2))
        down = remote(blk, dst, self.so.at[m, 1], self.rz.at[m, p.z], (p.dp, p.f - 2))
        return up, down

    def bz_copies(self, m):
        p = self.p
        src = self.low4(m, p.z)
        up = remote(src, src, self.co.at[m, 0], self.bz.at[m, p.z], (p.dp, p.f + 2))
        down = remote(src, src, self.co.at[m, 1], self.bz.at[m, p.z], (p.dp, p.f - 2))
        return up, down

    def pass_on(self, m, zs):
        p = self.p
        src = self.top(m, p.dp, zs)
        return remote(src, src, self.sf.at[m, zs], self.rz.at[m, zs], (p.dp, p.f + jnp.where(zs < p.z, 2, -2)))

    def pass_low(self, m, zs):
        p = self.p
        src = self.low4(m, zs)
        return remote(src, src, self.cf.at[m, zs], self.bz.at[m, zs], (p.dp, p.f + jnp.where(zs < p.z, 2, -2)))

    def x_copy(self, m, src, zs):
        return remote(src, self.top(m, self.p.dp, zs), self.sx.at[m, zs], self.rx.at[m, zs], self.p.x_dev)

    def y_copy(self, m, src, zs):
        return remote(src, self.top(m, self.p.dp, zs), self.sy.at[m, zs], self.ry.at[m, zs], self.p.y_dev)

    def d_copy(self, m, j, zs, half):
        p = self.p
        a, b = self.split(m, j)
        lo, n = ((0, a), (a, b))[half]
        src = cut(self.slot(m, p.xn if half == 0 else p.yn, zs), lo, n)
        return remote(src, src, self.sd.at[m, zs, half], self.rd.at[m, zs, half], p.y_dev if half == 0 else p.x_dev)

    def bd_copy(self, m, half):
        p = self.p
        h = 16 * ((MATS[m][2] // 16 + 1) // 2)
        lo, n = ((0, h), (h, MATS[m][2] - h))[half]
        src = cut(self.slot(m, p.xn if half == 0 else p.yn, p.z), self.a(m) + lo, n)
        return remote(src, src, self.cd.at[m, half], self.bd.at[m, half], p.y_dev if half == 0 else p.x_dev)

    def s_copy(self, m, zs):
        src = self.plane(m, zs, self.p.c)
        return remote(src, src, self.ss.at[m, zs], self.rs.at[m, zs], self.p.s_dev)

    def ends(self, copies, act):
        p = self.p

        @pl.when(p.z < 3)
        def _():
            act(copies[0])

        @pl.when(p.z > 0)
        def _():
            act(copies[1])

    def got(self, ref, recv):
        remote(ref, ref, self.so.at[0, 0], recv, self.p.x_dev).wait_recv()

    def own(self, m):
        p = self.p
        self.ends(self.z_copies(m), lambda c: c.start())
        blk = cut(self.blks[m], 0, self.a(m))
        self.x_copy(m, blk, p.z).start()
        self.y_copy(m, blk, p.z).start()
        if not MATS[m][2]:
            pltpu.make_async_copy(self.blks[m], self.slot(m, p.dp, p.z), self.loc.at[m]).start()

    def bown(self, m):
        p = self.p
        pltpu.make_async_copy(self.blks[m], self.slot(m, p.dp, p.z), self.loc.at[m]).start()
        blk = cut(self.blks[m], self.a(m), MATS[m][2])
        dst = self.low(m, p.dp, p.z)
        remote(blk, dst, self.cx.at[m], self.bx.at[m], p.x_dev).start()
        remote(blk, dst, self.cy.at[m], self.by.at[m], p.y_dev).start()

    def arr(self, m, j):
        p = self.p
        zs = p.order[j]
        src = self.top(m, p.dp, zs)
        self.got(src, self.rz.at[m, zs])

        @pl.when(p.middle)
        def _():
            self.pass_on(m, zs).start()

        self.x_copy(m, src, zs).start()
        self.y_copy(m, src, zs).start()

    def cross(self, m, j):
        p = self.p
        zs = p.order[j]
        self.got(self.top(m, p.xn, zs), self.rx.at[m, zs])
        self.d_copy(m, j, zs, 0).start()
        self.got(self.top(m, p.yn, zs), self.ry.at[m, zs])
        self.d_copy(m, j, zs, 1).start()

    def bcross(self, m):
        p = self.p
        self.got(self.low(m, p.xn, p.z), self.bx.at[m])
        self.bd_copy(m, 0).start()
        self.got(self.low(m, p.yn, p.z), self.by.at[m])
        self.bd_copy(m, 1).start()

    def bz_(self, m):
        p = self.p
        h = 16 * ((MATS[m][2] // 16 + 1) // 2)
        for half, (lo, n) in enumerate(((0, h), (h, MATS[m][2] - h))):
            self.got(cut(self.slot(m, p.dg, p.z), self.a(m) + lo, n), self.bd.at[m, half])
        pltpu.make_async_copy(self.blks[m], self.slot(m, p.dp, p.z), self.loc.at[m]).wait()
        self.ends(self.bz_copies(m), lambda c: c.start())

    def barr(self, m, j):
        zs = self.p.order[j]
        self.got(self.low4(m, zs), self.bz.at[m, zs])

        @pl.when(self.p.middle)
        def _():
            self.pass_low(m, zs).start()

    def fin(self, m, j):
        p = self.p
        zs = p.order[j]
        a, b = self.split(m, j)
        for half, (lo, n) in enumerate(((0, a), (a, b))):
            self.got(cut(self.slot(m, p.dg, zs), lo, n), self.rd.at[m, zs, half])
        if j == 0 and not MATS[m][2]:
            pltpu.make_async_copy(self.blks[m], self.slot(m, p.dp, p.z), self.loc.at[m]).wait()
        self.s_copy(m, zs).start()

    def have(self, m):
        for j in range(4):
            zs = self.p.order[j]
            self.got(self.plane(m, zs, 1 - self.p.c), self.rs.at[m, zs])

    def drain(self):
        p = self.p
        for m in range(4):
            blk = cut(self.blks[m], 0, self.a(m))
            self.ends(self.z_copies(m), lambda c: c.wait_send())
            if MATS[m][2]:
                low = cut(self.blks[m], self.a(m), MATS[m][2])
                dst = self.low(m, p.dp, p.z)
                remote(low, dst, self.cx.at[m], self.bx.at[m], p.x_dev).wait_send()
                remote(low, dst, self.cy.at[m], self.by.at[m], p.y_dev).wait_send()
                self.bd_copy(m, 0).wait_send()
                self.bd_copy(m, 1).wait_send()
                self.ends(self.bz_copies(m), lambda c: c.wait_send())
            for j in range(4):
                zs = p.order[j]
                src = self.top(m, p.dp, zs)
                if j:

                    @pl.when(p.middle)
                    def _(m=m, zs=zs):
                        self.pass_on(m, zs).wait_send()
                        if MATS[m][2]:
                            self.pass_low(m, zs).wait_send()

                self.x_copy(m, src, zs).wait_send()
                self.y_copy(m, src, zs).wait_send()
                self.d_copy(m, j, zs, 0).wait_send()
                self.d_copy(m, j, zs, 1).wait_send()
                self.s_copy(m, zs).wait_send()


def stage(p, shard, got, send, recv):
    rows = shard.shape[0] // 2
    return remote(cut(shard, (1 - p.c) * rows, rows), got, send, recv, p.s_dev)


def join(p, shard, got, blk):
    rows, width = got.shape
    own = shard[pl.ds(pl.multiple_of(p.c * rows, 16), rows), :]
    other = got[...]
    first = p.c == 0
    blk[:, 0:width] = jnp.where(first, own, other)
    blk[:, width : 2 * width] = jnp.where(first, other, own)


class Conditions:
    SEMS = dict(r1=(4,), s1=(4,), r2=(8,), s2=(8,), rb=(8,), sb=(8,), r3=(4,), s3=(4,), r4=(8,), s4=(8,))
    SHAPES = dict(sil4=(4, 2, 288), in1=(4, 2, 288), row8=(8, 288), in2=(8, 8, 288), pack=(1, D), inb=(8, 1, D), p3=(4, 16, 864),
                  in3=(4, 16, 864), m8=(8, 2, 864), in4=(8, 2, 864), mods=(6, 2, 1, D), bias=(8, 1, D), wide=(4, 1, D), qkvb=(4, 1, 864))

    @classmethod
    def scratch(cls):
        return [pltpu.VMEM(s, F32) for s in cls.SHAPES.values()] + [pltpu.SemaphoreType.DMA(s) for s in cls.SEMS.values()]

    def __init__(self, p, conds, w_ada, b_ada, biases, scratch):
        self.p, self.conds, self.w_ada, self.b_ada, self.biases = p, conds, w_ada, b_ada, biases
        for name, ref in zip(list(self.SHAPES) + list(self.SEMS), scratch, strict=True):
            setattr(self, name, ref)

    def over_dp(self, src_of, land, sem_s, sem_r):
        p = self.p
        return [remote(src_of(r), land.at[p.dp], sem_s.at[r], sem_r.at[p.dp], (r, p.f)) for r in p.rows]

    def over_f(self, src_of, land, sem_s, sem_r):
        p = self.p
        return [remote(src_of(c), land.at[p.f], sem_s.at[c], sem_r.at[p.f], (p.dp, c)) for c in p.cols]

    def copies(self, step):
        return {
            1: lambda: self.over_dp(lambda r: self.sil4.at[r], self.in1, self.s1, self.r1),
            2: lambda: self.over_f(lambda c: self.row8, self.in2, self.s2, self.r2),
            "b": lambda: self.over_f(lambda c: self.pack, self.inb, self.sb, self.rb),
            3: lambda: self.over_dp(lambda r: self.p3.at[r], self.in3, self.s3, self.r3),
            4: lambda: self.over_f(lambda c: self.m8.at[c], self.in4, self.s4, self.r4),
        }[step]()

    def send(self, step):
        for c in self.copies(step):
            c.start()

    def arrived(self, land, sem, peers):
        for q in peers:
            remote(land.at[q], land.at[q], self.s1.at[0], sem.at[q], self.p.x_dev).wait_recv()

    def begin(self):
        p = self.p
        at = 0
        for b in self.biases:
            n = b.shape[1]
            self.pack[:, at : at + n] = b[...].astype(F32)
            at += n
        self.send("b")
        self.inb[p.f] = self.pack[...]
        for s, cond in enumerate(self.conds):
            x = cond[...].astype(F32)
            y = (x / (1.0 + jnp.exp(-x))).astype(B16).astype(F32)
            for d in range(4):
                self.sil4[d, s : s + 1, :] = y[:, 288 * d : 288 * d + 288]
        self.send(1)
        self.in1[p.dp] = self.sil4[p.dp]

    def second(self):
        p = self.p
        self.arrived(self.in1, self.r1, p.rows)
        for d in range(4):
            self.row8[2 * d : 2 * d + 2, :] = self.in1[d]
        self.send(2)
        self.in2[p.f] = self.row8[...]

    def third(self):
        p = self.p
        self.arrived(self.in2, self.r2, p.cols)
        rows = self.in2[...].reshape(64, 288).astype(B16)
        part = nn(rows, self.w_ada[...])
        for d in range(4):
            for f in range(8):
                self.p3[d, 2 * f : 2 * f + 2, :] = part[8 * f + 2 * d : 8 * f + 2 * d + 2]
        self.send(3)
        self.in3[p.dp] = self.p3[p.dp]

    def fourth(self):
        p = self.p
        self.arrived(self.in3, self.r3, p.rows)
        total = self.in3[0] + self.in3[1] + self.in3[2] + self.in3[3] + self.b_ada[...].astype(F32)
        for f in range(8):
            self.m8[f] = total[2 * f : 2 * f + 2]
        self.send(4)
        self.in4[p.f] = self.m8[p.f]

    def last(self):
        p = self.p
        self.arrived(self.in4, self.r4, p.cols)
        self.arrived(self.inb, self.rb, p.cols)
        for f in range(8):
            rows = self.in4[f]
            at = 864 * f
            while at < 864 * (f + 1):
                b = at // D
                end = min(864 * (f + 1), D * (b + 1))
                for s in range(2):
                    self.mods[b, s, :, at - D * b : end - D * b] = rows[s : s + 1, at - 864 * f : end - 864 * f]
                at = end
        for f in range(8):
            row = self.inb[f]
            for i, lo in enumerate((0, 144, 288, 1008)):
                self.bias[i, :, 144 * f : 144 * f + 144] = row[:, lo : lo + 144]
            half = 576 * (f % 2)
            self.wide[f // 2, :, half : half + 576] = row[:, 432:1008]
        line = jnp.concatenate([self.bias[0], jnp.zeros((1, D), F32), self.bias[1]], axis=1)
        for k in range(4):
            self.qkvb[k] = line[:, 864 * k : 864 * k + 864]

    def drain(self):
        for step in (1, 2, "b", 3, 4):
            for c in self.copies(step):
                c.wait_send()


def layer_stats(x):
    mean = jnp.mean(x, axis=-1, keepdims=True)
    centered = x - mean
    inv = lax.rsqrt(jnp.mean(centered * centered, axis=-1, keepdims=True) + 1e-6)
    return centered * inv, inv


def by_rows(body):
    def step(i, carry):
        body(pl.ds(pl.multiple_of(i * 128, 128), 128), i // 2)
        return carry

    lax.fori_loop(0, 3, step, 0)


def transpose_into(src, dst):
    for i in range(3):
        for k in range(9):
            t = src[128 * i : 128 * i + 128, 128 * k : 128 * k + 128].astype(F32).T.astype(B16)
            at = 128 * k
            while at < 128 * (k + 1):
                b = at // 144
                end = min(128 * (k + 1), 144 * (b + 1))
                dst[b, at - 144 * b : end - 144 * b, 128 * i : 128 * i + 128] = t[at - 128 * k : end - 128 * k]
                at = end


def softmax(scores):
    e = jnp.exp(scores - jnp.max(scores, axis=-1, keepdims=True))
    return e / jnp.sum(e, axis=-1, keepdims=True)


def pair_rows(p, mine, land, half, send, recv, loc):
    to_sib = [remote(mine.at[2 * k + (1 - p.c)], land.at[k, :, pl.ds(384, 384)], send.at[k], recv.at[k], p.s_dev) for k in range(4)]
    to_own = [pltpu.make_async_copy(mine.at[2 * k + p.c], land.at[k, :, pl.ds(0, 384)], loc.at[k]) for k in range(4)]
    return to_sib, to_own


K1_VMEM = dict(
    gq=((144, 432), B16), g1=((144, 576), B16), bq=((144, 864), B16), b1=((144, 1152), B16),
    hid=((TOK, D), B16), hid2=((TOK, D), B16), tok=((TOK, D), B16), h1t=((8, 144, TOK), B16), h2t=((8, 144, TOK), B16), gbt=((8, 144, TOK), B16),
    gb=((TOK, D), B16), qkv=((48, TOK, HEAD_DIM), B16), mixh=((HEADS, TOK, HEAD_DIM), B16), mixed=((TOK, D), B16),
    attn=((TOK, D), F32), act=((4, TOK, D), B16), dact=((4, TOK, D), B16),
    wq=((2, 4, 2, 144, 864), B16), wo=((4, 4, 2, 144, 288), B16), w1=((2, 4, 2, 144, D), B16),
)
K1_SEMS = dict(st=(2,), rt=(2,), lq=(2,), lo=(4,), l1=(2,), pt=(3, 4), pr=(3, 4), pl_=(3, 4), ms=(1,), mr=(1,), as_=(4,), ar=(4,), ow=(16,))
K1_IN = dict(full=0, masked=0, keep=0, cond_full=0, cond_masked=0, w_ada=0, b_ada=0, w_qkv=0, b_q=0, b_v=0, w_out=0, b_out=0, w_fc1=0, b_fc1=0, w_fc2=0, b_fc2=0, cot_full=0, cot_masked=0)
K1_OUT = dict(
    t0=((4, 4, 2, 144, 864), B16), t1=((4, 4, 2, 144, 288), B16), t2=((4, 4, 2, 144, D), B16), t3=((4, 4, 2, 144, D), B16),
    mods=((6, 2, 1, D), F32), sil=((8, 8, 288), F32), bias=((8, 1, D), F32), tok=((TOK, D), B16), qkv=((48, TOK, HEAD_DIM), B16),
    mixed=((2 * TOK, D), B16), attn=((TOK, D), F32), h1p=((4, 144, 768), B16), h2p=((4, 144, 768), B16), gbp=((4, 144, 768), B16),
    act=((4, 2 * TOK, D), B16), dact=((4, TOK, D), B16), gb=((TOK, D), B16),
)


class Bag:
    pass


def k1_kernel(events, *refs):
    i = Bag()
    o = Bag()
    v = Bag()
    refs = list(refs)
    for n in K1_IN:
        setattr(i, n, refs.pop(0))
    for n in K1_OUT:
        setattr(o, n, refs.pop(0))
    for n in list(K1_VMEM) + list(K1_SEMS):
        setattr(v, n, refs.pop(0))
    n_cond = len(Conditions.SHAPES) + len(Conditions.SEMS)
    p = Place()
    con = Conditions(p, (i.cond_full, i.cond_masked), i.w_ada, i.b_ada, (i.b_q, i.b_v, i.b_out, i.b_fc1, i.b_fc2), refs[:n_cond])
    g = Gather(p, (o.t0, o.t1, o.t2, o.t3), (v.bq, i.w_out, v.b1, i.w_fc2), refs[n_cond:])
    saves = []

    def save(src, dst):
        c = pltpu.make_async_copy(src, dst, v.ow.at[len(saves)])
        c.start()
        saves.append(c)

    waits = []

    def pairs(k, mine, land):
        to_sib, to_own = pair_rows(p, mine, land, None, v.pt.at[k], v.pr.at[k], v.pl_.at[k])
        for c in to_sib + to_own:
            c.start()
        waits.append((to_sib, to_own))

    loads = {}

    def load(name, k, slot, src, dst, sem):
        c = pltpu.make_async_copy(src, dst, sem)
        c.start()
        loads[name, k] = c

    def tokens():
        v.tok[0:SEQ] = i.full[0]
        spread = (lax.broadcasted_iota(jnp.int32, (SEQ, KEEP), 0) == i.keep[...]).astype(B16)
        v.tok[SEQ:TOK] = tn(spread, i.masked[0]).astype(B16)
        save(v.tok, o.tok)

    def norm1():
        def body(r, s):
            n, _ = layer_stats(v.tok[r, :].astype(F32))
            v.hid[r, :] = (n * (1.0 + con.mods[1, s]) + con.mods[0, s]).astype(B16)

        by_rows(body)
        save(con.mods, o.mods)
        save(con.in2, o.sil)
        save(con.bias, o.bias)

    def grads_in():
        v.gb[0:SEQ] = (con.mods[5, 0] * i.cot_full[0].astype(F32)).astype(B16)
        v.gb[SEQ:TOK] = (con.mods[5, 1] * i.cot_masked[0].astype(F32)).astype(B16)
        save(v.gb, o.gb)
        transpose_into(v.gb, v.gbt)
        pairs(0, v.gbt, o.gbp)

    def turn1():
        transpose_into(v.hid, v.h1t)
        pairs(1, v.h1t, o.h1p)

    def load_q(k):
        load("q", k, k % 2, o.t0.at[k], v.wq.at[k % 2], v.lq.at[k % 2])

    def qkv(k):
        loads["q", k].wait()
        y = (nn(v.hid[...], v.wq[k % 2].reshape(D, 864)) + con.qkvb[k]).astype(B16)
        for h in range(12):
            v.qkv[12 * k + h] = y[:, 72 * h : 72 * h + 72]
        if k + 2 < 4:
            load_q(k + 2)
        if k == 3:
            save(v.qkv, o.qkv)

    def heads(k, n):
        def step(h, carry):
            q, key, val = v.qkv[h], v.qkv[16 + h], v.qkv[32 + h]
            for lo, hi in ((0, SEQ), (SEQ, TOK)):
                probs = softmax(nt(q[lo:hi], key[lo:hi]) * SCALE).astype(B16)
                v.mixh[h, lo:hi] = nn(probs, val[lo:hi]).astype(B16)
            return carry

        lax.fori_loop(k, k + n, step, 0)

    def mix():
        for h in range(HEADS):
            v.mixed[:, 72 * h : 72 * h + 72] = v.mixh[h]
        save(v.mixed, cut(o.mixed, 0, TOK))
        c = remote(v.mixed, cut(o.mixed, TOK, TOK), v.ms.at[0], v.mr.at[0], p.s_dev)
        c.start()
        waits.append(([c], []))

    def load_o():
        for k in range(4):
            load("o", k, k, o.t1.at[k], v.wo.at[k], v.lo.at[k])

    def attend():
        for k in range(4):
            loads["o", k].wait()

        def body(r, s):
            y = con.bias[2] + jnp.zeros((128, 1), F32)
            for k in range(4):
                y = y + nt(v.mixed[r, 288 * k : 288 * k + 288], v.wo[k].reshape(D, 288))
            v.attn[r, :] = y
            resid = v.tok[r, :].astype(F32) + con.mods[2, s] * y
            n, _ = layer_stats(resid)
            v.hid2[r, :] = (n * (1.0 + con.mods[4, s]) + con.mods[3, s]).astype(B16)

        by_rows(body)
        save(v.attn, o.attn)

    def turn2():
        transpose_into(v.hid2, v.h2t)
        pairs(2, v.h2t, o.h2p)

    def load_1(k):
        load("1", k, k % 2, o.t2.at[k], v.w1.at[k % 2], v.l1.at[k % 2])

    def fc1(k):
        loads["1", k].wait()

        def tile(t, carry):
            lanes = pl.ds(pl.multiple_of(t * 384, 128), 384)
            u = nn(v.hid2[...], v.w1[k % 2, :, :, :, lanes].reshape(D, 384)) + con.wide[k, :, lanes]
            w = u * u
            th = jnp.tanh(GELU_A * u * (1.0 + GELU_B * w))
            v.act[k, :, lanes] = (0.5 * u * (1.0 + th)).astype(B16)
            v.dact[k, :, lanes] = (0.5 * (1.0 + th) + 0.5 * u * (1.0 - th * th) * (GELU_A * (1.0 + 3.0 * GELU_B * w))).astype(B16)
            return carry

        lax.fori_loop(0, 3, tile, 0)
        if k + 2 < 4:
            load_1(k + 2)
        save(v.act.at[k], o.act.at[k, pl.ds(0, TOK)])
        save(v.dact.at[k], o.dact.at[k])
        c = remote(v.act.at[k], o.act.at[k, pl.ds(TOK, TOK)], v.as_.at[k], v.ar.at[k], p.s_dev)
        c.start()
        waits.append(([c], []))

    table = dict(
        own=g.own, bown=g.bown, arr=g.arr, cross=g.cross, bcross=g.bcross, bz=g.bz_, barr=g.barr, fin=g.fin, have=g.have,
        second=con.second, third=con.third, fourth=con.fourth, last=con.last, begin=con.begin,
        tokens=tokens, norm1=norm1, grads_in=grads_in, turn1=turn1, load_q=load_q, qkv=qkv, heads=heads, mix=mix, load_o=load_o,
        attend=attend, turn2=turn2, load_1=load_1, fc1=fc1,
    )

    p.barrier()
    cq = stage(p, i.w_qkv, v.gq, v.st.at[0], v.rt.at[0])
    cq.start()
    c1 = stage(p, i.w_fc1, v.g1, v.st.at[1], v.rt.at[1])
    c1.start()
    cq.wait_recv()
    join(p, i.w_qkv, v.gq, v.bq)
    g.own(QKV)
    c1.wait_recv()
    join(p, i.w_fc1, v.g1, v.b1)
    for name, args in events:
        table[name](*args)
    cq.wait_send()
    c1.wait_send()
    con.drain()
    g.drain()
    for c in saves:
        c.wait()
    for to_sib, to_own in waits:
        for c in to_own:
            c.wait()
        for c in to_sib:
            c.wait()


def k1_events():
    e = Script()
    e.own(OUT)
    e.begin()
    e.bown(FC1)
    e.bown(FC2)
    e.second()
    e.tokens()
    e.arr(QKV, 1)
    e.third()
    e.cross(QKV, 0)
    e.arr(QKV, 2)
    e.fourth()
    e.cross(QKV, 1)
    e.arr(QKV, 3)
    e.own(FC1)
    e.bcross(FC1)
    e.last()
    e.bz(FC1)
    e.cross(QKV, 2)
    e.arr(OUT, 1)
    e.bcross(FC2)
    e.cross(QKV, 3)
    e.norm1()
    e.bz(FC2)
    e.arr(OUT, 2)
    e.fin(QKV, 0)
    e.cross(OUT, 0)
    e.arr(OUT, 3)
    e.fin(QKV, 1)
    e.cross(OUT, 1)
    e.arr(FC1, 1)
    e.fin(QKV, 2)
    e.own(FC2)
    e.grads_in()
    e.fin(QKV, 3)
    e.cross(OUT, 2)
    e.arr(FC1, 2)
    e.cross(OUT, 3)
    e.have(QKV)
    e.load_q(0)
    e.load_q(1)
    e.cross(FC1, 0)
    e.turn1()
    e.qkv(0)
    e.arr(FC1, 3)
    e.fin(OUT, 0)
    e.qkv(1)
    e.cross(FC1, 1)
    e.fin(OUT, 1)
    e.qkv(2)
    e.barr(FC1, 1)
    e.fin(OUT, 2)
    e.fin(OUT, 3)
    e.qkv(3)
    e.cross(FC1, 2)
    e.arr(FC2, 1)
    e.heads(0, 4)
    e.cross(FC1, 3)
    e.barr(FC1, 2)
    e.heads(4, 4)
    e.arr(FC2, 2)
    e.cross(FC2, 0)
    e.heads(8, 4)
    e.have(OUT)
    e.load_o()
    e.arr(FC2, 3)
    e.heads(12, 4)
    e.cross(FC2, 1)
    e.mix()
    e.barr(FC1, 3)
    e.attend()
    e.fin(FC1, 0)
    e.fin(FC1, 1)
    e.cross(FC2, 2)
    e.fin(FC1, 2)
    e.fin(FC1, 3)
    e.barr(FC2, 1)
    e.cross(FC2, 3)
    e.turn2()
    e.have(FC1)
    e.load_1(0)
    e.load_1(1)
    e.fc1(0)
    e.barr(FC2, 2)
    e.fin(FC2, 0)
    e.fc1(1)
    e.fin(FC2, 1)
    e.fc1(2)
    e.barr(FC2, 3)
    e.fin(FC2, 2)
    e.fc1(3)
    e.fin(FC2, 3)
    e.have(FC2)
    return e.steps


def k1(events, args):
    V, A = pl.BlockSpec(memory_space=pltpu.VMEM), pl.BlockSpec(memory_space=pl.ANY)
    outs = pl.pallas_call(
        functools.partial(k1_kernel, events),
        out_shape=[jax.ShapeDtypeStruct(s, d) for s, d in K1_OUT.values()],
        in_specs=[V] * len(K1_IN),
        out_specs=[A] * len(K1_OUT),
        scratch_shapes=[pltpu.VMEM(s, d) for s, d in K1_VMEM.values()] + [pltpu.SemaphoreType.DMA(s) for s in K1_SEMS.values()] + Conditions.scratch() + Gather.scratch(),
        compiler_params=pltpu.CompilerParams(collective_id=0, has_side_effects=True, vmem_limit_bytes=60 * 2**20),
        name="forward",
    )(*args)
    return dict(zip(K1_OUT, outs, strict=True))


def k1_args(full_input, masked_input, keep_index, cond_full, cond_masked, w_ada, b_ada, w_qkv, b_q, b_v, w_out, b_out, w_fc1, b_fc1, w_fc2, b_fc2, cot_full, cot_masked):
    row = lambda b: b[None, :]
    return (full_input, masked_input, keep_index, cond_full, cond_masked, w_ada, row(b_ada), w_qkv, row(b_q), row(b_v), w_out.T, row(b_out), w_fc1, row(b_fc1), w_fc2.T, row(b_fc2), cot_full, cot_masked)


LANES = (896, 288, 1152, 1152)
B_ROWS = (0, 0, 48, 48)


class Scatter:
    SEMS = dict(sd=(4, 4, 2), rd=(4, 4, 2), sx=(4, 4), rx=(4, 4), sy=(4, 4), ry=(4, 4), sz=(4, 4), rz=(4, 5),
                cz=(4, 4), bz=(4, 5), cd=(4, 2), bd=(4, 2), cx=(4,), bx=(4,), cy=(4,), by=(4,))

    @classmethod
    def scratch(cls):
        out = []
        for m in range(4):
            b, n = B_ROWS[m], LANES[m]
            a = 144 - b
            out += [pltpu.VMEM(s, B16) for s in ((4, a, n), (4, a, n), (4, a, n), (5, a, n))]
            if b:
                out += [pltpu.VMEM(s, B16) for s in ((5, 4, b, n), (b, n), (b, n), (b, n))]
        return out + [pltpu.SemaphoreType.DMA(s) for s in cls.SEMS.values()]

    @classmethod
    def count(cls):
        return sum(8 if b else 4 for b in B_ROWS) + len(cls.SEMS)

    def __init__(self, p, r, refs):
        self.p, self.r = p, r
        refs = list(refs)
        self.ld, self.lx, self.ly, self.lz = [], [], [], []
        self.lbz, self.lbx, self.lby, self.lbd = {}, {}, {}, {}
        for m in range(4):
            for part in (self.ld, self.lx, self.ly, self.lz):
                part.append(refs.pop(0))
            if B_ROWS[m]:
                for part in (self.lbz, self.lbx, self.lby, self.lbd):
                    part[m] = refs.pop(0)
        for name in self.SEMS:
            setattr(self, name, refs.pop(0))

    def blk(self, m, dp, zs, lo, n):
        return self.r[m].at[dp, zs, pl.ds(lo, n), pl.ds(0, LANES[m])]

    def a(self, m):
        return 144 - B_ROWS[m]

    def half(self, m, j):
        a = self.a(m)
        h = (a // 32) * 16
        return a - h if j % 2 == 0 else h

    def got(self, ref, sem):
        remote(ref, ref, self.sd.at[0, 0, 0], sem, self.p.x_dev).wait_recv()

    def add(self, dst, *lands):
        y = dst[...].astype(F32)
        for land in lands:
            y = y + land[...].astype(F32)
        dst[...] = y.astype(B16)

    def c1(self, m, j):
        p, zs, a, h = self.p, self.p.order[j], self.a(m), self.half(m, j)
        one = remote(self.blk(m, p.dg, zs, 0, h), self.ld[m].at[zs, pl.ds(0, h)], self.sd.at[m, zs, 0], self.rd.at[m, zs, 0], p.x_dev)
        two = remote(self.blk(m, p.dg, zs, h, a - h), self.ld[m].at[zs, pl.ds(h, a - h)], self.sd.at[m, zs, 1], self.rd.at[m, zs, 1], p.y_dev)
        return one, two

    def c2(self, m, j):
        p, zs, a = self.p, self.p.order[j], self.a(m)
        y = remote(self.blk(m, p.yn, zs, 0, a), self.ly[m].at[zs], self.sy.at[m, zs], self.ry.at[m, zs], p.y_dev)
        x = remote(self.blk(m, p.xn, zs, 0, a), self.lx[m].at[zs], self.sx.at[m, zs], self.rx.at[m, zs], p.x_dev)
        return y, x

    def cz_(self, m, j):
        p, zs, a = self.p, self.p.order[j], self.a(m)
        up = zs > p.z
        slot = jnp.where(up, zs, jnp.where(zs == p.z - 1, 4, zs))
        return remote(self.blk(m, p.dp, zs, 0, a), self.lz[m].at[slot], self.sz.at[m, zs], self.rz.at[m, slot], (p.dp, p.f + jnp.where(up, 2, -2)))

    def cb(self, m, j):
        p, zs, a, b = self.p, self.p.order[j], self.a(m), B_ROWS[m]
        up = zs > p.z
        slot = jnp.where(up, zs, jnp.where(zs == p.z - 1, 4, zs))
        src = self.r[m].at[:, zs, pl.ds(a, b), pl.ds(0, LANES[m])]
        return remote(src, self.lbz[m].at[slot], self.cz.at[m, zs], self.bz.at[m, slot], (p.dp, p.f + jnp.where(up, 2, -2)))

    def cb2(self, m):
        p, a, b = self.p, self.a(m), B_ROWS[m]
        h = 16 * ((b // 16 + 1) // 2)
        one = remote(self.blk(m, p.dg, p.z, a, h), self.lbd[m].at[pl.ds(0, h)], self.cd.at[m, 0], self.bd.at[m, 0], p.x_dev)
        two = remote(self.blk(m, p.dg, p.z, a + h, b - h), self.lbd[m].at[pl.ds(h, b - h)], self.cd.at[m, 1], self.bd.at[m, 1], p.y_dev)
        return one, two

    def cb3(self, m):
        p, a, b = self.p, self.a(m), B_ROWS[m]
        y = remote(self.blk(m, p.yn, p.z, a, b), self.lby[m], self.cy.at[m], self.by.at[m], p.y_dev)
        x = remote(self.blk(m, p.xn, p.z, a, b), self.lbx[m], self.cx.at[m], self.bx.at[m], p.x_dev)
        return y, x

    def s1(self, m, j):
        for c in self.c1(m, j):
            c.start()

    def s2(self, m, j):
        p, zs, a, h = self.p, self.p.order[j], self.a(m), self.half(m, j)
        y, x = self.c2(m, j)
        land = self.ld[m].at[zs, pl.ds(0, h)]
        self.got(land, self.rd.at[m, zs, 0])
        self.add(self.blk(m, p.yn, zs, 0, h), land)
        y.start()
        land = self.ld[m].at[zs, pl.ds(h, a - h)]
        self.got(land, self.rd.at[m, zs, 1])
        self.add(self.blk(m, p.xn, zs, h, a - h), land)
        x.start()

    def s3(self, m, j):
        p, zs, a = self.p, self.p.order[j], self.a(m)
        self.got(self.lx[m].at[zs], self.rx.at[m, zs])
        self.got(self.ly[m].at[zs], self.ry.at[m, zs])
        self.add(self.blk(m, p.dp, zs, 0, a), self.lx[m].at[zs], self.ly[m].at[zs])

    def zt(self, m, j):
        p, zs, a = self.p, self.p.order[j], self.a(m)

        @pl.when(p.middle)
        def _():
            land = self.lz[m].at[zs]
            self.got(land, self.rz.at[m, zs])
            self.add(self.blk(m, p.dp, zs, 0, a), land)

        self.cz_(m, j).start()

    def both(self, act):
        @pl.when(self.p.z > 0)
        def _():
            act(self.p.z)

        @pl.when(self.p.z < 3)
        def _():
            act(4)

    def zf(self, m):
        p = self.p

        def take(slot):
            land = self.lz[m].at[slot]
            self.got(land, self.rz.at[m, slot])
            self.add(self.blk(m, p.dp, p.z, 0, self.a(m)), land)

        self.both(take)

    def b1(self, m, j):
        p, zs, a, b = self.p, self.p.order[j], self.a(m), B_ROWS[m]

        @pl.when(p.middle)
        def _():
            self.got(self.lbz[m].at[zs], self.bz.at[m, zs])
            for d in range(4):
                self.add(self.blk(m, d, zs, a, b), self.lbz[m].at[zs, d])

        self.cb(m, j).start()

    def bf(self, m):
        p, a, b = self.p, self.a(m), B_ROWS[m]

        def take(slot):
            self.got(self.lbz[m].at[slot], self.bz.at[m, slot])
            for d in range(4):
                self.add(self.blk(m, d, p.z, a, b), self.lbz[m].at[slot, d])

        self.both(take)
        for c in self.cb2(m):
            c.start()

    def b3(self, m):
        p, a, b = self.p, self.a(m), B_ROWS[m]
        h = 16 * ((b // 16 + 1) // 2)
        y, x = self.cb3(m)
        land = self.lbd[m].at[pl.ds(0, h)]
        self.got(land, self.bd.at[m, 0])
        self.add(self.blk(m, p.yn, p.z, a, h), land)
        y.start()
        land = self.lbd[m].at[pl.ds(h, b - h)]
        self.got(land, self.bd.at[m, 1])
        self.add(self.blk(m, p.xn, p.z, a + h, b - h), land)
        x.start()

    def b4(self, m):
        p, a, b = self.p, self.a(m), B_ROWS[m]
        self.got(self.lbx[m], self.bx.at[m])
        self.got(self.lby[m], self.by.at[m])
        self.add(self.blk(m, p.dp, p.z, a, b), self.lbx[m], self.lby[m])

    def sent(self, m):
        for j in range(4):
            for c in self.c1(m, j) + self.c2(m, j):
                c.wait_send()
            if j:
                self.cz_(m, j).wait_send()
                if B_ROWS[m]:
                    self.cb(m, j).wait_send()
        if B_ROWS[m]:
            for c in self.cb2(m) + self.cb3(m):
                c.wait_send()


class Back:
    SEMS = dict(r1=(8,), s1=(8,), r2=(4,), s2=(4,), rb=(4,), sb=(4,), r3=(8,), s3=(8,), r4=(4,), s4=(4,))
    SHAPES = dict(msg=(8, 4, D), in1=(8, 4, D), gm=(16, 864), in2=(4, 16, 864), bs=(1, D), inb=(4, 1, D), sil=(8, 8, 288), silr=(64, 288),
                  gmr=(64, 864), b8=(8, 8, 288), in3=(8, 8, 288), b4=(4, 2, 288), in4=(4, 2, 288))

    @classmethod
    def scratch(cls):
        return [pltpu.VMEM(s, F32) for s in cls.SHAPES.values()] + [pltpu.SemaphoreType.DMA(s) for s in cls.SEMS.values()]

    def __init__(self, p, gmods, gbias, w_ada, scratch):
        self.p, self.gmods, self.gbias, self.w_ada = p, gmods, gbias, w_ada
        for name, ref in zip(list(self.SHAPES) + list(self.SEMS), scratch, strict=True):
            setattr(self, name, ref)

    def over_dp(self, src_of, land, sem_s, sem_r):
        p = self.p
        return [remote(src_of(r), land.at[p.dp], sem_s.at[r], sem_r.at[p.dp], (r, p.f)) for r in p.rows]

    def over_f(self, src_of, land, sem_s, sem_r):
        p = self.p
        return [remote(src_of(c), land.at[p.f], sem_s.at[c], sem_r.at[p.f], (p.dp, c)) for c in p.cols]

    def copies(self, step):
        return {
            1: lambda: self.over_f(lambda c: self.msg.at[c], self.in1, self.s1, self.r1),
            2: lambda: self.over_dp(lambda r: self.gm, self.in2, self.s2, self.r2),
            "b": lambda: self.over_dp(lambda r: self.bs, self.inb, self.sb, self.rb),
            3: lambda: self.over_f(lambda c: self.b8.at[c], self.in3, self.s3, self.r3),
            4: lambda: self.over_dp(lambda r: self.b4.at[r], self.in4, self.s4, self.r4),
        }[step]()

    def send(self, step):
        for c in self.copies(step):
            c.start()

    def arrived(self, land, sem, peers):
        for q in peers:
            remote(land.at[q], land.at[q], self.s1.at[0], sem.at[q], self.p.x_dev).wait_recv()

    def begin(self):
        p = self.p
        for s in range(2):
            for f in range(8):
                at = 864 * f
                while at < 864 * (f + 1):
                    b = at // D
                    end = min(864 * (f + 1), D * (b + 1))
                    self.msg[f, s : s + 1, at - 864 * f : end - 864 * f] = self.gmods[b, s, :, at - D * b : end - D * b].astype(B16).astype(F32)
                    at = end
                self.msg[f, s : s + 1, 864:D] = jnp.zeros((1, D - 864), F32)
        for f in range(8):
            for i, lo in enumerate((0, 144, 288, 1008)):
                self.msg[f, 2:3, lo : lo + 144] = self.gbias[i, :, 144 * f : 144 * f + 144]
            half = 576 * (f % 2)
            self.msg[f, 2:3, 432:1008] = self.gbias[4 + f // 2, :, half : half + 576]
            self.msg[f, 3:4, :] = jnp.zeros((1, D), F32)
        self.send(1)
        self.in1[p.f] = self.msg[p.f]

    def second(self, sil):
        p = self.p
        self.arrived(self.in1, self.r1, p.cols)
        total = jnp.zeros((1, D), F32)
        for f in range(8):
            rows = self.in1[f]
            self.gm[2 * f : 2 * f + 2, :] = rows[0:2, 0:864]
            total = total + rows[2:3]
        self.bs[...] = total
        self.send(2)
        self.send("b")
        self.in2[p.dp] = self.gm[...]
        self.inb[p.dp] = self.bs[...]
        for f in range(8):
            for d in range(4):
                self.silr[16 * d + 2 * f : 16 * d + 2 * f + 2, :] = sil[f, 2 * d : 2 * d + 2]

    def third(self, out_w, out_b, out_biases):
        p = self.p
        self.arrived(self.in2, self.r2, p.rows)
        self.arrived(self.inb, self.rb, p.rows)
        gm = self.in2[...].reshape(64, 864)
        low = gm.astype(B16)
        back = nt(low, self.w_ada[...])
        for f in range(8):
            for d in range(4):
                self.b8[f, 2 * d : 2 * d + 2, :] = back[16 * d + 2 * f : 16 * d + 2 * f + 2]
        self.send(3)
        self.in3[p.f] = self.b8[p.f]
        out_b[...] = jnp.sum(gm, axis=0, keepdims=True)
        out_w[...] = tn(self.silr[...].astype(B16), low)
        row = self.inb[0] + self.inb[1] + self.inb[2] + self.inb[3]
        for ref, lo in zip(out_biases, (0, 144, 288, 432, 1008), strict=True):
            ref[...] = row[:, lo : lo + ref.shape[1]]

    def fourth(self):
        p = self.p
        self.arrived(self.in3, self.r3, p.cols)
        total = self.in3[0]
        for f in range(1, 8):
            total = total + self.in3[f]
        for d in range(4):
            self.b4[d] = total[2 * d : 2 * d + 2]
        self.send(4)
        self.in4[p.dp] = self.b4[p.dp]

    def last(self, conds, outs):
        p = self.p
        self.arrived(self.in4, self.r4, p.rows)
        for s in range(2):
            x = conds[s][...].astype(F32)
            sig = 1.0 / (1.0 + jnp.exp(-x))
            slope = sig * (1.0 + x * (1.0 - sig))
            for d in range(4):
                outs[s][:, 288 * d : 288 * d + 288] = self.in4[d, s : s + 1, :] * slope[:, 288 * d : 288 * d + 288]

    def drain(self):
        for step in (1, 2, "b", 3, 4):
            for c in self.copies(step):
                c.wait_send()


K2_IN_V = dict(keep=0, cond_full=0, cond_masked=0, w_ada=0)
K2_IN_A = tuple(K1_OUT)
K2_OUT_V = dict(
    gc_full=((1, D), F32), gc_masked=((1, D), F32),
    gw_ada=((288, 864), F32), gb_ada=((1, 864), F32), gw_qkv=((2, 144, 432), F32), gb_q=((1, 144), F32), gb_v=((1, 144), F32),
    gw_out=((144, 288), F32), gb_out=((1, 144), F32), gw_fc1=((2, 144, 576), F32), gb_fc1=((1, 576), F32), gw_fc2=((144, D), F32), gb_fc2=((1, 144), F32),
)
K2_OUT_A = dict(result=((TOK, D), B16), gfull=((SEQ, D), F32), gmasked=((SEQ, D), F32), gupp=((4, 2 * TOK, D), B16), gqp=((4, 2 * TOK, 864), B16), gap=((4, 144, 768), B16))
K2_VMEM = dict(
    r_big=((4, 4, 144, D), B16), r_fc1=((4, 4, 144, D), B16), r_out=((4, 4, 144, 288), B16),
    mods=((6, 2, 1, D), F32), bias=((8, 1, D), F32), sil=((8, 8, 288), F32), gmods=((6, 2, 1, D), F32), gbias=((8, 1, D), F32),
    gres=((TOK, D), F32), ga=((TOK, D), B16), tq=((144, 432), B16), rq=((144, 432), B16), t1=((144, 576), B16), r1=((144, 576), B16),
)
K2_SEMS = dict(ms=(4,), ld=(24,), ws=(24,), gs=(4,), gr=(4,), qs=(4,), qr=(4,), ps=(4,), pr=(4,), pl_=(4,), xs=(2,), xr=(2,), fs=(2,))
SCOPE_M = dict(gb=((TOK, D), B16), branch=((TOK, D), F32), gh2=((TOK, D), F32))
SCOPE_W = dict(gbp=((4, 144, 768), B16), actp=((2, 2 * TOK, D), B16), w2=((2, 4, 2, 144, D), B16), w1=((1, 4, 2, 144, D), B16),
           dact=((2, TOK, D), B16), gup=((2, TOK, D), B16))
SCOPE_G = dict(h2p=((4, 144, 768), B16), gupv=((2, 2 * TOK, D), B16))
SCOPE_N = dict(tok=((TOK, D), B16), attn=((TOK, D), F32), cot=((TOK, D), B16), res=((TOK, D), B16))
SCOPE_S = dict(spr=((SEQ, D), F32))
SCOPE_A = dict(gmh=((HEADS, TOK, HEAD_DIM), B16))
SCOPE_O = dict(gat=((8, 144, TOK), B16), gapv=((4, 144, 768), B16), mixp=((2 * TOK, D), B16), wo=((4, 4, 2, 144, 288), B16))
SCOPE_Q = dict(qkv=((48, TOK, HEAD_DIM), B16), wq=((2, 4, 2, 144, 864), B16), gq=((2, TOK, 864), B16),
           gqv=((2, 2 * TOK, 864), B16), h1p=((4, 144, 768), B16), gh1=((TOK, D), F32), tok=((TOK, D), B16))


def k2_kernel(events, *refs):
    i, o, v = Bag(), Bag(), Bag()
    refs = list(refs)
    for n in K2_IN_V:
        setattr(i, n, refs.pop(0))
    for n in ("cot_full", "cot_masked"):
        setattr(i, n, refs.pop(0))
    for n in K2_IN_A:
        setattr(i, "k_" + n, refs.pop(0))
    for n in list(K2_OUT_V) + list(K2_OUT_A):
        setattr(o, n, refs.pop(0))
    for n in list(K2_VMEM) + list(K2_SEMS):
        setattr(v, n, refs.pop(0))
    p = Place()
    n_back = len(Back.SHAPES) + len(Back.SEMS)
    back = Back(p, v.gmods, v.gbias, i.w_ada, refs[:n_back])
    sc = Scatter(p, (v.r_big, v.r_out, v.r_fc1, v.r_big), refs[n_back:])
    loads, ends = {}, []
    count = dict(ld=0, ws=0)

    def load(key, src, dst):
        c = pltpu.make_async_copy(src, dst, v.ld.at[count["ld"] % 24])
        count["ld"] += 1
        c.start()
        loads[key] = c

    def save(src, dst):
        c = pltpu.make_async_copy(src, dst, v.ws.at[count["ws"]])
        count["ws"] += 1
        c.start()
        return c

    pending = {}

    by_dp = (p.dg, p.yn, p.xn, p.dp)
    by_z = p.order[::-1]

    def small():
        for key, dst in (("mods", v.mods), ("bias", v.bias), ("sil", v.sil)):
            load(key, getattr(i, "k_" + key), dst)

    def load_gbp():
        load("gbp", i.k_gbp, v.gbp)

    def load_act(n):
        load(("actp", n), i.k_act.at[by_dp[n]], v.actp.at[n % 2])

    def grad_fc2(n):
        if n == 0:
            loads["gbp"].wait()
        loads["actp", n].wait()
        dp = by_dp[n]

        def tile(t, carry):
            lanes = pl.ds(pl.multiple_of(t * 384, 128), 384)
            y = nn(v.gbp[...].reshape(576, 768), v.actp[n % 2, :, lanes]).astype(B16)
            for z in range(4):
                v.r_big[dp, z, :, lanes] = y[144 * z : 144 * z + 144]
            return carry

        lax.fori_loop(0, 3, tile, 0)
        if n + 2 < 4:
            load_act(n + 2)

    def load_mlp(k):
        s = k % 2
        if k == 0:
            load("gb", i.k_gb, v.gb)
        load(("w2", k), i.k_t3.at[k], v.w2.at[s])
        if k == 0:
            load_w1(k)
        load(("dact", k), i.k_dact.at[k], v.dact.at[s])
        load(("act", k), i.k_act.at[k, pl.ds(0, TOK)], v.actp.at[s, pl.ds(0, TOK)])

    def load_w1(k):
        load(("w1", k), i.k_t2.at[k], v.w1.at[0])

    def mlp(k):
        s = k % 2
        if k == 0:
            loads["gb"].wait()
        loads["w2", k].wait()
        loads["dact", k].wait()
        if k >= 2:
            c, w = pending.pop(("gup", k - 2))
            c.wait_send()
            w.wait()

        def tile(t, carry):
            lanes = pl.ds(pl.multiple_of(t * 384, 128), 384)
            gu = (nn(v.gb[...], v.w2[s, :, :, :, lanes].reshape(D, 384)) * v.dact[s, :, lanes].astype(F32)).astype(B16)
            v.gup[s, :, lanes] = gu
            v.gbias[4 + k, :, lanes] = jnp.sum(gu.astype(F32), axis=0, keepdims=True)
            return carry

        lax.fori_loop(0, 3, tile, 0)
        c = remote(v.gup.at[s], o.gupp.at[k, pl.ds(TOK, TOK)], v.gs.at[k], v.gr.at[k], p.s_dev)
        c.start()
        pending["gup", k] = (c, save(v.gup.at[s], o.gupp.at[k, pl.ds(0, TOK)]))
        loads["w1", k].wait()
        loads["act", k].wait()

        def rows(t, carry):
            r = pl.ds(pl.multiple_of(t * 128, 128), 128)
            one = nt(v.actp[s, r, :], v.w2[s].reshape(D, D))
            two = nt(v.gup[s, r, :], v.w1[0].reshape(D, D))
            if k == 0:
                v.branch[r, :] = one
                v.gh2[r, :] = two
            else:
                v.branch[r, :] += one
                v.gh2[r, :] += two
            return carry

        lax.fori_loop(0, 3, rows, 0)
        if k + 1 < 4:
            load_w1(k + 1)
        if k + 2 < 4:
            load_mlp(k + 2)

    def end_mlp():
        for k in (2, 3):
            c, w = pending.pop(("gup", k))
            c.wait_send()
            w.wait()

    def load_g():
        load("h2p", i.k_h2p, v.h2p)
        for n in range(2):
            load_gup(n)

    def load_gup(n):
        if n == 0:
            for k in range(4):
                sib = o.gupp.at[k, pl.ds(TOK, TOK)]
                remote(sib, sib, v.gs.at[k], v.gr.at[k], p.s_dev).wait_recv()
        load(("gupv", n), o.gupp.at[by_z[n]], v.gupv.at[n % 2])

    def grad_fc1(n):
        if n == 0:
            loads["h2p"].wait()
        loads["gupv", n].wait()
        z = by_z[n]

        def tile(t, carry):
            lanes = pl.ds(pl.multiple_of(t * 384, 128), 384)
            y = nn(v.h2p[...].reshape(576, 768), v.gupv[n % 2, :, lanes]).astype(B16)
            for d in range(4):
                v.r_fc1[d, z, :, lanes] = y[144 * d : 144 * d + 144]
            return carry

        lax.fori_loop(0, 3, tile, 0)
        if n + 2 < 4:
            load_gup(n + 2)

    def end_norm2():
        pending.pop("res").wait()

    def load_n():
        load("cot0", i.cot_full.at[0], cut(v.cot, 0, SEQ))
        load("cot1", i.cot_masked.at[0], cut(v.cot, SEQ, KEEP))
        load("tok", i.k_tok, v.tok)
        load("attn", i.k_attn, v.attn)

    def norm2():
        for key in ("tok", "attn", "cot0", "cot1"):
            loads[key].wait()
        zero = jnp.zeros((1, D), F32)
        for b in range(6):
            for s in range(2):
                v.gmods[b, s] = zero
        v.gbias[2] = zero
        v.gbias[3] = zero

        def body(r, s):
            tok = v.tok[r, :].astype(F32)
            attn = v.attn[r, :]
            resid = tok + v.mods[2, s] * attn
            n, inv = layer_stats(resid)
            branch = v.branch[r, :] + v.bias[3]
            v.res[r, :] = (resid + v.mods[5, s] * branch).astype(B16)
            cot = v.cot[r, :].astype(F32)
            v.gmods[5, s] += jnp.sum(cot * branch, axis=0, keepdims=True)
            gh = v.gh2[r, :]
            v.gmods[4, s] += jnp.sum(gh * n, axis=0, keepdims=True)
            v.gmods[3, s] += jnp.sum(gh, axis=0, keepdims=True)
            u = gh * (1.0 + v.mods[4, s])
            gres = cot + inv * (u - jnp.mean(u, axis=-1, keepdims=True) - n * jnp.mean(u * n, axis=-1, keepdims=True))
            v.gres[r, :] = gres
            v.gmods[2, s] += jnp.sum(gres * attn, axis=0, keepdims=True)
            ga = (v.mods[2, s] * gres).astype(B16)
            v.ga[r, :] = ga
            v.gbias[2] += jnp.sum(ga.astype(F32), axis=0, keepdims=True)
            v.gbias[3] += jnp.sum(v.gb[r, :].astype(F32), axis=0, keepdims=True)

        by_rows(body)
        c = pltpu.make_async_copy(v.res, o.result, v.fs.at[0])
        c.start()
        pending["res"] = c

    def load_o():
        for k in range(4):
            load(("wo", k), i.k_t1.at[k], v.wo.at[k])
        load("mixp", i.k_mixed, v.mixp)

    def turn_a():
        transpose_into(v.ga, v.gat)
        to_sib, to_own = pair_rows(p, v.gat, o.gap, None, v.ps, v.pr, v.pl_)
        for c in to_sib + to_own:
            c.start()
        pending["gap"] = (to_sib, to_own)

    def grad_mixed():
        for k in range(4):
            loads["wo", k].wait()
            y = nn(v.ga[...], v.wo[k].reshape(D, 288)).astype(B16)
            for h in range(4):
                v.gmh[4 * k + h] = y[:, 72 * h : 72 * h + 72]

    def grad_out():
        to_sib, to_own = pending.pop("gap")
        for c in to_sib:
            c.wait()
        for c in to_own:
            c.wait()
        load("gapv", o.gap, v.gapv)
        loads["gapv"].wait()
        loads["mixp"].wait()
        y = nn(v.gapv[...].reshape(576, 768), v.mixp[...]).astype(B16)
        for d in range(4):
            for z in range(4):
                v.r_out[d, z] = y[144 * z : 144 * z + 144, 288 * d : 288 * d + 288]

    def load_q():
        load("qkv", i.k_qkv, v.qkv)
        load("tok", i.k_tok, v.tok)
        load("h1p", i.k_h1p, v.h1p)
        for k in range(2):
            load_wq(k)

    def load_wq(k):
        load(("wq", k), i.k_t0.at[k], v.wq.at[k % 2])

    def heads(k, n):
        if k == 0:
            loads["qkv"].wait()

        def step(h, carry):
            q, key, val, gm = v.qkv[h], v.qkv[16 + h], v.qkv[32 + h], v.gmh[h]
            for lo, hi in ((0, SEQ), (SEQ, TOK)):
                qs, ks, vs, gs = q[lo:hi], key[lo:hi], val[lo:hi], gm[lo:hi]
                probs = softmax(nt(qs, ks) * SCALE)
                gp = nt(gs, vs)
                v.qkv[32 + h, lo:hi] = tn(probs.astype(B16), gs).astype(B16)
                gsc = (probs * (gp - jnp.sum(probs * gp, axis=-1, keepdims=True))).astype(B16)
                v.qkv[h, lo:hi] = (nn(gsc, ks) * SCALE).astype(B16)
                v.qkv[16 + h, lo:hi] = (tn(gsc, qs) * SCALE).astype(B16)
            return carry

        lax.fori_loop(k, k + n, step, 0)

    def grad_h1(k):
        s = k % 2
        if k >= 2:
            c, w = pending.pop(("gq", k - 2))
            c.wait_send()
            w.wait()
        for h in range(12):
            v.gq[s, :, 72 * h : 72 * h + 72] = v.qkv[12 * k + h]
        c = remote(v.gq.at[s], o.gqp.at[k, pl.ds(TOK, TOK)], v.qs.at[k], v.qr.at[k], p.s_dev)
        c.start()
        pending["gq", k] = (c, save(v.gq.at[s], o.gqp.at[k, pl.ds(0, TOK)]))
        if k != 2:
            total = jnp.sum(v.gq[s].astype(F32), axis=0, keepdims=True)
        else:
            total = jnp.sum(v.gq[s, :, 576:864].astype(F32), axis=0, keepdims=True)
        if k == 0:
            v.gbias[0, :, 0:864] = total
        elif k == 1:
            v.gbias[0, :, 864:D] = total[:, 0:288]
        elif k == 2:
            v.gbias[1, :, 0:288] = total
        else:
            v.gbias[1, :, 288:D] = total
        loads["wq", k].wait()

        def rows(t, carry):
            r = pl.ds(pl.multiple_of(t * 128, 128), 128)
            y = nt(v.gq[s, r, :], v.wq[s].reshape(D, 864))
            if k == 0:
                v.gh1[r, :] = y
            else:
                v.gh1[r, :] += y
            return carry

        lax.fori_loop(0, 3, rows, 0)
        if k + 2 < 4:
            load_wq(k + 2)

    def load_gq(n):
        if n == 0:
            for k in range(4):
                sib = o.gqp.at[k, pl.ds(TOK, TOK)]
                remote(sib, sib, v.qs.at[k], v.qr.at[k], p.s_dev).wait_recv()
            for k in (2, 3):
                c, w = pending.pop(("gq", k))
                c.wait_send()
                w.wait()
        load(("gqv", n), o.gqp.at[by_z[n]], v.gqv.at[n % 2])

    def grad_qkv(n):
        if n == 0:
            loads["h1p"].wait()
        loads["gqv", n].wait()
        y = nn(v.h1p[...].reshape(576, 768), v.gqv[n % 2]).astype(B16)
        pad = jnp.zeros((144, 32), B16)
        for d in range(4):
            v.r_big[d, by_z[n], :, 0:864] = y[144 * d : 144 * d + 144]
            v.r_big[d, by_z[n], :, 864:896] = pad
        if n + 2 < 4:
            load_gq(n + 2)

    def norm1():
        loads["tok"].wait()

        def body(r, s):
            n, inv = layer_stats(v.tok[r, :].astype(F32))
            gh = v.gh1[r, :]
            v.gmods[1, s] += jnp.sum(gh * n, axis=0, keepdims=True)
            v.gmods[0, s] += jnp.sum(gh, axis=0, keepdims=True)
            u = gh * (1.0 + v.mods[1, s])
            v.gres[r, :] += inv * (u - jnp.mean(u, axis=-1, keepdims=True) - n * jnp.mean(u * n, axis=-1, keepdims=True))

        by_rows(body)

    def put_full():
        pltpu.make_async_copy(cut(v.gres, 0, SEQ), o.gfull, v.fs.at[0]).start()

    def end_full():
        pltpu.make_async_copy(cut(v.gres, 0, SEQ), o.gfull, v.fs.at[0]).wait()

    def spread():
        hot = (lax.broadcasted_iota(jnp.int32, (SEQ, KEEP), 0) == i.keep[...]).astype(F32)
        v.spr[...] = lax.dot_general(hot, v.gres[SEQ:TOK], (((1,), (0,)), ((), ())), precision=lax.Precision.HIGHEST, preferred_element_type=F32)
        pltpu.make_async_copy(v.spr, o.gmasked, v.fs.at[1]).start()

    def end_spread():
        pltpu.make_async_copy(v.spr, o.gmasked, v.fs.at[1]).wait()

    def out_fc2():
        o.gw_fc2[...] = v.r_big[p.dp, p.z].astype(F32)

    def out_out():
        o.gw_out[...] = v.r_out[p.dp, p.z].astype(F32)

    def swap(block, width, keep, give, land, n):
        first = p.c == 0
        lo, hi = block[:, 0:width], block[:, width : 2 * width]
        give[...] = jnp.where(first, hi, lo)
        keep[p.c] = jnp.where(first, lo, hi).astype(F32)
        remote(give, land, v.xs.at[n], v.xr.at[n], p.s_dev).start()

    def out_fc1():
        swap(v.r_fc1[p.dp, p.z], 576, o.gw_fc1, v.t1, v.r1, 0)

    def out_qkv():
        swap(v.r_big[p.dp, p.z, :, 0:864], 432, o.gw_qkv, v.tq, v.rq, 1)

    def end_fc1():
        remote(v.t1, v.r1, v.xs.at[0], v.xr.at[0], p.s_dev).wait()
        o.gw_fc1[1 - p.c] = v.r1[...].astype(F32)

    def end_qkv():
        remote(v.tq, v.rq, v.xs.at[1], v.xr.at[1], p.s_dev).wait()
        o.gw_qkv[1 - p.c] = v.rq[...].astype(F32)

    def back_second():
        back.second(v.sil)

    def back_third():
        back.third(o.gw_ada, o.gb_ada, (o.gb_q, o.gb_v, o.gb_out, o.gb_fc1, o.gb_fc2))

    def back_last():
        back.last((i.cond_full, i.cond_masked), (o.gc_full, o.gc_masked))

    def ready():
        for key in ("mods", "bias", "sil"):
            loads[key].wait()

    table = {n: f for n, f in locals().items() if callable(f)}
    for n in ("s1", "s2", "s3", "zt", "zf", "b1", "bf", "b3", "b4", "sent"):
        table[n] = getattr(sc, n)
    table.update(back_begin=back.begin, back_fourth=back.fourth)

    def run(queue):
        for name, args in queue:
            if args and isinstance(args[0], dict):
                spec = args[0]

                def scope(*inner, spec=spec):
                    for n, ref in zip(spec, inner, strict=True):
                        setattr(v, n, ref)
                    run(queue)

                pl.run_scoped(scope, *[pltpu.VMEM(s, d) for s, d in spec.values()])
            elif name not in table:
                return
            else:
                table[name](*args)

    p.barrier()
    run(iter(events))
    back.drain()
    pass


def k2_events():
    e = Script()
    e.small()
    e.open(SCOPE_M)
    e.open(SCOPE_W)
    e.load_gbp()
    e.load_act(0)
    e.load_act(1)
    e.grad_fc2(0)
    e.s1(FC2, 3)
    e.s1(FC2, 2)
    e.s1(FC2, 1)
    e.s1(FC2, 0)
    e.grad_fc2(1)
    e.grad_fc2(2)
    e.s2(FC2, 3)
    e.s2(FC2, 2)
    e.grad_fc2(3)
    e.b1(FC2, 3)
    e.s2(FC2, 1)
    e.s2(FC2, 0)
    e.load_mlp(0)
    e.load_mlp(1)
    e.ready()
    e.b1(FC2, 2)
    e.b1(FC2, 1)
    e.mlp(0)
    e.s3(FC2, 3)
    e.zt(FC2, 3)
    e.bf(FC2)
    e.mlp(1)
    e.s3(FC2, 2)
    e.zt(FC2, 2)
    e.b3(FC2)
    e.mlp(2)
    e.s3(FC2, 1)
    e.zt(FC2, 1)
    e.mlp(3)
    e.s3(FC2, 0)
    e.zf(FC2)
    e.b4(FC2)
    e.out_fc2()
    e.end_mlp()
    e.close()
    e.open(SCOPE_G)
    e.load_g()
    e.grad_fc1(0)
    e.b1(FC1, 3)
    e.s1(FC1, 3)
    e.grad_fc1(1)
    e.b1(FC1, 2)
    e.s1(FC1, 2)
    e.s2(FC1, 3)
    e.grad_fc1(2)
    e.b1(FC1, 1)
    e.s1(FC1, 1)
    e.s2(FC1, 2)
    e.grad_fc1(3)
    e.s1(FC1, 0)
    e.close()
    e.s2(FC1, 1)
    e.bf(FC1)
    e.s2(FC1, 0)
    e.open(SCOPE_N)
    e.load_n()
    e.norm2()
    e.s3(FC1, 3)
    e.zt(FC1, 3)
    e.b3(FC1)
    e.s3(FC1, 2)
    e.zt(FC1, 2)
    e.end_norm2()
    e.close()
    e.close()
    e.open(SCOPE_A)
    e.open(SCOPE_O)
    e.load_o()
    e.turn_a()
    e.s3(FC1, 1)
    e.zt(FC1, 1)
    e.grad_mixed()
    e.grad_out()
    e.close()
    e.s1(OUT, 3)
    e.s1(OUT, 2)
    e.s1(OUT, 1)
    e.s1(OUT, 0)
    e.s3(FC1, 0)
    e.zf(FC1)
    e.b4(FC1)
    e.out_fc1()
    e.open(SCOPE_Q)
    e.load_q()
    e.s2(OUT, 3)
    e.s2(OUT, 2)
    e.heads(0, 4)
    e.s2(OUT, 1)
    e.s2(OUT, 0)
    e.heads(4, 4)
    e.s3(OUT, 3)
    e.zt(OUT, 3)
    e.s3(OUT, 2)
    e.zt(OUT, 2)
    e.heads(8, 4)
    e.s3(OUT, 1)
    e.zt(OUT, 1)
    e.s3(OUT, 0)
    e.heads(12, 4)
    e.zf(OUT)
    e.out_out()
    e.sent(FC2)
    e.grad_h1(0)
    e.grad_h1(1)
    e.grad_h1(2)
    e.grad_h1(3)
    e.load_gq(0)
    e.load_gq(1)
    e.grad_qkv(0)
    e.s1(QKV, 3)
    e.grad_qkv(1)
    e.s1(QKV, 2)
    e.s2(QKV, 3)
    e.grad_qkv(2)
    e.s1(QKV, 1)
    e.s2(QKV, 2)
    e.grad_qkv(3)
    e.s1(QKV, 0)
    e.s2(QKV, 1)
    e.norm1()
    e.put_full()
    e.s2(QKV, 0)
    e.close()
    e.close()
    e.open(SCOPE_S)
    e.back_begin()
    e.s3(QKV, 3)
    e.zt(QKV, 3)
    e.back_second()
    e.s3(QKV, 2)
    e.zt(QKV, 2)
    e.back_third()
    e.s3(QKV, 1)
    e.zt(QKV, 1)
    e.back_fourth()
    e.spread()
    e.back_last()
    e.s3(QKV, 0)
    e.zf(QKV)
    e.out_qkv()
    e.end_fc1()
    e.end_qkv()
    e.sent(OUT)
    e.sent(FC1)
    e.sent(QKV)
    e.end_full()
    e.end_spread()
    e.close()
    return e.steps


def k2(events, args, saved):
    V, A = pl.BlockSpec(memory_space=pltpu.VMEM), pl.BlockSpec(memory_space=pl.ANY)
    outs = {**K2_OUT_V, **K2_OUT_A}
    got = pl.pallas_call(
        functools.partial(k2_kernel, events),
        out_shape=[jax.ShapeDtypeStruct(s, d) for s, d in outs.values()],
        in_specs=[V] * len(K2_IN_V) + [A] * (2 + len(K2_IN_A)),
        out_specs=[V] * len(K2_OUT_V) + [A] * len(K2_OUT_A),
        scratch_shapes=[pltpu.VMEM(s, d) for s, d in K2_VMEM.values()] + [pltpu.SemaphoreType.DMA(s) for s in K2_SEMS.values()] + Back.scratch() + Scatter.scratch(),
        compiler_params=pltpu.CompilerParams(collective_id=1, has_side_effects=True, vmem_limit_bytes=63 * 2**20),
        name="backward",
    )(*args, *[saved[n] for n in K2_IN_A])
    return dict(zip(outs, got, strict=True))


def whole(full_input, masked_input, keep_index, cond_full, cond_masked, w_ada, b_ada, w_qkv, b_q, b_v, w_out, b_out, w_fc1, b_fc1, w_fc2, b_fc2, cot_full, cot_masked):
    saved = k1(k1_events(), k1_args(full_input, masked_input, keep_index, cond_full, cond_masked, w_ada, b_ada, w_qkv, b_q, b_v, w_out, b_out, w_fc1, b_fc1, w_fc2, b_fc2, cot_full, cot_masked))
    g = k2(k2_events(), (keep_index, cond_full, cond_masked, w_ada, cot_full, cot_masked), saved)
    return (
        g["result"][None, :SEQ], g["result"][None, SEQ:], g["gfull"][None], g["gmasked"][None], g["gc_full"], g["gc_masked"],
        g["gw_ada"], g["gb_ada"][0], g["gw_qkv"].reshape(288, 432), g["gb_q"][0], g["gb_v"][0], g["gw_out"].T, g["gb_out"][0],
        g["gw_fc1"].reshape(288, 576), g["gb_fc1"][0], g["gw_fc2"].T, g["gb_fc2"][0],
    )


def plain_layer_stats(values):
    centered = values - jnp.mean(values, axis=-1, keepdims=True)
    inverse = lax.rsqrt(jnp.mean(centered * centered, axis=-1, keepdims=True) + 1e-06)
    return (centered * inverse, inverse)


def plain_layer_back(upstream, normed, inverse):
    return inverse * (
        upstream
        - jnp.mean(upstream, axis=-1, keepdims=True)
        - normed * jnp.mean(upstream * normed, axis=-1, keepdims=True)
    )


def plain_gelu_tanh(values):
    return jax.nn.gelu(values, approximate=True)


def plain_expand_mods(piece, full_length, kept_length):
    head_part = jnp.broadcast_to(piece[:, 0:1], (piece.shape[0], full_length, piece.shape[2]))
    tail_part = jnp.broadcast_to(piece[:, 1:2], (piece.shape[0], kept_length, piece.shape[2]))
    return jnp.concatenate([head_part, tail_part], axis=1)


def plain_image_sums(values, full_length):
    return jnp.stack(
        [jnp.sum(values[:, :full_length], axis=1), jnp.sum(values[:, full_length:], axis=1)], axis=1
    )


def plain_forward_pass(tokens, mods, weights, biases, full_length):
    images, length, features = tokens.shape
    head_count = features // HEAD_DIM
    pieces = [
        plain_expand_mods(
            mods[:, :, column * features : (column + 1) * features],
            full_length,
            length - full_length,
        )
        for column in range(6)
    ]
    norm_one, inverse_one = plain_layer_stats(tokens)
    hidden_one = (norm_one * (1.0 + pieces[1]) + pieces[0]).astype(jnp.bfloat16)
    bias_all = jnp.concatenate([biases[1], jnp.zeros((features,), jnp.bfloat16), biases[2]]).astype(
        jnp.float32
    )
    projected = (
        jnp.einsum("itd,de->ite", hidden_one, weights[1], preferred_element_type=jnp.float32)
        + bias_all
    )
    projected = projected.astype(jnp.bfloat16).reshape(images, length, 3, head_count, HEAD_DIM)
    query_rows = projected[:, :, 0]
    key_rows = projected[:, :, 1]
    value_rows = projected[:, :, 2]
    scale_factor = 1.0 / math.sqrt(HEAD_DIM)
    scores = (
        jnp.einsum("iqhc,ikhc->ihqk", query_rows, key_rows, preferred_element_type=jnp.float32)
        * scale_factor
    )
    marker = jnp.arange(length) >= full_length
    same_image = marker[:, None] == marker[None, :]
    scores = jnp.where(same_image, scores, -1e30)
    row_max = jnp.max(scores, axis=-1, keepdims=True)
    exponent = jnp.exp(scores - row_max)
    attention = exponent / jnp.sum(exponent, axis=-1, keepdims=True)
    attention_low = attention.astype(jnp.bfloat16)
    mixed = jnp.einsum(
        "ihqk,ikhc->iqhc", attention_low, value_rows, preferred_element_type=jnp.float32
    )
    mixed = mixed.astype(jnp.bfloat16).reshape(images, length, features)
    attn_out = jnp.einsum(
        "itd,de->ite", mixed, weights[2], preferred_element_type=jnp.float32
    ) + biases[3].astype(jnp.float32)
    residual = tokens + pieces[2] * attn_out
    norm_two, inverse_two = plain_layer_stats(residual)
    hidden_two = (norm_two * (1.0 + pieces[4]) + pieces[3]).astype(jnp.bfloat16)
    upper = jnp.einsum(
        "itd,df->itf", hidden_two, weights[3], preferred_element_type=jnp.float32
    ) + biases[4].astype(jnp.float32)
    activated = plain_gelu_tanh(upper).astype(jnp.bfloat16)
    branch = jnp.einsum(
        "itf,fd->itd", activated, weights[4], preferred_element_type=jnp.float32
    ) + biases[5].astype(jnp.float32)
    result = residual + pieces[5] * branch
    return (
        result,
        pieces,
        norm_one,
        inverse_one,
        hidden_one,
        query_rows,
        key_rows,
        value_rows,
        attention,
        attention_low,
        mixed,
        attn_out,
        norm_two,
        inverse_two,
        hidden_two,
        upper,
        activated,
        branch,
    )


def general(
    full_input,
    masked_input,
    keep_index,
    cond_full,
    cond_masked,
    w_ada,
    b_ada,
    w_qkv,
    b_q,
    b_v,
    w_out,
    b_out,
    w_fc1,
    b_fc1,
    w_fc2,
    b_fc2,
    cot_full,
    cot_masked,
):
    def columns(shard):
        return lax.all_gather(lax.all_gather(shard, ROWS, axis=0, tiled=True), COLS, axis=1, tiled=True)

    weights = (None, columns(w_qkv), columns(w_out), columns(w_fc1), columns(w_fc2))
    widths = [b.shape[0] for b in (b_q, b_v, b_out, b_fc1, b_fc2)]
    packed = lax.all_gather(jnp.concatenate([b_q, b_v, b_out, b_fc1, b_fc2]), COLS, axis=0, tiled=False)
    biases, at = [None], 0
    for width in widths:
        biases.append(packed[:, at : at + width].reshape(-1))
        at += width
    full_length = full_input.shape[1]
    images = full_input.shape[0]
    features = full_input.shape[2]
    picked = jnp.take_along_axis(masked_input, keep_index[:, :, None], axis=1)
    tokens = jnp.concatenate([full_input, picked], axis=1).astype(jnp.float32)
    conds = jnp.stack([cond_full, cond_masked], axis=1).astype(jnp.float32)
    silu_low = jax.nn.silu(conds).astype(jnp.bfloat16)
    n_dp, n_fsdp = lax.axis_size(ROWS), lax.axis_size(COLS)
    rows_ada, cols_ada = w_ada.shape
    every_silu = lax.all_gather(silu_low, (ROWS, COLS), axis=0, tiled=True)
    my_silu = lax.dynamic_slice_in_dim(every_silu, lax.axis_index(ROWS) * rows_ada, rows_ada, axis=2)
    part = jnp.einsum("ijd,de->ije", my_silu, w_ada, preferred_element_type=jnp.float32)
    part = lax.psum_scatter(part, ROWS, scatter_dimension=0, tiled=True)
    part = part + b_ada.astype(jnp.float32)
    mods = lax.all_to_all(part, COLS, split_axis=0, concat_axis=2, tiled=True)
    (
        result,
        pieces,
        norm_one,
        inverse_one,
        hidden_one,
        query_rows,
        key_rows,
        value_rows,
        attention,
        attention_low,
        mixed,
        attn_out,
        norm_two,
        inverse_two,
        hidden_two,
        upper,
        activated,
        branch,
    ) = plain_forward_pass(tokens, mods, weights, biases, full_length)
    length = tokens.shape[1]
    head_count = features // HEAD_DIM
    scale_factor = 1.0 / math.sqrt(HEAD_DIM)
    grad_result = jnp.concatenate([cot_full, cot_masked], axis=1).astype(jnp.float32)
    grad_gate_two = plain_image_sums(grad_result * branch, full_length)
    grad_branch = (pieces[5] * grad_result).astype(jnp.bfloat16)
    grad_b_fc2 = jnp.sum(grad_branch.astype(jnp.float32), axis=(0, 1))
    grad_w_fc2 = jnp.einsum(
        "itf,itd->fd", activated, grad_branch, preferred_element_type=jnp.float32
    )
    grad_act = jnp.einsum(
        "itd,fd->itf", grad_branch, weights[4], preferred_element_type=jnp.float32
    )
    grad_upper = jax.vjp(plain_gelu_tanh, upper)[1](grad_act)[0].astype(jnp.bfloat16)
    grad_b_fc1 = jnp.sum(grad_upper.astype(jnp.float32), axis=(0, 1))
    grad_w_fc1 = jnp.einsum(
        "itd,itf->df", hidden_two, grad_upper, preferred_element_type=jnp.float32
    )
    grad_hidden_two = jnp.einsum(
        "itf,df->itd", grad_upper, weights[3], preferred_element_type=jnp.float32
    )
    grad_scale_two = plain_image_sums(grad_hidden_two * norm_two, full_length)
    grad_shift_two = plain_image_sums(grad_hidden_two, full_length)
    grad_residual = grad_result + plain_layer_back(
        grad_hidden_two * (1.0 + pieces[4]), norm_two, inverse_two
    )
    grad_gate_one = plain_image_sums(grad_residual * attn_out, full_length)
    grad_attn = (pieces[2] * grad_residual).astype(jnp.bfloat16)
    grad_b_out = jnp.sum(grad_attn.astype(jnp.float32), axis=(0, 1))
    grad_w_out = jnp.einsum("itd,ite->de", mixed, grad_attn, preferred_element_type=jnp.float32)
    grad_mixed = jnp.einsum(
        "ite,de->itd", grad_attn, weights[2], preferred_element_type=jnp.float32
    )
    grad_mixed = grad_mixed.astype(jnp.bfloat16).reshape(images, length, head_count, HEAD_DIM)
    grad_attention = jnp.einsum(
        "iqhc,ikhc->ihqk", grad_mixed, value_rows, preferred_element_type=jnp.float32
    )
    grad_values = jnp.einsum(
        "ihqk,iqhc->ikhc", attention_low, grad_mixed, preferred_element_type=jnp.float32
    )
    grad_scores = attention * (
        grad_attention - jnp.sum(attention * grad_attention, axis=-1, keepdims=True)
    )
    grad_scores = grad_scores.astype(jnp.bfloat16)
    grad_queries = (
        jnp.einsum("ihqk,ikhc->iqhc", grad_scores, key_rows, preferred_element_type=jnp.float32)
        * scale_factor
    )
    grad_keys = (
        jnp.einsum("ihqk,iqhc->ikhc", grad_scores, query_rows, preferred_element_type=jnp.float32)
        * scale_factor
    )
    grad_projected = jnp.stack([grad_queries, grad_keys, grad_values], axis=2)
    grad_projected = grad_projected.reshape(images, length, 3 * features).astype(jnp.bfloat16)
    grad_b_q = jnp.sum(grad_projected[:, :, :features].astype(jnp.float32), axis=(0, 1))
    grad_b_v = jnp.sum(grad_projected[:, :, 2 * features :].astype(jnp.float32), axis=(0, 1))
    grad_w_qkv = jnp.einsum(
        "itd,ite->de", hidden_one, grad_projected, preferred_element_type=jnp.float32
    )
    grad_hidden_one = jnp.einsum(
        "ite,de->itd", grad_projected, weights[1], preferred_element_type=jnp.float32
    )
    grad_scale_one = plain_image_sums(grad_hidden_one * norm_one, full_length)
    grad_shift_one = plain_image_sums(grad_hidden_one, full_length)
    grad_tokens = grad_residual + plain_layer_back(
        grad_hidden_one * (1.0 + pieces[1]), norm_one, inverse_one
    )
    grad_mods = jnp.concatenate(
        [
            grad_shift_one,
            grad_scale_one,
            grad_gate_one,
            grad_shift_two,
            grad_scale_two,
            grad_gate_two,
        ],
        axis=-1,
    ).astype(jnp.bfloat16)
    cut = grad_mods.reshape(images, 2, n_fsdp, cols_ada)
    mine = lax.all_to_all(cut, COLS, split_axis=2, concat_axis=0, tiled=False)
    mine = lax.all_gather(mine.reshape(n_fsdp * images, 2, cols_ada), ROWS, axis=0, tiled=True)
    grad_b_ada = jnp.sum(mine.astype(jnp.float32), axis=(0, 1))
    grad_w_ada = jnp.einsum("ijd,ije->de", my_silu, mine, preferred_element_type=jnp.float32)
    back = jnp.einsum("ije,de->ijd", mine, w_ada, preferred_element_type=jnp.float32)
    back = lax.psum_scatter(back.reshape(n_dp, n_fsdp * images, 2, rows_ada), COLS, scatter_dimension=1, tiled=True)
    grad_silu = lax.all_to_all(back, ROWS, split_axis=0, concat_axis=3, tiled=True).reshape(images, 2, features)
    grad_cond = jax.vjp(jax.nn.silu, conds)[1](grad_silu)[0]
    image_rows = jnp.arange(images)[:, None]
    grad_masked = (
        jnp.zeros((images, full_length, features), jnp.float32)
        .at[image_rows, keep_index]
        .set(grad_tokens[:, full_length:])
    )
    def owned(grad):
        inner = lax.psum_scatter(grad.astype(jnp.bfloat16), ROWS, scatter_dimension=0, tiled=True)
        return lax.psum_scatter(inner, COLS, scatter_dimension=1, tiled=True).astype(jnp.float32)

    matrices = (grad_w_ada, owned(grad_w_qkv), owned(grad_w_out), owned(grad_w_fc1), owned(grad_w_fc2))
    sums = (grad_b_q, grad_b_v, grad_b_out, grad_b_fc1, grad_b_fc2)
    line = jnp.concatenate([g.reshape(n_fsdp, -1) for g in sums], axis=1)
    line = lax.psum(lax.psum_scatter(line, COLS, scatter_dimension=0, tiled=True), ROWS)[0]
    vectors, at = [grad_b_ada], 0
    for width in widths:
        vectors.append(line[at : at + width])
        at += width
    return (
        result[:, :full_length].astype(jnp.bfloat16),
        result[:, full_length:].astype(jnp.bfloat16),
        grad_tokens[:, :full_length],
        grad_masked,
        grad_cond[:, 0],
        grad_cond[:, 1],
        matrices[0],
        vectors[0],
        matrices[1],
        vectors[1],
        vectors[2],
        matrices[2],
        vectors[3],
        matrices[3],
        vectors[4],
        matrices[4],
        vectors[5],
    )


def solution(mesh):
    special = dict(mesh.shape) == {ROWS: 4, COLS: 8}
    return jax.shard_map(
        whole if special else general,
        mesh=mesh,
        in_specs=(
            P((ROWS, COLS), None, None),
            P((ROWS, COLS), None, None),
            P((ROWS, COLS), None),
            P((ROWS, COLS), None),
            P((ROWS, COLS), None),
            P(ROWS, COLS),
            P(COLS),
            P(ROWS, COLS),
            P(COLS),
            P(COLS),
            P(ROWS, COLS),
            P(COLS),
            P(ROWS, COLS),
            P(COLS),
            P(ROWS, COLS),
            P(COLS),
            P((ROWS, COLS), None, None),
            P((ROWS, COLS), None, None),
        ),
        out_specs=(
            P((ROWS, COLS), None, None),
            P((ROWS, COLS), None, None),
            P((ROWS, COLS), None, None),
            P((ROWS, COLS), None, None),
            P((ROWS, COLS), None),
            P((ROWS, COLS), None),
            P(ROWS, COLS),
            P(COLS),
            P(ROWS, COLS),
            P(COLS),
            P(COLS),
            P(ROWS, COLS),
            P(COLS),
            P(ROWS, COLS),
            P(COLS),
            P(ROWS, COLS),
            P(COLS),
        ),
        check_vma=False,
    )
```

```python
import functools
import math
import jax
import jax.numpy as jnp
from jax import lax
from jax.experimental import pallas as pl
from jax.experimental.pallas import tpu as pltpu
from jax.sharding import PartitionSpec as P


MESH = pl.DeviceIdType.MESH
ROWS, COLS = "dp", "fsdp"
F32, B16 = jnp.float32, jnp.bfloat16
D, HEADS, HEAD_DIM, SEQ, KEEP, TOK = 1152, 16, 72, 256, 128, 384
SCALE = 1.0 / math.sqrt(HEAD_DIM)
GELU_A, GELU_B = math.sqrt(2.0 / math.pi), 0.044715
MATS = ((864, True, 32), (288, False, 0), (1152, True, 32), (1152, False, 32))
QKV, OUT, FC1, FC2 = range(4)


def nn(a, b):
    return lax.dot_general(a, b, (((1,), (0,)), ((), ())), preferred_element_type=F32)


def nt(a, b):
    return lax.dot_general(a, b, (((1,), (1,)), ((), ())), preferred_element_type=F32)


def tn(a, b):
    return lax.dot_general(a, b, (((0,), (0,)), ((), ())), preferred_element_type=F32)


class Script:
    def __init__(self):
        self.steps = []

    def __getattr__(self, name):
        return lambda *args: self.steps.append((name, args))


class Place:
    def __init__(self):
        self.dp = dp = lax.axis_index(ROWS)
        self.f = f = lax.axis_index(COLS)
        self.z, self.c = f // 2, f % 2
        self.xn = dp + 1 - 2 * (dp % 2)
        self.yn = (dp + 2) % 4
        self.dg = 3 - dp
        self.sf = f + 1 - 2 * self.c
        z = self.z
        self.middle = (z == 1) | (z == 2)
        low = z < 2
        self.order = (z, z + 1 - 2 * (z % 2), jnp.where(low, 2, 1), jnp.where(low, 3, 0))
        self.x_dev, self.y_dev, self.d_dev, self.s_dev = (self.xn, f), (self.yn, f), (self.dg, f), (dp, self.sf)
        self.rows = [(self.dp + k) % 4 for k in (1, 2, 3)]
        self.cols = [(self.f + k) % 8 for k in range(1, 8)]

    def barrier(self):
        sem = pltpu.get_barrier_semaphore()
        for dev in [(r, self.f) for r in self.rows] + [(self.dp, c) for c in self.cols]:
            pl.semaphore_signal(sem, inc=1, device_id=dev, device_id_type=MESH)
        pl.semaphore_wait(sem, 10)


def remote(src, dst, send, recv, dev):
    return pltpu.make_async_remote_copy(src_ref=src, dst_ref=dst, send_sem=send, recv_sem=recv, device_id=dev, device_id_type=MESH)


def cut(ref, lo, n):
    return ref.at[pl.ds(lo, n)]


class Gather:
    SEMS = dict(rz=(4, 4), rx=(4, 4), ry=(4, 4), rd=(4, 4, 2), rs=(4, 4), so=(4, 2), sf=(4, 4), sx=(4, 4), sy=(4, 4), sd=(4, 4, 2),
                ss=(4, 4), loc=(4,), bx=(4,), by=(4,), bd=(4, 2), bz=(4, 4), cx=(4,), cy=(4,), cd=(4, 2), co=(4, 2), cf=(4, 4))

    def __init__(self, p, bufs, blks, sems):
        self.p, self.bufs, self.blks = p, bufs, blks
        for name, sem in zip(self.SEMS, sems, strict=True):
            setattr(self, name, sem)

    @classmethod
    def scratch(cls):
        return [pltpu.SemaphoreType.DMA(s) for s in cls.SEMS.values()]

    def a(self, m):
        return 144 - MATS[m][2]

    def split(self, m, j):
        a = self.a(m)
        h = (a // 32) * 16
        return (a - h, h) if j % 2 == 0 else (h, a - h)

    def slot(self, m, dp, zs):
        t = self.bufs[m]
        return t.at[zs, dp, self.p.c] if MATS[m][1] else t.at[dp, zs, self.p.c]

    def top(self, m, dp, zs):
        return cut(self.slot(m, dp, zs), 0, self.a(m))

    def low(self, m, dp, zs):
        return cut(self.slot(m, dp, zs), self.a(m), MATS[m][2])

    def low4(self, m, zs):
        t, rows = self.bufs[m], pl.ds(self.a(m), MATS[m][2])
        return t.at[zs, :, self.p.c, rows] if MATS[m][1] else t.at[:, zs, self.p.c, rows]

    def plane(self, m, zs, c):
        t = self.bufs[m]
        return t.at[zs, :, c] if MATS[m][1] else t.at[:, zs, c]

    def z_copies(self, m):
        p = self.p
        blk = cut(self.blks[m], 0, self.a(m))
        dst = self.top(m, p.dp, p.z)
        up = remote(blk, dst, self.so.at[m, 0], self.rz.at[m, p.z], (p.dp, p.f + 2))
        down = remote(blk, dst, self.so.at[m, 1], self.rz.at[m, p.z], (p.dp, p.f - 2))
        return up, down

    def bz_copies(self, m):
        p = self.p
        src = self.low4(m, p.z)
        up = remote(src, src, self.co.at[m, 0], self.bz.at[m, p.z], (p.dp, p.f + 2))
        down = remote(src, src, self.co.at[m, 1], self.bz.at[m, p.z], (p.dp, p.f - 2))
        return up, down

    def pass_on(self, m, zs):
        p = self.p
        src = self.top(m, p.dp, zs)
        return remote(src, src, self.sf.at[m, zs], self.rz.at[m, zs], (p.dp, p.f + jnp.where(zs < p.z, 2, -2)))

    def pass_low(self, m, zs):
        p = self.p
        src = self.low4(m, zs)
        return remote(src, src, self.cf.at[m, zs], self.bz.at[m, zs], (p.dp, p.f + jnp.where(zs < p.z, 2, -2)))

    def x_copy(self, m, src, zs):
        return remote(src, self.top(m, self.p.dp, zs), self.sx.at[m, zs], self.rx.at[m, zs], self.p.x_dev)

    def y_copy(self, m, src, zs):
        return remote(src, self.top(m, self.p.dp, zs), self.sy.at[m, zs], self.ry.at[m, zs], self.p.y_dev)

    def d_copy(self, m, j, zs, half):
        p = self.p
        a, b = self.split(m, j)
        lo, n = ((0, a), (a, b))[half]
        src = cut(self.slot(m, p.xn if half == 0 else p.yn, zs), lo, n)
        return remote(src, src, self.sd.at[m, zs, half], self.rd.at[m, zs, half], p.y_dev if half == 0 else p.x_dev)

    def bd_copy(self, m, half):
        p = self.p
        h = 16 * ((MATS[m][2] // 16 + 1) // 2)
        lo, n = ((0, h), (h, MATS[m][2] - h))[half]
        src = cut(self.slot(m, p.xn if half == 0 else p.yn, p.z), self.a(m) + lo, n)
        return remote(src, src, self.cd.at[m, half], self.bd.at[m, half], p.y_dev if half == 0 else p.x_dev)

    def s_copy(self, m, zs):
        src = self.plane(m, zs, self.p.c)
        return remote(src, src, self.ss.at[m, zs], self.rs.at[m, zs], self.p.s_dev)

    def ends(self, copies, act):
        p = self.p

        @pl.when(p.z < 3)
        def _():
            act(copies[0])

        @pl.when(p.z > 0)
        def _():
            act(copies[1])

    def got(self, ref, recv):
        remote(ref, ref, self.so.at[0, 0], recv, self.p.x_dev).wait_recv()

    def own(self, m):
        p = self.p
        self.ends(self.z_copies(m), lambda c: c.start())
        blk = cut(self.blks[m], 0, self.a(m))
        self.x_copy(m, blk, p.z).start()
        self.y_copy(m, blk, p.z).start()
        if not MATS[m][2]:
            pltpu.make_async_copy(self.blks[m], self.slot(m, p.dp, p.z), self.loc.at[m]).start()

    def bown(self, m):
        p = self.p
        pltpu.make_async_copy(self.blks[m], self.slot(m, p.dp, p.z), self.loc.at[m]).start()
        blk = cut(self.blks[m], self.a(m), MATS[m][2])
        dst = self.low(m, p.dp, p.z)
        remote(blk, dst, self.cx.at[m], self.bx.at[m], p.x_dev).start()
        remote(blk, dst, self.cy.at[m], self.by.at[m], p.y_dev).start()

    def arr(self, m, j):
        p = self.p
        zs = p.order[j]
        src = self.top(m, p.dp, zs)
        self.got(src, self.rz.at[m, zs])

        @pl.when(p.middle)
        def _():
            self.pass_on(m, zs).start()

        self.x_copy(m, src, zs).start()
        self.y_copy(m, src, zs).start()

    def cross(self, m, j):
        p = self.p
        zs = p.order[j]
        self.got(self.top(m, p.xn, zs), self.rx.at[m, zs])
        self.d_copy(m, j, zs, 0).start()
        self.got(self.top(m, p.yn, zs), self.ry.at[m, zs])
        self.d_copy(m, j, zs, 1).start()

    def bcross(self, m):
        p = self.p
        self.got(self.low(m, p.xn, p.z), self.bx.at[m])
        self.bd_copy(m, 0).start()
        self.got(self.low(m, p.yn, p.z), self.by.at[m])
        self.bd_copy(m, 1).start()

    def bz_(self, m):
        p = self.p
        h = 16 * ((MATS[m][2] // 16 + 1) // 2)
        for half, (lo, n) in enumerate(((0, h), (h, MATS[m][2] - h))):
            self.got(cut(self.slot(m, p.dg, p.z), self.a(m) + lo, n), self.bd.at[m, half])
        pltpu.make_async_copy(self.blks[m], self.slot(m, p.dp, p.z), self.loc.at[m]).wait()
        self.ends(self.bz_copies(m), lambda c: c.start())

    def barr(self, m, j):
        zs = self.p.order[j]
        self.got(self.low4(m, zs), self.bz.at[m, zs])

        @pl.when(self.p.middle)
        def _():
            self.pass_low(m, zs).start()

    def fin(self, m, j):
        p = self.p
        zs = p.order[j]
        a, b = self.split(m, j)
        for half, (lo, n) in enumerate(((0, a), (a, b))):
            self.got(cut(self.slot(m, p.dg, zs), lo, n), self.rd.at[m, zs, half])
        if j == 0 and not MATS[m][2]:
            pltpu.make_async_copy(self.blks[m], self.slot(m, p.dp, p.z), self.loc.at[m]).wait()
        self.s_copy(m, zs).start()

    def have(self, m):
        for j in range(4):
            zs = self.p.order[j]
            self.got(self.plane(m, zs, 1 - self.p.c), self.rs.at[m, zs])

    def drain(self):
        p = self.p
        for m in range(4):
            blk = cut(self.blks[m], 0, self.a(m))
            self.ends(self.z_copies(m), lambda c: c.wait_send())
            if MATS[m][2]:
                low = cut(self.blks[m], self.a(m), MATS[m][2])
                dst = self.low(m, p.dp, p.z)
                remote(low, dst, self.cx.at[m], self.bx.at[m], p.x_dev).wait_send()
                remote(low, dst, self.cy.at[m], self.by.at[m], p.y_dev).wait_send()
                self.bd_copy(m, 0).wait_send()
                self.bd_copy(m, 1).wait_send()
                self.ends(self.bz_copies(m), lambda c: c.wait_send())
            for j in range(4):
                zs = p.order[j]
                src = self.top(m, p.dp, zs)
                if j:

                    @pl.when(p.middle)
                    def _(m=m, zs=zs):
                        self.pass_on(m, zs).wait_send()
                        if MATS[m][2]:
                            self.pass_low(m, zs).wait_send()

                self.x_copy(m, src, zs).wait_send()
                self.y_copy(m, src, zs).wait_send()
                self.d_copy(m, j, zs, 0).wait_send()
                self.d_copy(m, j, zs, 1).wait_send()
                self.s_copy(m, zs).wait_send()


def stage(p, shard, got, send, recv):
    rows = shard.shape[0] // 2
    return remote(cut(shard, (1 - p.c) * rows, rows), got, send, recv, p.s_dev)


def join(p, shard, got, blk):
    rows, width = got.shape
    own = shard[pl.ds(pl.multiple_of(p.c * rows, 16), rows), :]
    other = got[...]
    first = p.c == 0
    blk[:, 0:width] = jnp.where(first, own, other)
    blk[:, width : 2 * width] = jnp.where(first, other, own)


class Conditions:
    SEMS = dict(r1=(4,), s1=(4,), r2=(8,), s2=(8,), rb=(8,), sb=(8,), r3=(4,), s3=(4,), r4=(8,), s4=(8,))
    SHAPES = dict(sil4=(4, 2, 288), in1=(4, 2, 288), row8=(8, 288), in2=(8, 8, 288), pack=(1, D), inb=(8, 1, D), p3=(4, 16, 864),
                  in3=(4, 16, 864), m8=(8, 2, 864), in4=(8, 2, 864), mods=(6, 2, 1, D), bias=(8, 1, D), wide=(4, 1, D), qkvb=(4, 1, 864))

    @classmethod
    def scratch(cls):
        return [pltpu.VMEM(s, F32) for s in cls.SHAPES.values()] + [pltpu.SemaphoreType.DMA(s) for s in cls.SEMS.values()]

    def __init__(self, p, conds, w_ada, pack, scratch):
        self.p, self.conds, self.w_ada, self.given = p, conds, w_ada, pack
        for name, ref in zip(list(self.SHAPES) + list(self.SEMS), scratch, strict=True):
            setattr(self, name, ref)

    def over_dp(self, src_of, land, sem_s, sem_r):
        p = self.p
        return [remote(src_of(r), land.at[p.dp], sem_s.at[r], sem_r.at[p.dp], (r, p.f)) for r in p.rows]

    def over_f(self, src_of, land, sem_s, sem_r):
        p = self.p
        return [remote(src_of(c), land.at[p.f], sem_s.at[c], sem_r.at[p.f], (p.dp, c)) for c in p.cols]

    def copies(self, step):
        return {
            1: lambda: self.over_dp(lambda r: self.sil4.at[r], self.in1, self.s1, self.r1),
            2: lambda: self.over_f(lambda c: self.row8, self.in2, self.s2, self.r2),
            "b": lambda: self.over_f(lambda c: self.pack, self.inb, self.sb, self.rb),
            3: lambda: self.over_dp(lambda r: self.p3.at[r], self.in3, self.s3, self.r3),
            4: lambda: self.over_f(lambda c: self.m8.at[c], self.in4, self.s4, self.r4),
        }[step]()

    def send(self, step):
        for c in self.copies(step):
            c.start()

    def arrived(self, land, sem, peers):
        for q in peers:
            remote(land.at[q], land.at[q], self.s1.at[0], sem.at[q], self.p.x_dev).wait_recv()

    def begin(self):
        p = self.p
        self.pack[...] = self.given[:, 864:2016].astype(F32)
        self.send("b")
        self.inb[p.f] = self.pack[...]
        for s, cond in enumerate(self.conds):
            x = cond[...].astype(F32)
            y = (x / (1.0 + jnp.exp(-x))).astype(B16).astype(F32)
            for d in range(4):
                self.sil4[d, s : s + 1, :] = y[:, 288 * d : 288 * d + 288]
        self.send(1)
        self.in1[p.dp] = self.sil4[p.dp]

    def second(self):
        p = self.p
        self.arrived(self.in1, self.r1, p.rows)
        for d in range(4):
            self.row8[2 * d : 2 * d + 2, :] = self.in1[d]
        self.send(2)
        self.in2[p.f] = self.row8[...]

    def third(self):
        p = self.p
        self.arrived(self.in2, self.r2, p.cols)
        rows = self.in2[...].reshape(64, 288).astype(B16)
        part = nn(rows, self.w_ada[...])
        for d in range(4):
            for f in range(8):
                self.p3[d, 2 * f : 2 * f + 2, :] = part[8 * f + 2 * d : 8 * f + 2 * d + 2]
        self.send(3)
        self.in3[p.dp] = self.p3[p.dp]

    def fourth(self):
        p = self.p
        self.arrived(self.in3, self.r3, p.rows)
        total = self.in3[0] + self.in3[1] + self.in3[2] + self.in3[3] + self.given[:, 0:864].astype(F32)
        for f in range(8):
            self.m8[f] = total[2 * f : 2 * f + 2]
        self.send(4)
        self.in4[p.f] = self.m8[p.f]

    def last(self):
        p = self.p
        self.arrived(self.in4, self.r4, p.cols)
        self.arrived(self.inb, self.rb, p.cols)
        for f in range(8):
            rows = self.in4[f]
            at = 864 * f
            while at < 864 * (f + 1):
                b = at // D
                end = min(864 * (f + 1), D * (b + 1))
                for s in range(2):
                    self.mods[b, s, :, at - D * b : end - D * b] = rows[s : s + 1, at - 864 * f : end - 864 * f]
                at = end
        for f in range(8):
            row = self.inb[f]
            for i, lo in enumerate((0, 144, 288, 1008)):
                self.bias[i, :, 144 * f : 144 * f + 144] = row[:, lo : lo + 144]
            half = 576 * (f % 2)
            self.wide[f // 2, :, half : half + 576] = row[:, 432:1008]
        line = jnp.concatenate([self.bias[0], jnp.zeros((1, D), F32), self.bias[1]], axis=1)
        for k in range(4):
            self.qkvb[k] = line[:, 864 * k : 864 * k + 864]

    def drain(self):
        for step in (1, 2, "b", 3, 4):
            for c in self.copies(step):
                c.wait_send()


def layer_stats(x):
    mean = jnp.mean(x, axis=-1, keepdims=True)
    centered = x - mean
    inv = lax.rsqrt(jnp.mean(centered * centered, axis=-1, keepdims=True) + 1e-6)
    return centered * inv, inv


def by_rows(body):
    def step(i, carry):
        body(pl.ds(pl.multiple_of(i * 128, 128), 128), i // 2)
        return carry

    lax.fori_loop(0, 3, step, 0)


def transpose_into(src, dst):
    for i in range(3):
        for k in range(9):
            t = src[128 * i : 128 * i + 128, 128 * k : 128 * k + 128].astype(F32).T.astype(B16)
            at = 128 * k
            while at < 128 * (k + 1):
                b = at // 144
                end = min(128 * (k + 1), 144 * (b + 1))
                dst[b, at - 144 * b : end - 144 * b, 128 * i : 128 * i + 128] = t[at - 128 * k : end - 128 * k]
                at = end


def pair_rows(p, mine, land, send, recv, loc):
    to_sib = [remote(mine.at[2 * k + (1 - p.c)], land.at[k, :, pl.ds(384, 384)], send.at[k], recv.at[k], p.s_dev) for k in range(4)]
    to_own = [pltpu.make_async_copy(mine.at[2 * k + p.c], land.at[k, :, pl.ds(0, 384)], loc.at[k]) for k in range(4)]
    return to_sib + to_own


class Bag:
    pass


def forward_steps(p, i, o, v, con):
    saves = []

    def save(pair):
        n = len(saves)
        saves.append(lambda: pltpu.make_async_copy(*pair(), v.ow.at[n]))
        saves[n]().start()

    waits = []

    def pairs(k, mine, land):
        waits.append(lambda: pair_rows(p, mine(), land, v.pt.at[k], v.pr.at[k], v.pl_.at[k]))
        for c in waits[-1]():
            c.start()

    loads = {}

    def load(name, k, slot, src, dst, sem):
        c = pltpu.make_async_copy(src, dst, sem)
        c.start()
        loads[name, k] = c

    def get_tokens():
        for n, (key, src, dst) in enumerate((("full", i.full, cut(v.tok, 0, SEQ)), ("masked", i.masked, v.masked), ("cot0", i.cot_full, cut(v.cot, 0, SEQ)), ("cot1", i.cot_masked, cut(v.cot, SEQ, KEEP)))):
            loads[key] = pltpu.make_async_copy(src.at[0], dst, v.lt.at[n])
            loads[key].start()

    def tokens():
        for key in ("full", "masked", "cot0", "cot1"):
            loads[key].wait()
        spread = (lax.broadcasted_iota(jnp.int32, (SEQ, KEEP), 0) == i.keep[...]).astype(B16)
        v.tok[SEQ:TOK] = tn(spread, v.masked[...]).astype(B16)
        save(lambda: (v.tok, o.tok))

    def norm1():
        def body(r, s):
            n, _ = layer_stats(v.tok[r, :].astype(F32))
            v.hid[r, :] = (n * (1.0 + con.mods[1, s]) + con.mods[0, s]).astype(B16)

        by_rows(body)

    def grads_in():
        v.gb[0:SEQ] = (con.mods[5, 0] * v.cot[0:SEQ].astype(F32)).astype(B16)
        v.gb[SEQ:TOK] = (con.mods[5, 1] * v.cot[SEQ:TOK].astype(F32)).astype(B16)
        save(lambda: (v.gb, o.gb))
        transpose_into(v.gb, v.gbt)
        pairs(0, lambda: v.gbt, o.gbp)

    def turn1():
        transpose_into(v.hid, v.h1t)
        pairs(1, lambda: v.h1t, o.h1p)

    def load_q(k):
        load("q", k, k % 2, o.t0.at[k], v.wq.at[k % 2], v.lq.at[k % 2])

    def qkv(k):
        loads["q", k].wait()
        y = (nn(v.hid[...], v.wq[k % 2].reshape(D, 864)) + con.qkvb[k]).astype(B16)
        for h in range(12):
            v.qkv[12 * k + h] = y[:, 72 * h : 72 * h + 72]
        if k + 2 < 4:
            load_q(k + 2)
        if k == 3:
            pltpu.make_async_copy(v.qkv, o.qkv, v.oq.at[0]).start()

    def end_qkv():
        pltpu.make_async_copy(v.qkv, o.qkv, v.oq.at[0]).wait()

    def f_end():
        for s in saves:
            s().wait()
        for w in waits:
            for c in w():
                c.wait()

    def heads(k, n):
        def step(g, carry):
            parts = [(4 * g + u, lo, hi) for u in range(4) for lo, hi in ((0, SEQ), (SEQ, TOK))]
            scores = [nt(v.qkv[h, lo:hi], v.qkv[16 + h, lo:hi]) * SCALE for h, lo, hi in parts]
            exps = [jnp.exp(x - jnp.max(x, axis=-1, keepdims=True)) for x in scores]
            probs = [(e * (1.0 / jnp.sum(e, axis=-1, keepdims=True))).astype(B16) for e in exps]
            for (h, lo, hi), pr in zip(parts, probs):
                v.mixh[h, lo:hi] = nn(pr, v.qkv[32 + h, lo:hi]).astype(B16)
            return carry

        lax.fori_loop(k // 4, (k + n) // 4, step, 0)

    def mix():
        for h in range(HEADS):
            v.mixed[:, 72 * h : 72 * h + 72] = v.mixh[h]
        save(lambda: (v.mixed, cut(o.mixed, 0, TOK)))
        waits.append(lambda: [remote(v.mixed, cut(o.mixed, TOK, TOK), v.ms.at[0], v.mr.at[0], p.s_dev)])
        waits[-1]()[0].start()

    def load_o():
        for k in range(4):
            load("o", k, k, o.t1.at[k], v.wo.at[k], v.lo.at[k])

    def attend():
        for k in range(4):
            loads["o", k].wait()

        def body(r, s):
            y = con.bias[2] + jnp.zeros((128, 1), F32)
            for k in range(4):
                y = y + nt(v.mixed[r, 288 * k : 288 * k + 288], v.wo[k].reshape(D, 288))
            v.attn[r, :] = y
            resid = v.tok[r, :].astype(F32) + con.mods[2, s] * y
            n, _ = layer_stats(resid)
            v.hid2[r, :] = (n * (1.0 + con.mods[4, s]) + con.mods[3, s]).astype(B16)

        by_rows(body)
        save(lambda: (v.attn, o.attn))

    def turn2():
        transpose_into(v.hid2, v.h2t)
        pairs(2, lambda: v.h2t, o.h2p)

    def load_1(k):
        load("1", k, k % 2, o.t2.at[k], v.w1.at[k % 2], v.l1.at[k % 2])

    def fc1(k):
        loads["1", k].wait()

        def tile(t, carry):
            lanes = pl.ds(pl.multiple_of(t * 384, 128), 384)
            u = nn(v.hid2[...], v.w1[k % 2, :, :, :, lanes].reshape(D, 384)) + con.wide[k, :, lanes]
            w = u * u
            th = jnp.tanh(GELU_A * u * (1.0 + GELU_B * w))
            v.act[k, :, lanes] = (0.5 * u * (1.0 + th)).astype(B16)
            v.dact[k, :, lanes] = (0.5 * (1.0 + th) + 0.5 * u * (1.0 - th * th) * (GELU_A * (1.0 + 3.0 * GELU_B * w))).astype(B16)
            return carry

        lax.fori_loop(0, 3, tile, 0)
        if k + 2 < 4:
            load_1(k + 2)
        save(lambda: (v.act.at[k], o.act.at[k, pl.ds(0, TOK)]))
        save(lambda: (v.dact.at[k], o.dact.at[k]))
        waits.append(lambda: [remote(v.act.at[k], o.act.at[k, pl.ds(TOK, TOK)], v.as_.at[k], v.ar.at[k], p.s_dev)])
        waits[-1]()[0].start()

    return dict(get_tokens=get_tokens, tokens=tokens, norm1=norm1, grads_in=grads_in, turn1=turn1, load_q=load_q, qkv=qkv, heads=heads, mix=mix, load_o=load_o,
                attend=attend, turn2=turn2, load_1=load_1, fc1=fc1, end_qkv=end_qkv, f_end=f_end)


LANES = (896, 288, 1152, 1152)
B_ROWS = (32, 0, 32, 32)


class Scatter:
    SEMS = dict(sd=(4, 4, 2), rd=(4, 4, 2), sx=(4, 4), rx=(4, 4), sy=(4, 4), ry=(4, 4), sz=(4, 4), rz=(4, 5),
                cz=(4, 4), bz=(4, 5), cd=(4, 2), bd=(4, 2), cx=(4,), bx=(4,), cy=(4,), by=(4,))

    @classmethod
    def scratch(cls):
        out = []
        for m in range(4):
            b, n = B_ROWS[m], LANES[m]
            a = 144 - b
            out += [pltpu.VMEM(s, B16) for s in ((4, a, n), (4, a, n), (4, a, n), (5, a, n))]
            if b:
                out += [pltpu.VMEM(s, B16) for s in ((5, 4, b, n), (b, n), (b, n), (b, n))]
        return out + [pltpu.SemaphoreType.DMA(s) for s in cls.SEMS.values()]

    @classmethod
    def count(cls):
        return sum(8 if b else 4 for b in B_ROWS) + len(cls.SEMS)

    def __init__(self, p, r, refs):
        self.p, self.r = p, r
        refs = list(refs)
        self.ld, self.lx, self.ly, self.lz = [], [], [], []
        self.lbz, self.lbx, self.lby, self.lbd = {}, {}, {}, {}
        for m in range(4):
            for part in (self.ld, self.lx, self.ly, self.lz):
                part.append(refs.pop(0))
            if B_ROWS[m]:
                for part in (self.lbz, self.lbx, self.lby, self.lbd):
                    part[m] = refs.pop(0)
        for name in self.SEMS:
            setattr(self, name, refs.pop(0))

    def blk(self, m, dp, zs, lo, n):
        return self.r[m].at[dp, zs, pl.ds(lo, n), pl.ds(0, LANES[m])]

    def a(self, m):
        return 144 - B_ROWS[m]

    def half(self, m, j):
        a = self.a(m)
        h = (a // 32) * 16
        return a - h if j % 2 == 0 else h

    def got(self, ref, sem):
        remote(ref, ref, self.sd.at[0, 0, 0], sem, self.p.x_dev).wait_recv()

    def add(self, dst, *lands):
        y = dst[...].astype(F32)
        for land in lands:
            y = y + land[...].astype(F32)
        dst[...] = y.astype(B16)

    def c1(self, m, j):
        p, zs, a, h = self.p, self.p.order[j], self.a(m), self.half(m, j)
        one = remote(self.blk(m, p.dg, zs, 0, h), self.ld[m].at[zs, pl.ds(0, h)], self.sd.at[m, zs, 0], self.rd.at[m, zs, 0], p.x_dev)
        two = remote(self.blk(m, p.dg, zs, h, a - h), self.ld[m].at[zs, pl.ds(h, a - h)], self.sd.at[m, zs, 1], self.rd.at[m, zs, 1], p.y_dev)
        return one, two

    def c2(self, m, j):
        p, zs, a = self.p, self.p.order[j], self.a(m)
        y = remote(self.blk(m, p.yn, zs, 0, a), self.ly[m].at[zs], self.sy.at[m, zs], self.ry.at[m, zs], p.y_dev)
        x = remote(self.blk(m, p.xn, zs, 0, a), self.lx[m].at[zs], self.sx.at[m, zs], self.rx.at[m, zs], p.x_dev)
        return y, x

    def cz_(self, m, j):
        p, zs, a = self.p, self.p.order[j], self.a(m)
        up = zs > p.z
        slot = jnp.where(up, zs, jnp.where(zs == p.z - 1, 4, zs))
        return remote(self.blk(m, p.dp, zs, 0, a), self.lz[m].at[slot], self.sz.at[m, zs], self.rz.at[m, slot], (p.dp, p.f + jnp.where(up, 2, -2)))

    def cb(self, m, j):
        p, zs, a, b = self.p, self.p.order[j], self.a(m), B_ROWS[m]
        up = zs > p.z
        slot = jnp.where(up, zs, jnp.where(zs == p.z - 1, 4, zs))
        src = self.r[m].at[:, zs, pl.ds(a, b), pl.ds(0, LANES[m])]
        return remote(src, self.lbz[m].at[slot], self.cz.at[m, zs], self.bz.at[m, slot], (p.dp, p.f + jnp.where(up, 2, -2)))

    def cb2(self, m):
        p, a, b = self.p, self.a(m), B_ROWS[m]
        h = 16 * ((b // 16 + 1) // 2)
        one = remote(self.blk(m, p.dg, p.z, a, h), self.lbd[m].at[pl.ds(0, h)], self.cd.at[m, 0], self.bd.at[m, 0], p.x_dev)
        two = remote(self.blk(m, p.dg, p.z, a + h, b - h), self.lbd[m].at[pl.ds(h, b - h)], self.cd.at[m, 1], self.bd.at[m, 1], p.y_dev)
        return one, two

    def cb3(self, m):
        p, a, b = self.p, self.a(m), B_ROWS[m]
        y = remote(self.blk(m, p.yn, p.z, a, b), self.lby[m], self.cy.at[m], self.by.at[m], p.y_dev)
        x = remote(self.blk(m, p.xn, p.z, a, b), self.lbx[m], self.cx.at[m], self.bx.at[m], p.x_dev)
        return y, x

    def s1(self, m, j):
        for c in self.c1(m, j):
            c.start()

    def s2(self, m, j):
        p, zs, a, h = self.p, self.p.order[j], self.a(m), self.half(m, j)
        y, x = self.c2(m, j)
        land = self.ld[m].at[zs, pl.ds(0, h)]
        self.got(land, self.rd.at[m, zs, 0])
        self.add(self.blk(m, p.yn, zs, 0, h), land)
        y.start()
        land = self.ld[m].at[zs, pl.ds(h, a - h)]
        self.got(land, self.rd.at[m, zs, 1])
        self.add(self.blk(m, p.xn, zs, h, a - h), land)
        x.start()

    def s3(self, m, j):
        p, zs, a = self.p, self.p.order[j], self.a(m)
        self.got(self.lx[m].at[zs], self.rx.at[m, zs])
        self.got(self.ly[m].at[zs], self.ry.at[m, zs])
        self.add(self.blk(m, p.dp, zs, 0, a), self.lx[m].at[zs], self.ly[m].at[zs])

    def zt(self, m, j):
        p, zs, a = self.p, self.p.order[j], self.a(m)

        @pl.when(p.middle)
        def _():
            land = self.lz[m].at[zs]
            self.got(land, self.rz.at[m, zs])
            self.add(self.blk(m, p.dp, zs, 0, a), land)

        self.cz_(m, j).start()

    def both(self, act):
        @pl.when(self.p.z > 0)
        def _():
            act(self.p.z)

        @pl.when(self.p.z < 3)
        def _():
            act(4)

    def zf(self, m):
        p = self.p

        def take(slot):
            land = self.lz[m].at[slot]
            self.got(land, self.rz.at[m, slot])
            self.add(self.blk(m, p.dp, p.z, 0, self.a(m)), land)

        self.both(take)

    def b1(self, m, j):
        p, zs, a, b = self.p, self.p.order[j], self.a(m), B_ROWS[m]

        @pl.when(p.middle)
        def _():
            self.got(self.lbz[m].at[zs], self.bz.at[m, zs])
            for d in range(4):
                self.add(self.blk(m, d, zs, a, b), self.lbz[m].at[zs, d])

        self.cb(m, j).start()

    def bf(self, m):
        p, a, b = self.p, self.a(m), B_ROWS[m]

        def take(slot):
            self.got(self.lbz[m].at[slot], self.bz.at[m, slot])
            for d in range(4):
                self.add(self.blk(m, d, p.z, a, b), self.lbz[m].at[slot, d])

        self.both(take)
        for c in self.cb2(m):
            c.start()

    def b3(self, m):
        p, a, b = self.p, self.a(m), B_ROWS[m]
        h = 16 * ((b // 16 + 1) // 2)
        y, x = self.cb3(m)
        land = self.lbd[m].at[pl.ds(0, h)]
        self.got(land, self.bd.at[m, 0])
        self.add(self.blk(m, p.yn, p.z, a, h), land)
        y.start()
        land = self.lbd[m].at[pl.ds(h, b - h)]
        self.got(land, self.bd.at[m, 1])
        self.add(self.blk(m, p.xn, p.z, a + h, b - h), land)
        x.start()

    def b4(self, m):
        p, a, b = self.p, self.a(m), B_ROWS[m]
        self.got(self.lbx[m], self.bx.at[m])
        self.got(self.lby[m], self.by.at[m])
        self.add(self.blk(m, p.dp, p.z, a, b), self.lbx[m], self.lby[m])

    def sent(self, m):
        for j in range(4):
            for c in self.c1(m, j) + self.c2(m, j):
                c.wait_send()
            if j:
                self.cz_(m, j).wait_send()
                if B_ROWS[m]:
                    self.cb(m, j).wait_send()
        if B_ROWS[m]:
            for c in self.cb2(m) + self.cb3(m):
                c.wait_send()


class Back:
    SEMS = dict(r1=(8,), s1=(8,), r2=(4,), s2=(4,), rb=(4,), sb=(4,), r3=(8,), s3=(8,), r4=(4,), s4=(4,))
    SHAPES = dict(msg=(8, 4, D), in1=(8, 4, D), gm=(16, 864), in2=(4, 16, 864), bs=(1, D), inb=(4, 1, D), sil=(8, 8, 288), silr=(64, 288),
                  gmr=(64, 864), b8=(8, 8, 288), in3=(8, 8, 288), b4=(4, 2, 288), in4=(4, 2, 288))

    @classmethod
    def scratch(cls):
        return [pltpu.VMEM(s, F32) for s in cls.SHAPES.values()] + [pltpu.SemaphoreType.DMA(s) for s in cls.SEMS.values()]

    def __init__(self, p, gmods, gbias, w_ada, scratch):
        self.p, self.gmods, self.gbias, self.w_ada = p, gmods, gbias, w_ada
        for name, ref in zip(list(self.SHAPES) + list(self.SEMS), scratch, strict=True):
            setattr(self, name, ref)

    def over_dp(self, src_of, land, sem_s, sem_r):
        p = self.p
        return [remote(src_of(r), land.at[p.dp], sem_s.at[r], sem_r.at[p.dp], (r, p.f)) for r in p.rows]

    def over_f(self, src_of, land, sem_s, sem_r):
        p = self.p
        return [remote(src_of(c), land.at[p.f], sem_s.at[c], sem_r.at[p.f], (p.dp, c)) for c in p.cols]

    def copies(self, step):
        return {
            1: lambda: self.over_f(lambda c: self.msg.at[c], self.in1, self.s1, self.r1),
            2: lambda: self.over_dp(lambda r: self.gm, self.in2, self.s2, self.r2),
            "b": lambda: self.over_dp(lambda r: self.bs, self.inb, self.sb, self.rb),
            3: lambda: self.over_f(lambda c: self.b8.at[c], self.in3, self.s3, self.r3),
            4: lambda: self.over_dp(lambda r: self.b4.at[r], self.in4, self.s4, self.r4),
        }[step]()

    def send(self, step):
        for c in self.copies(step):
            c.start()

    def arrived(self, land, sem, peers):
        for q in peers:
            remote(land.at[q], land.at[q], self.s1.at[0], sem.at[q], self.p.x_dev).wait_recv()

    def begin(self):
        p = self.p
        for s in range(2):
            for f in range(8):
                at = 864 * f
                while at < 864 * (f + 1):
                    b = at // D
                    end = min(864 * (f + 1), D * (b + 1))
                    self.msg[f, s : s + 1, at - 864 * f : end - 864 * f] = self.gmods[b, s, :, at - D * b : end - D * b].astype(B16).astype(F32)
                    at = end
                self.msg[f, s : s + 1, 864:D] = jnp.zeros((1, D - 864), F32)
        for f in range(8):
            for i, lo in enumerate((0, 144, 288, 1008)):
                self.msg[f, 2:3, lo : lo + 144] = self.gbias[i, :, 144 * f : 144 * f + 144]
            half = 576 * (f % 2)
            self.msg[f, 2:3, 432:1008] = self.gbias[4 + f // 2, :, half : half + 576]
            self.msg[f, 3:4, :] = jnp.zeros((1, D), F32)
        self.send(1)
        self.in1[p.f] = self.msg[p.f]

    def second(self, sil):
        p = self.p
        self.arrived(self.in1, self.r1, p.cols)
        total = jnp.zeros((1, D), F32)
        for f in range(8):
            rows = self.in1[f]
            self.gm[2 * f : 2 * f + 2, :] = rows[0:2, 0:864]
            total = total + rows[2:3]
        self.bs[...] = total
        self.send(2)
        self.send("b")
        self.in2[p.dp] = self.gm[...]
        self.inb[p.dp] = self.bs[...]
        for f in range(8):
            for d in range(4):
                self.silr[16 * d + 2 * f : 16 * d + 2 * f + 2, :] = sil[f, 2 * d : 2 * d + 2]

    def third(self, out_w, out_b, out_biases):
        p = self.p
        self.arrived(self.in2, self.r2, p.rows)
        self.arrived(self.inb, self.rb, p.rows)
        gm = self.in2[...].reshape(64, 864)
        low = gm.astype(B16)
        back = nt(low, self.w_ada[...])
        for f in range(8):
            for d in range(4):
                self.b8[f, 2 * d : 2 * d + 2, :] = back[16 * d + 2 * f : 16 * d + 2 * f + 2]
        self.send(3)
        self.in3[p.f] = self.b8[p.f]
        out_b[...] = jnp.sum(gm, axis=0, keepdims=True)
        out_w[...] = tn(self.silr[...].astype(B16), low)
        row = self.inb[0] + self.inb[1] + self.inb[2] + self.inb[3]
        for ref, lo in zip(out_biases, (0, 144, 288, 432, 1008), strict=True):
            ref[...] = row[:, lo : lo + ref.shape[1]]

    def fourth(self):
        p = self.p
        self.arrived(self.in3, self.r3, p.cols)
        total = self.in3[0]
        for f in range(1, 8):
            total = total + self.in3[f]
        for d in range(4):
            self.b4[d] = total[2 * d : 2 * d + 2]
        self.send(4)
        self.in4[p.dp] = self.b4[p.dp]

    def last(self, conds, outs):
        p = self.p
        self.arrived(self.in4, self.r4, p.rows)
        for s in range(2):
            x = conds[s][...].astype(F32)
            sig = 1.0 / (1.0 + jnp.exp(-x))
            slope = sig * (1.0 + x * (1.0 - sig))
            for d in range(4):
                outs[s][:, 288 * d : 288 * d + 288] = self.in4[d, s : s + 1, :] * slope[:, 288 * d : 288 * d + 288]

    def drain(self):
        for step in (1, 2, "b", 3, 4):
            for c in self.copies(step):
                c.wait_send()


def backward_steps(p, i, o, v, con, back):
    loads, ends = {}, []
    count = dict(ld=0, ws=0)

    def load(key, src, dst):
        c = pltpu.make_async_copy(src, dst, v.ld.at[count["ld"] % 24])
        count["ld"] += 1
        c.start()
        loads[key] = c

    def save(src, dst):
        c = pltpu.make_async_copy(src, dst, v.ws.at[count["ws"]])
        count["ws"] += 1
        c.start()
        return c

    pending = {}

    by_dp = (p.dg, p.yn, p.xn, p.dp)
    by_z = p.order[::-1]

    def load_gbp():
        load("gbp", o.gbp, v.gbp)

    def load_act(n):
        load(("actp", n), o.act.at[by_dp[n]], v.actp.at[n % 2])

    def grad_fc2(n):
        if n == 0:
            loads["gbp"].wait()
        loads["actp", n].wait()
        dp = by_dp[n]

        y = nn(v.gbp[...].reshape(576, 768), v.actp[n % 2]).astype(B16)
        for z in range(4):
            v.r_big[dp, z] = y[144 * z : 144 * z + 144]
        if n + 2 < 4:
            load_act(n + 2)

    def load_mlp(k):
        s = k % 2
        if k == 0:
            load("gb", o.gb, v.gb)
        load(("w2", k), o.t3.at[k], v.w2.at[s])
        if k == 0:
            load_w1(k)
        load(("dact", k), o.dact.at[k], v.dact.at[s])

    def load_w1(k):
        load(("w1", k), o.t2.at[k], v.w1.at[0])

    def mlp(k):
        s = k % 2
        if k == 0:
            loads["gb"].wait()
        loads["w2", k].wait()
        loads["dact", k].wait()
        if k >= 2:
            c, w = pending.pop(("gup", k - 2))
            c.wait_send()
            w.wait()

        gu = (nn(v.gb[...], v.w2[s].reshape(D, D)) * v.dact[s].astype(F32)).astype(B16)
        v.gup[s] = gu
        v.gbias[4 + k] = jnp.sum(gu.astype(F32), axis=0, keepdims=True)
        c = remote(v.gup.at[s], o.gupp.at[k, pl.ds(TOK, TOK)], v.gs.at[k], v.gr.at[k], p.s_dev)
        c.start()
        pending["gup", k] = (c, save(v.gup.at[s], o.gupp.at[k, pl.ds(0, TOK)]))
        loads["w1", k].wait()

        two = nt(v.gup[s], v.w1[0].reshape(D, D))
        v.gh2[...] = two if k == 0 else v.gh2[...] + two
        if k + 1 < 4:
            load_w1(k + 1)
        if k + 2 < 4:
            load_mlp(k + 2)

    def end_mlp():
        for k in (2, 3):
            c, w = pending.pop(("gup", k))
            c.wait_send()
            w.wait()

    def load_g():
        load("h2p", o.h2p, v.h2p)
        for n in range(2):
            load_gup(n)

    def load_gup(n):
        if n == 0:
            for k in range(4):
                sib = o.gupp.at[k, pl.ds(TOK, TOK)]
                remote(sib, sib, v.gs.at[k], v.gr.at[k], p.s_dev).wait_recv()
        load(("gupv", n), o.gupp.at[by_z[n]], v.gupv.at[n % 2])

    def grad_fc1(n):
        if n == 0:
            loads["h2p"].wait()
        loads["gupv", n].wait()
        z = by_z[n]

        y = nn(v.h2p[...].reshape(576, 768), v.gupv[n % 2]).astype(B16)
        for d in range(4):
            v.r_fc1[d, z] = y[144 * d : 144 * d + 144]
        if n + 2 < 4:
            load_gup(n + 2)

    def load_x():
        for n in range(2):
            load_branch(n)
        load_n()

    def load_branch(k):
        load(("w2", k), o.t3.at[k], v.w2.at[k % 2])
        load(("act", k), o.act.at[k, pl.ds(0, TOK)], v.acto.at[k % 2])

    def branch(k):
        loads["w2", k].wait()
        loads["act", k].wait()
        one = nt(v.acto[k % 2], v.w2[k % 2].reshape(D, D))
        v.branch[...] = one if k == 0 else v.branch[...] + one
        if k + 2 < 4:
            load_branch(k + 2)

    def result():
        for key in ("tok", "attn", "cot0", "cot1"):
            loads[key].wait()

        def body(r, s):
            branch = v.branch[r, :] + con.bias[3]
            v.res[r, :] = (v.tok[r, :].astype(F32) + con.mods[2, s] * v.attn[r, :] + con.mods[5, s] * branch).astype(B16)
            v.gmods[5, s] += jnp.sum(v.cot[r, :].astype(F32) * branch, axis=0, keepdims=True)

        by_rows(body)
        pltpu.make_async_copy(v.res, o.result, v.fs.at[0]).start()

    def end_result():
        pltpu.make_async_copy(v.res, o.result, v.fs.at[0]).wait()

    def load_n():
        load("cot0", i.cot_full.at[0], cut(v.cot, 0, SEQ))
        load("cot1", i.cot_masked.at[0], cut(v.cot, SEQ, KEEP))
        load("tok", o.tok, v.tok)
        load("attn", o.attn, v.attn)

    def norm2():
        for key in ("tok", "attn", "cot0", "cot1"):
            loads[key].wait()
        zero = jnp.zeros((1, D), F32)
        for b in range(6):
            for s in range(2):
                v.gmods[b, s] = zero
        v.gbias[2] = zero
        v.gbias[3] = zero

        def body(r, s):
            tok = v.tok[r, :].astype(F32)
            attn = v.attn[r, :]
            resid = tok + con.mods[2, s] * attn
            n, inv = layer_stats(resid)
            cot = v.cot[r, :].astype(F32)
            gh = v.gh2[r, :]
            v.gmods[4, s] += jnp.sum(gh * n, axis=0, keepdims=True)
            v.gmods[3, s] += jnp.sum(gh, axis=0, keepdims=True)
            u = gh * (1.0 + con.mods[4, s])
            gres = cot + inv * (u - jnp.mean(u, axis=-1, keepdims=True) - n * jnp.mean(u * n, axis=-1, keepdims=True))
            v.gres[r, :] = gres
            v.gmods[2, s] += jnp.sum(gres * attn, axis=0, keepdims=True)
            ga = (con.mods[2, s] * gres).astype(B16)
            v.ga[r, :] = ga
            v.gbias[2] += jnp.sum(ga.astype(F32), axis=0, keepdims=True)
            v.gbias[3] += jnp.sum(v.gb[r, :].astype(F32), axis=0, keepdims=True)

        by_rows(body)

    def load_o():
        for k in range(4):
            load(("wo", k), o.t1.at[k], v.wo.at[k])

    def load_m():
        load("mixp", o.mixed, v.mixp)

    def turn_a():
        transpose_into(v.ga, v.gat)
        pending["gap"] = pair_rows(p, v.gat, o.gap, v.ps, v.gpr, v.pb)
        for c in pending["gap"]:
            c.start()

    def grad_mixed():
        for k in range(4):
            loads["wo", k].wait()
            y = nn(v.ga[...], v.wo[k].reshape(D, 288)).astype(B16)
            for h in range(4):
                v.gmh[4 * k + h] = y[:, 72 * h : 72 * h + 72]

    def grad_out():
        for c in pending.pop("gap"):
            c.wait()
        load("gapv", o.gap, v.gapv)
        loads["gapv"].wait()
        loads["mixp"].wait()
        y = nn(v.gapv[...].reshape(576, 768), v.mixp[...]).astype(B16)
        for d in range(4):
            for z in range(4):
                v.r_out[d, z] = y[144 * z : 144 * z + 144, 288 * d : 288 * d + 288]

    def load_q():
        load("qkv", o.qkv, v.qkv)
        load("tok", o.tok, v.tok)
        load("h1p", o.h1p, v.h1p)
        for k in range(2):
            load_wq(k)

    def load_wq(k):
        load(("wq", k), o.t0.at[k], v.wq.at[k % 2])

    def heads(k, n):
        if k == 0:
            loads["qkv"].wait()

        def step(g, carry):
            parts = [(4 * g + u, lo, hi) for u in range(4) for lo, hi in ((0, SEQ), (SEQ, TOK))]
            qs, ks, vs = ([v.qkv[16 * n + h, lo:hi] for h, lo, hi in parts] for n in range(3))
            gs = [v.gmh[h, lo:hi] for h, lo, hi in parts]
            scores = [nt(key, q) * SCALE for q, key in zip(qs, ks)]
            gps = [nt(val, gm) for val, gm in zip(vs, gs)]
            exps = [jnp.exp(x - jnp.max(x, axis=0, keepdims=True)) for x in scores]
            probs = [e * (1.0 / jnp.sum(e, axis=0, keepdims=True)) for e in exps]
            gsc = [(pr * (gp - jnp.sum(pr * gp, axis=0, keepdims=True))).astype(B16) for pr, gp in zip(probs, gps)]
            for (h, lo, hi), pr, gc, q, key, gm in zip(parts, probs, gsc, qs, ks, gs):
                v.qkv[32 + h, lo:hi] = nn(pr.astype(B16), gm).astype(B16)
                v.qkv[h, lo:hi] = (tn(gc, key) * SCALE).astype(B16)
                v.qkv[16 + h, lo:hi] = (nn(gc, q) * SCALE).astype(B16)
            return carry

        lax.fori_loop(k // 4, (k + n) // 4, step, 0)

    def grad_h1(k):
        s = k % 2
        if k >= 2:
            c, w = pending.pop(("gq", k - 2))
            c.wait_send()
            w.wait()
        for h in range(12):
            v.gq[s, :, 72 * h : 72 * h + 72] = v.qkv[12 * k + h]
        c = remote(v.gq.at[s], o.gqp.at[k, pl.ds(TOK, TOK)], v.qs.at[k], v.qr.at[k], p.s_dev)
        c.start()
        pending["gq", k] = (c, save(v.gq.at[s], o.gqp.at[k, pl.ds(0, TOK)]))
        if k != 2:
            total = jnp.sum(v.gq[s].astype(F32), axis=0, keepdims=True)
        else:
            total = jnp.sum(v.gq[s, :, 576:864].astype(F32), axis=0, keepdims=True)
        if k == 0:
            v.gbias[0, :, 0:864] = total
        elif k == 1:
            v.gbias[0, :, 864:D] = total[:, 0:288]
        elif k == 2:
            v.gbias[1, :, 0:288] = total
        else:
            v.gbias[1, :, 288:D] = total
        loads["wq", k].wait()

        y = nt(v.gq[s], v.wq[s].reshape(D, 864))
        v.gh1[...] = y if k == 0 else v.gh1[...] + y
        if k + 2 < 4:
            load_wq(k + 2)

    def load_gq(n):
        if n == 0:
            for k in range(4):
                sib = o.gqp.at[k, pl.ds(TOK, TOK)]
                remote(sib, sib, v.qs.at[k], v.qr.at[k], p.s_dev).wait_recv()
            for k in (2, 3):
                c, w = pending.pop(("gq", k))
                c.wait_send()
                w.wait()
        load(("gqv", n), o.gqp.at[by_z[n]], v.gqv.at[n % 2])

    def grad_qkv(n):
        if n == 0:
            loads["h1p"].wait()
        loads["gqv", n].wait()
        y = nn(v.h1p[...].reshape(576, 768), v.gqv[n % 2]).astype(B16)
        pad = jnp.zeros((144, 32), B16)
        for d in range(4):
            v.r_big[d, by_z[n], :, 0:864] = y[144 * d : 144 * d + 144]
            v.r_big[d, by_z[n], :, 864:896] = pad
        if n + 2 < 4:
            load_gq(n + 2)

    def norm1():
        loads["tok"].wait()

        def body(r, s):
            n, inv = layer_stats(v.tok[r, :].astype(F32))
            gh = v.gh1[r, :]
            v.gmods[1, s] += jnp.sum(gh * n, axis=0, keepdims=True)
            v.gmods[0, s] += jnp.sum(gh, axis=0, keepdims=True)
            u = gh * (1.0 + con.mods[1, s])
            v.gres[r, :] += inv * (u - jnp.mean(u, axis=-1, keepdims=True) - n * jnp.mean(u * n, axis=-1, keepdims=True))

        by_rows(body)

    def put_full():
        pltpu.make_async_copy(cut(v.gres, 0, SEQ), o.gfull, v.fs.at[3]).start()

    def end_full():
        pltpu.make_async_copy(cut(v.gres, 0, SEQ), o.gfull, v.fs.at[3]).wait()

    def spread():
        hot = (lax.broadcasted_iota(jnp.int32, (SEQ, KEEP), 0) == i.keep[...]).astype(F32)
        v.spr[...] = lax.dot_general(hot, v.gres[SEQ:TOK], (((1,), (0,)), ((), ())), precision=lax.Precision.HIGHEST, preferred_element_type=F32)
        pltpu.make_async_copy(v.spr, o.gmasked, v.fs.at[1]).start()

    def end_spread():
        pltpu.make_async_copy(v.spr, o.gmasked, v.fs.at[1]).wait()

    def put(n, src, dst):
        return pltpu.make_async_copy(src, dst, v.fo.at[n])

    def finals(n):
        if n == 0:
            return put(0, v.r_big.at[p.dp, p.z], o.gw_fc2)
        if n == 1:
            return put(1, v.r_out.at[p.dp, p.z], o.gw_out)
        return put(n, (v.t1, v.tq)[n - 2].at[0], (o.gw_fc1, o.gw_qkv)[n - 2].at[p.c])

    def swaps(n):
        return remote((v.t1, v.tq)[n].at[1], (o.gw_fc1, o.gw_qkv)[n].at[p.c], v.xs.at[n], v.xr.at[n], p.s_dev)

    def out_fc2():
        finals(0).start()

    def out_out():
        finals(1).start()

    def swap(block, width, part, n):
        first = p.c == 0
        lo, hi = block[:, 0:width], block[:, width : 2 * width]
        part[1] = jnp.where(first, hi, lo)
        part[0] = jnp.where(first, lo, hi)
        finals(2 + n).start()
        swaps(n).start()

    def out_fc1():
        swap(v.r_fc1[p.dp, p.z], 576, v.t1, 0)

    def out_qkv():
        swap(v.r_big[p.dp, p.z, :, 0:864], 432, v.tq, 1)

    def end_swap(n):
        swaps(n).wait_send()
        land = (o.gw_fc1, o.gw_qkv)[n].at[1 - p.c]
        remote(land, land, v.xs.at[n], v.xr.at[n], p.s_dev).wait_recv()

    def end_fc2():
        finals(0).wait()

    def end_out():
        finals(1).wait()

    def end_fc1():
        finals(2).wait()
        end_swap(0)

    def end_gqkv():
        finals(3).wait()
        end_swap(1)

    def back_second():
        back.second(con.in2)

    def back_third():
        back.third(v.gwa, o.gb_ada, (o.gb_q, o.gb_v, o.gb_out, o.gb_fc1, o.gb_fc2))

        pltpu.make_async_copy(v.gwa, o.gw_ada, v.fs.at[2]).start()

    def end_ada():
        pltpu.make_async_copy(v.gwa, o.gw_ada, v.fs.at[2]).wait()

    def back_last():
        back.last((i.cond_full, i.cond_masked), (o.gc_full, o.gc_masked))

    table = {n: f for n, f in locals().items() if callable(f)}
    table.update(back_begin=back.begin, back_fourth=back.fourth)
    return table


STAGE = dict(got_q=((144, 432), B16), got_1=((144, 576), B16), bq=((144, 864), B16), b1=((144, 1152), B16),
             gmods=((6, 2, 1, D), F32), gbias=((8, 1, D), F32), t1=((2, 144, 576), B16), tq=((2, 144, 432), B16))
SIGNALS = dict(st=(2,), rt=(2,), lq=(2,), lo=(4,), l1=(2,), lt=(4,), pt=(3, 4), pr=(3, 4), pl_=(3, 4), ms=(1,), mr=(1,), as_=(4,), ar=(4,), ow=(16,), oq=(1,),
               ld=(24,), ws=(24,), gs=(4,), gr=(4,), qs=(4,), qr=(4,), ps=(4,), pb=(4,), gpr=(4,), xs=(2,), xr=(2,), fs=(4,), fo=(4,))
SCOPE_P = dict(hid=((TOK, D), B16), hid2=((TOK, D), B16), tok=((TOK, D), B16), h1t=((8, 144, TOK), B16), h2t=((8, 144, TOK), B16), gbt=((8, 144, TOK), B16),
           gb=((TOK, D), B16), mixed=((TOK, D), B16), attn=((TOK, D), F32), act=((4, TOK, D), B16), dact=((4, TOK, D), B16))
SCOPE_I = dict(masked=((SEQ, D), B16), cot=((TOK, D), B16))
SCOPE_H = dict(qkv=((48, TOK, HEAD_DIM), B16), mixh=((HEADS, TOK, HEAD_DIM), B16), wq=((2, 4, 2, 144, 864), B16))
SCOPE_U = dict(wo=((4, 4, 2, 144, 288), B16), w1=((2, 4, 2, 144, D), B16))
SCOPE_R = dict(r_big=((4, 4, 144, D), B16), r_fc1=((4, 4, 144, D), B16), r_out=((4, 4, 144, 288), B16), gres=((TOK, D), F32), ga=((TOK, D), B16))
SCOPE_M = dict(gb=((TOK, D), B16), gh2=((TOK, D), F32))
SCOPE_W = dict(gbp=((4, 144, 768), B16), actp=((2, 2 * TOK, D), B16), w2=((2, 4, 2, 144, D), B16), w1=((1, 4, 2, 144, D), B16),
           dact=((2, TOK, D), B16), gup=((2, TOK, D), B16))
SCOPE_G = dict(h2p=((4, 144, 768), B16), gupv=((2, 2 * TOK, D), B16))
SCOPE_N = dict(tok=((TOK, D), B16), attn=((TOK, D), F32), cot=((TOK, D), B16))
SCOPE_X = dict(w2=((2, 4, 2, 144, D), B16), acto=((2, TOK, D), B16), branch=((TOK, D), F32), tok=((TOK, D), B16), attn=((TOK, D), F32), cot=((TOK, D), B16), res=((TOK, D), B16))
SCOPE_S = dict(spr=((SEQ, D), F32), gwa=((288, 864), F32))
SCOPE_A = dict(gmh=((HEADS, TOK, HEAD_DIM), B16))
SCOPE_B = dict(wo=((4, 4, 2, 144, 288), B16))
SCOPE_O = dict(gat=((8, 144, TOK), B16), gapv=((4, 144, 768), B16), mixp=((2 * TOK, D), B16))
SCOPE_Q = dict(qkv=((48, TOK, HEAD_DIM), B16), wq=((2, 4, 2, 144, 864), B16), gq=((2, TOK, 864), B16),
           gqv=((2, 2 * TOK, 864), B16), h1p=((4, 144, 768), B16), gh1=((TOK, D), F32), tok=((TOK, D), B16))
INS_V = dict(keep=0, cond_full=0, cond_masked=0, w_ada=0, pack=0, w_qkv=0, w_out=0, w_fc1=0, w_fc2=0)
INS_A = dict(full=0, masked=0, cot_full=0, cot_masked=0)
OUT_V = dict(gc_full=((1, D), F32), gc_masked=((1, D), F32), gb_ada=((1, 864), F32), gb_q=((1, 144), F32), gb_v=((1, 144), F32),
             gb_out=((1, 144), F32), gb_fc1=((1, 576), F32), gb_fc2=((1, 144), F32))
OUT_A = dict(
    result=((TOK, D), B16), gfull=((SEQ, D), F32), gmasked=((SEQ, D), F32), gw_ada=((288, 864), F32), gw_qkv=((2, 144, 432), B16),
    gw_out=((144, 288), B16), gw_fc1=((2, 144, 576), B16), gw_fc2=((144, D), B16),
    t0=((4, 4, 2, 144, 864), B16), t1=((4, 4, 2, 144, 288), B16), t2=((4, 4, 2, 144, D), B16), t3=((4, 4, 2, 144, D), B16),
    tok=((TOK, D), B16), qkv=((48, TOK, HEAD_DIM), B16), mixed=((2 * TOK, D), B16), attn=((TOK, D), F32),
    h1p=((4, 144, 768), B16), h2p=((4, 144, 768), B16), gbp=((4, 144, 768), B16), act=((4, 2 * TOK, D), B16), dact=((4, TOK, D), B16), gb=((TOK, D), B16),
    gupp=((4, 2 * TOK, D), B16), gqp=((4, 2 * TOK, 864), B16), gap=((4, 144, 768), B16),
)


def block_kernel(events, *refs):
    i, o, v = Bag(), Bag(), Bag()
    refs = list(refs)
    for bag, names in ((i, INS_V), (i, INS_A), (o, OUT_V), (o, OUT_A), (v, STAGE), (v, SIGNALS)):
        for n in names:
            setattr(bag, n, refs.pop(0))
    p = Place()
    con_refs = [refs.pop(0) for _ in range(len(Conditions.SHAPES) + len(Conditions.SEMS))]
    back_refs = [refs.pop(0) for _ in range(len(Back.SHAPES) + len(Back.SEMS))]
    sc_refs = [refs.pop(0) for _ in range(Scatter.count())]
    con = Conditions(p, (i.cond_full, i.cond_masked), i.w_ada, i.pack, con_refs)
    back = Back(p, v.gmods, v.gbias, i.w_ada, back_refs)
    sc = Scatter(p, None, sc_refs)
    g = Gather(p, (o.t0, o.t1, o.t2, o.t3), (v.bq, i.w_out, v.b1, i.w_fc2), refs)
    f_table = forward_steps(p, i, o, v, con)
    table = backward_steps(p, i, o, v, con, back)
    f_table.update(second=con.second, third=con.third, fourth=con.fourth, last=con.last, begin=con.begin)
    table.update({"f_" + n.removeprefix("f_"): f for n, f in f_table.items()})
    table.update(own=g.own, bown=g.bown, arr=g.arr, cross=g.cross, bcross=g.bcross, bz=g.bz_, barr=g.barr, fin=g.fin, have=g.have)
    table.update(s1=sc.s1, s2=sc.s2, s3=sc.s3, zt=sc.zt, zf=sc.zf, b1=sc.b1, bf=sc.bf, b3=sc.b3, b4=sc.b4, sent=sc.sent)

    def stages(n):
        return stage(p, (i.w_qkv, i.w_fc1)[n], (v.got_q, v.got_1)[n], v.st.at[n], v.rt.at[n])

    def join_q():
        stages(0).wait_recv()
        join(p, i.w_qkv, v.got_q, v.bq)

    def join_1():
        stages(1).wait_recv()
        join(p, i.w_fc1, v.got_1, v.b1)

    table.update(join_q=join_q, join_1=join_1)

    def run(queue):
        for name, args in queue:
            if args and isinstance(args[0], dict):
                spec = args[0]

                def scope(*inner, spec=spec):
                    for n, ref in zip(spec, inner, strict=True):
                        setattr(v, n, ref)
                    if spec is SCOPE_R:
                        sc.r = (v.r_big, v.r_out, v.r_fc1, v.r_big)
                    run(queue)

                pl.run_scoped(scope, *[pltpu.VMEM(s, d) for s, d in spec.values()])
            elif name not in table:
                return
            else:
                table[name](*args)

    p.barrier()
    for n in range(2):
        stages(n).start()
    run(iter(events))
    for n in range(2):
        stages(n).wait_send()
    con.drain()
    back.drain()
    g.drain()


def block_events():
    e = Script()
    e.own(OUT)
    e.join_q()
    e.bown(FC2)
    e.bown(QKV)
    e.own(QKV)
    e.join_1()
    e.open(SCOPE_P)
    e.bown(FC1)
    e.open(SCOPE_I)
    e.own(FC1)
    e.f_get_tokens()
    e.bcross(QKV)
    e.f_begin()
    e.f_second()
    e.arr(OUT, 2)
    e.f_tokens()
    e.arr(QKV, 1)
    e.bcross(FC1)
    e.f_third()
    e.arr(QKV, 3)
    e.f_fourth()
    e.bz(QKV)
    e.cross(QKV, 1)
    e.arr(QKV, 2)
    e.f_last()
    e.f_norm1()
    e.f_grads_in()
    e.barr(QKV, 1)
    e.barr(QKV, 2)
    e.cross(QKV, 3)
    e.fin(QKV, 1)
    e.close()
    e.cross(QKV, 2)
    e.cross(QKV, 0)
    e.arr(OUT, 1)
    e.arr(FC1, 2)
    e.fin(QKV, 2)
    e.arr(OUT, 3)
    e.bz(FC1)
    e.cross(FC1, 0)
    e.fin(QKV, 0)
    e.barr(QKV, 3)
    e.arr(FC1, 1)
    e.cross(OUT, 0)
    e.cross(OUT, 2)
    e.f_turn1()
    e.fin(QKV, 3)
    e.open(SCOPE_H)
    e.have(QKV)
    e.f_load_q(0)
    e.f_load_q(1)
    e.cross(OUT, 1)
    e.cross(OUT, 3)
    e.f_qkv(0)
    e.barr(FC1, 2)
    e.f_qkv(1)
    e.barr(FC1, 1)
    e.arr(FC1, 3)
    e.bcross(FC2)
    e.cross(FC1, 1)
    e.f_qkv(2)
    e.f_qkv(3)
    e.fin(OUT, 3)
    e.f_heads(0, 4)
    e.fin(OUT, 0)
    e.cross(FC1, 2)
    e.barr(FC1, 3)
    e.f_heads(4, 4)
    e.fin(FC1, 0)
    e.own(FC2)
    e.f_heads(8, 4)
    e.bz(FC2)
    e.fin(OUT, 2)
    e.fin(OUT, 1)
    e.cross(FC1, 3)
    e.fin(FC1, 1)
    e.f_heads(12, 4)
    e.have(OUT)
    e.f_mix()
    e.fin(FC1, 2)
    e.f_end_qkv()
    e.close()
    e.open(SCOPE_U)
    e.f_load_o()
    e.f_attend()
    e.cross(FC2, 0)
    e.arr(FC2, 1)
    e.f_turn2()
    e.fin(FC1, 3)
    e.arr(FC2, 2)
    e.barr(FC2, 1)
    e.fin(FC2, 0)
    e.arr(FC2, 3)
    e.have(FC1)
    e.f_load_1(0)
    e.f_load_1(1)
    e.f_fc1(0)
    e.f_fc1(1)
    e.barr(FC2, 2)
    e.cross(FC2, 2)
    e.f_fc1(2)
    e.cross(FC2, 3)
    e.f_fc1(3)
    e.close()
    e.fin(FC2, 2)
    e.f_end()
    e.close()
    e.barr(FC2, 3)
    e.open(SCOPE_R)
    e.cross(FC2, 1)
    e.open(SCOPE_M)
    e.open(SCOPE_W)
    e.load_gbp()
    e.load_act(0)
    e.load_act(1)
    e.fin(FC2, 3)
    e.grad_fc2(0)
    e.grad_fc2(1)
    e.grad_fc2(2)
    e.s1(FC2, 2)
    e.fin(FC2, 1)
    e.s1(FC2, 1)
    e.grad_fc2(3)
    e.s1(FC2, 3)
    e.have(FC2)
    e.b1(FC2, 3)
    e.load_mlp(0)
    e.s2(FC2, 1)
    e.s1(FC2, 0)
    e.load_mlp(1)
    e.mlp(0)
    e.b1(FC2, 2)
    e.mlp(1)
    e.b1(FC2, 1)
    e.s2(FC2, 3)
    e.s3(FC2, 1)
    e.s2(FC2, 2)
    e.mlp(2)
    e.mlp(3)
    e.s3(FC2, 3)
    e.zt(FC2, 3)
    e.end_mlp()
    e.close()
    e.open(SCOPE_N)
    e.load_n()
    e.norm2()
    e.s2(FC2, 0)
    e.close()
    e.close()
    e.open(SCOPE_G)
    e.s3(FC2, 2)
    e.zt(FC2, 2)
    e.load_g()
    e.grad_fc1(0)
    e.bf(FC2)
    e.b1(FC1, 3)
    e.s1(FC1, 3)
    e.grad_fc1(1)
    e.grad_fc1(2)
    e.grad_fc1(3)
    e.close()
    e.open(SCOPE_A)
    e.s1(FC1, 2)
    e.open(SCOPE_B)
    e.s2(FC1, 3)
    e.zt(FC2, 1)
    e.load_o()
    e.grad_mixed()
    e.close()
    e.b1(FC1, 1)
    e.s1(FC1, 1)
    e.s2(FC1, 2)
    e.open(SCOPE_Q)
    e.load_q()
    e.s3(FC2, 0)
    e.b3(FC2)
    e.heads(0, 4)
    e.heads(4, 4)
    e.heads(8, 4)
    e.s1(FC1, 0)
    e.s3(FC1, 3)
    e.heads(12, 4)
    e.b1(FC1, 2)
    e.s2(FC1, 1)
    e.grad_h1(0)
    e.grad_h1(1)
    e.grad_h1(2)
    e.zt(FC1, 3)
    e.b4(FC2)
    e.grad_h1(3)
    e.bf(FC1)
    e.zf(FC2)
    e.s3(FC1, 2)
    e.zt(FC1, 2)
    e.s2(FC1, 0)
    e.out_fc2()
    e.end_fc2()
    e.load_gq(0)
    e.sent(FC2)
    e.load_gq(1)
    e.b3(FC1)
    e.grad_qkv(0)
    e.grad_qkv(1)
    e.s1(QKV, 2)
    e.b1(QKV, 3)
    e.grad_qkv(2)
    e.s3(FC1, 1)
    e.s1(QKV, 1)
    e.grad_qkv(3)
    e.b1(QKV, 2)
    e.s1(QKV, 3)
    e.zt(FC1, 1)
    e.norm1()
    e.b4(FC1)
    e.put_full()
    e.close()
    e.s1(QKV, 0)
    e.close()
    e.open(SCOPE_O)
    e.b1(QKV, 1)
    e.load_m()
    e.turn_a()
    e.s2(QKV, 3)
    e.s2(QKV, 2)
    e.grad_out()
    e.s1(OUT, 1)
    e.s2(QKV, 0)
    e.s3(QKV, 3)
    e.close()
    e.open(SCOPE_X)
    e.s3(FC1, 0)
    e.load_x()
    e.branch(0)
    e.zf(FC1)
    e.s1(OUT, 0)
    e.s2(QKV, 1)
    e.branch(1)
    e.branch(2)
    e.sent(FC1)
    e.s1(OUT, 3)
    e.s3(QKV, 0)
    e.bf(QKV)
    e.zt(QKV, 3)
    e.branch(3)
    e.result()
    e.s3(QKV, 1)
    e.s3(QKV, 2)
    e.end_result()
    e.s1(OUT, 2)
    e.zt(QKV, 1)
    e.s2(OUT, 3)
    e.close()
    e.open(SCOPE_S)
    e.s2(OUT, 1)
    e.back_begin()
    e.zt(QKV, 2)
    e.s2(OUT, 2)
    e.back_second()
    e.s3(OUT, 3)
    e.s2(OUT, 0)
    e.zt(OUT, 3)
    e.back_third()
    e.s3(OUT, 1)
    e.s3(OUT, 2)
    e.b3(QKV)
    e.back_fourth()
    e.b4(QKV)
    e.s3(OUT, 0)
    e.zf(QKV)
    e.out_fc1()
    e.out_qkv()
    e.zt(OUT, 2)
    e.zt(OUT, 1)
    e.spread()
    e.back_last()
    e.end_gqkv()
    e.zf(OUT)
    e.out_out()
    e.end_full()
    e.end_fc1()
    e.end_spread()
    e.end_ada()
    e.sent(OUT)
    e.close()
    e.sent(QKV)
    e.end_out()
    e.close()
    return e.steps


def block(events, args):
    V, A = pl.BlockSpec(memory_space=pltpu.VMEM), pl.BlockSpec(memory_space=pl.ANY)
    outs = {**OUT_V, **OUT_A}
    got = pl.pallas_call(
        functools.partial(block_kernel, events),
        out_shape=[jax.ShapeDtypeStruct(s, d) for s, d in outs.values()],
        in_specs=[V] * len(INS_V) + [A] * len(INS_A),
        out_specs=[V] * len(OUT_V) + [A] * len(OUT_A),
        scratch_shapes=[pltpu.VMEM(s, d) for s, d in STAGE.values()] + [pltpu.SemaphoreType.DMA(s) for s in SIGNALS.values()]
        + Conditions.scratch() + Back.scratch() + Scatter.scratch() + Gather.scratch(),
        compiler_params=pltpu.CompilerParams(collective_id=0, has_side_effects=True, vmem_limit_bytes=62 * 2**20),
        name="block",
    )(*args)
    return dict(zip(outs, got, strict=True))


FINAL_A = dict(result=((TOK, D), B16), gfull=((SEQ, D), F32), gmasked=((SEQ, D), F32), gw_ada=((288, 864), F32))
FINAL_V = dict(gw_qkv=(2, 144, 432), gw_out=(144, 288), gw_fc1=(2, 144, 576), gw_fc2=(144, D))


def final_kernel(result, gfull, gmasked, gw_ada, *refs):
    blocks, refs = refs[:4], refs[4:]
    small, refs = refs[:8], refs[8:]
    outs, sem = refs[:-1], refs[-1]
    moves = ((cut(result, 0, SEQ), outs[0].at[0]), (cut(result, SEQ, KEEP), outs[1].at[0]), (gfull, outs[2].at[0]), (gmasked, outs[3].at[0]), (gw_ada, outs[4]))
    copies = [pltpu.make_async_copy(src, dst, sem.at[n]) for n, (src, dst) in enumerate(moves)]
    for c in copies:
        c.start()
    for src, dst in zip(blocks, outs[5:9], strict=True):
        dst[...] = src[...].astype(F32)
    for src, dst in zip(small, outs[9:], strict=True):
        dst[...] = src[...].reshape(dst.shape)
    for c in copies:
        c.wait()


def whole(full_input, masked_input, keep_index, cond_full, cond_masked, w_ada, b_ada, w_qkv, b_q, b_v, w_out, b_out, w_fc1, b_fc1, w_fc2, b_fc2, cot_full, cot_masked):
    pack = jnp.concatenate([b_ada, b_q, b_v, b_out, b_fc1, b_fc2])[None]
    g = block(block_events(), (keep_index, cond_full, cond_masked, w_ada, pack, w_qkv, w_out.T, w_fc1, w_fc2.T, full_input, masked_input, cot_full, cot_masked))
    V, A = pl.BlockSpec(memory_space=pltpu.VMEM), pl.BlockSpec(memory_space=pl.ANY)
    shapes = [((1, SEQ, D), B16), ((1, KEEP, D), B16), ((1, SEQ, D), F32), ((1, SEQ, D), F32), ((288, 864), F32)]
    shapes += [(s, F32) for s in FINAL_V.values()]
    shapes += [((1, D), F32)] * 2 + [(s, F32) for s in ((1, 864), (1, 144), (1, 144), (1, 144), (1, 576), (1, 144))]
    out = pl.pallas_call(
        final_kernel,
        out_shape=[jax.ShapeDtypeStruct(s, d) for s, d in shapes],
        in_specs=[V] * 16,
        out_specs=[A] * 5 + [V] * (len(shapes) - 5),
        scratch_shapes=[pltpu.SemaphoreType.DMA((5,))],
        name="results",
    )(*[g[n] for n in FINAL_A], *[g[n] for n in FINAL_V], *[g[n] for n in OUT_V])
    out_full, out_masked, gfull, gmasked, gw_ada, gw_qkv, gw_out, gw_fc1, gw_fc2, gc_full, gc_masked, gb_ada, gb_q, gb_v, gb_out, gb_fc1, gb_fc2 = out
    return (
        out_full, out_masked, gfull, gmasked, gc_full, gc_masked, gw_ada, gb_ada[0], gw_qkv.reshape(288, 432), gb_q[0], gb_v[0], gw_out.T, gb_out[0],
        gw_fc1.reshape(288, 576), gb_fc1[0], gw_fc2.T, gb_fc2[0],
    )


def plain_layer_stats(values):
    centered = values - jnp.mean(values, axis=-1, keepdims=True)
    inverse = lax.rsqrt(jnp.mean(centered * centered, axis=-1, keepdims=True) + 1e-06)
    return (centered * inverse, inverse)


def plain_layer_back(upstream, normed, inverse):
    return inverse * (
        upstream
        - jnp.mean(upstream, axis=-1, keepdims=True)
        - normed * jnp.mean(upstream * normed, axis=-1, keepdims=True)
    )


def plain_gelu_tanh(values):
    return jax.nn.gelu(values, approximate=True)


def plain_expand_mods(piece, full_length, kept_length):
    head_part = jnp.broadcast_to(piece[:, 0:1], (piece.shape[0], full_length, piece.shape[2]))
    tail_part = jnp.broadcast_to(piece[:, 1:2], (piece.shape[0], kept_length, piece.shape[2]))
    return jnp.concatenate([head_part, tail_part], axis=1)


def plain_image_sums(values, full_length):
    return jnp.stack(
        [jnp.sum(values[:, :full_length], axis=1), jnp.sum(values[:, full_length:], axis=1)], axis=1
    )


def plain_forward_pass(tokens, mods, weights, biases, full_length):
    images, length, features = tokens.shape
    head_count = features // HEAD_DIM
    pieces = [
        plain_expand_mods(
            mods[:, :, column * features : (column + 1) * features],
            full_length,
            length - full_length,
        )
        for column in range(6)
    ]
    norm_one, inverse_one = plain_layer_stats(tokens)
    hidden_one = (norm_one * (1.0 + pieces[1]) + pieces[0]).astype(jnp.bfloat16)
    bias_all = jnp.concatenate([biases[1], jnp.zeros((features,), jnp.bfloat16), biases[2]]).astype(
        jnp.float32
    )
    projected = (
        jnp.einsum("itd,de->ite", hidden_one, weights[1], preferred_element_type=jnp.float32)
        + bias_all
    )
    projected = projected.astype(jnp.bfloat16).reshape(images, length, 3, head_count, HEAD_DIM)
    query_rows = projected[:, :, 0]
    key_rows = projected[:, :, 1]
    value_rows = projected[:, :, 2]
    scale_factor = 1.0 / math.sqrt(HEAD_DIM)
    scores = (
        jnp.einsum("iqhc,ikhc->ihqk", query_rows, key_rows, preferred_element_type=jnp.float32)
        * scale_factor
    )
    marker = jnp.arange(length) >= full_length
    same_image = marker[:, None] == marker[None, :]
    scores = jnp.where(same_image, scores, -1e30)
    row_max = jnp.max(scores, axis=-1, keepdims=True)
    exponent = jnp.exp(scores - row_max)
    attention = exponent / jnp.sum(exponent, axis=-1, keepdims=True)
    attention_low = attention.astype(jnp.bfloat16)
    mixed = jnp.einsum(
        "ihqk,ikhc->iqhc", attention_low, value_rows, preferred_element_type=jnp.float32
    )
    mixed = mixed.astype(jnp.bfloat16).reshape(images, length, features)
    attn_out = jnp.einsum(
        "itd,de->ite", mixed, weights[2], preferred_element_type=jnp.float32
    ) + biases[3].astype(jnp.float32)
    residual = tokens + pieces[2] * attn_out
    norm_two, inverse_two = plain_layer_stats(residual)
    hidden_two = (norm_two * (1.0 + pieces[4]) + pieces[3]).astype(jnp.bfloat16)
    upper = jnp.einsum(
        "itd,df->itf", hidden_two, weights[3], preferred_element_type=jnp.float32
    ) + biases[4].astype(jnp.float32)
    activated = plain_gelu_tanh(upper).astype(jnp.bfloat16)
    branch = jnp.einsum(
        "itf,fd->itd", activated, weights[4], preferred_element_type=jnp.float32
    ) + biases[5].astype(jnp.float32)
    result = residual + pieces[5] * branch
    return (
        result,
        pieces,
        norm_one,
        inverse_one,
        hidden_one,
        query_rows,
        key_rows,
        value_rows,
        attention,
        attention_low,
        mixed,
        attn_out,
        norm_two,
        inverse_two,
        hidden_two,
        upper,
        activated,
        branch,
    )


def general(
    full_input,
    masked_input,
    keep_index,
    cond_full,
    cond_masked,
    w_ada,
    b_ada,
    w_qkv,
    b_q,
    b_v,
    w_out,
    b_out,
    w_fc1,
    b_fc1,
    w_fc2,
    b_fc2,
    cot_full,
    cot_masked,
):
    def columns(shard):
        return lax.all_gather(lax.all_gather(shard, ROWS, axis=0, tiled=True), COLS, axis=1, tiled=True)

    weights = (None, columns(w_qkv), columns(w_out), columns(w_fc1), columns(w_fc2))
    widths = [b.shape[0] for b in (b_q, b_v, b_out, b_fc1, b_fc2)]
    packed = lax.all_gather(jnp.concatenate([b_q, b_v, b_out, b_fc1, b_fc2]), COLS, axis=0, tiled=False)
    biases, at = [None], 0
    for width in widths:
        biases.append(packed[:, at : at + width].reshape(-1))
        at += width
    full_length = full_input.shape[1]
    images = full_input.shape[0]
    features = full_input.shape[2]
    picked = jnp.take_along_axis(masked_input, keep_index[:, :, None], axis=1)
    tokens = jnp.concatenate([full_input, picked], axis=1).astype(jnp.float32)
    conds = jnp.stack([cond_full, cond_masked], axis=1).astype(jnp.float32)
    silu_low = jax.nn.silu(conds).astype(jnp.bfloat16)
    n_dp, n_fsdp = lax.axis_size(ROWS), lax.axis_size(COLS)
    rows_ada, cols_ada = w_ada.shape
    every_silu = lax.all_gather(silu_low, (ROWS, COLS), axis=0, tiled=True)
    my_silu = lax.dynamic_slice_in_dim(every_silu, lax.axis_index(ROWS) * rows_ada, rows_ada, axis=2)
    part = jnp.einsum("ijd,de->ije", my_silu, w_ada, preferred_element_type=jnp.float32)
    part = lax.psum_scatter(part, ROWS, scatter_dimension=0, tiled=True)
    part = part + b_ada.astype(jnp.float32)
    mods = lax.all_to_all(part, COLS, split_axis=0, concat_axis=2, tiled=True)
    (
        result,
        pieces,
        norm_one,
        inverse_one,
        hidden_one,
        query_rows,
        key_rows,
        value_rows,
        attention,
        attention_low,
        mixed,
        attn_out,
        norm_two,
        inverse_two,
        hidden_two,
        upper,
        activated,
        branch,
    ) = plain_forward_pass(tokens, mods, weights, biases, full_length)
    length = tokens.shape[1]
    head_count = features // HEAD_DIM
    scale_factor = 1.0 / math.sqrt(HEAD_DIM)
    grad_result = jnp.concatenate([cot_full, cot_masked], axis=1).astype(jnp.float32)
    grad_gate_two = plain_image_sums(grad_result * branch, full_length)
    grad_branch = (pieces[5] * grad_result).astype(jnp.bfloat16)
    grad_b_fc2 = jnp.sum(grad_branch.astype(jnp.float32), axis=(0, 1))
    grad_w_fc2 = jnp.einsum(
        "itf,itd->fd", activated, grad_branch, preferred_element_type=jnp.float32
    )
    grad_act = jnp.einsum(
        "itd,fd->itf", grad_branch, weights[4], preferred_element_type=jnp.float32
    )
    grad_upper = jax.vjp(plain_gelu_tanh, upper)[1](grad_act)[0].astype(jnp.bfloat16)
    grad_b_fc1 = jnp.sum(grad_upper.astype(jnp.float32), axis=(0, 1))
    grad_w_fc1 = jnp.einsum(
        "itd,itf->df", hidden_two, grad_upper, preferred_element_type=jnp.float32
    )
    grad_hidden_two = jnp.einsum(
        "itf,df->itd", grad_upper, weights[3], preferred_element_type=jnp.float32
    )
    grad_scale_two = plain_image_sums(grad_hidden_two * norm_two, full_length)
    grad_shift_two = plain_image_sums(grad_hidden_two, full_length)
    grad_residual = grad_result + plain_layer_back(
        grad_hidden_two * (1.0 + pieces[4]), norm_two, inverse_two
    )
    grad_gate_one = plain_image_sums(grad_residual * attn_out, full_length)
    grad_attn = (pieces[2] * grad_residual).astype(jnp.bfloat16)
    grad_b_out = jnp.sum(grad_attn.astype(jnp.float32), axis=(0, 1))
    grad_w_out = jnp.einsum("itd,ite->de", mixed, grad_attn, preferred_element_type=jnp.float32)
    grad_mixed = jnp.einsum(
        "ite,de->itd", grad_attn, weights[2], preferred_element_type=jnp.float32
    )
    grad_mixed = grad_mixed.astype(jnp.bfloat16).reshape(images, length, head_count, HEAD_DIM)
    grad_attention = jnp.einsum(
        "iqhc,ikhc->ihqk", grad_mixed, value_rows, preferred_element_type=jnp.float32
    )
    grad_values = jnp.einsum(
        "ihqk,iqhc->ikhc", attention_low, grad_mixed, preferred_element_type=jnp.float32
    )
    grad_scores = attention * (
        grad_attention - jnp.sum(attention * grad_attention, axis=-1, keepdims=True)
    )
    grad_scores = grad_scores.astype(jnp.bfloat16)
    grad_queries = (
        jnp.einsum("ihqk,ikhc->iqhc", grad_scores, key_rows, preferred_element_type=jnp.float32)
        * scale_factor
    )
    grad_keys = (
        jnp.einsum("ihqk,iqhc->ikhc", grad_scores, query_rows, preferred_element_type=jnp.float32)
        * scale_factor
    )
    grad_projected = jnp.stack([grad_queries, grad_keys, grad_values], axis=2)
    grad_projected = grad_projected.reshape(images, length, 3 * features).astype(jnp.bfloat16)
    grad_b_q = jnp.sum(grad_projected[:, :, :features].astype(jnp.float32), axis=(0, 1))
    grad_b_v = jnp.sum(grad_projected[:, :, 2 * features :].astype(jnp.float32), axis=(0, 1))
    grad_w_qkv = jnp.einsum(
        "itd,ite->de", hidden_one, grad_projected, preferred_element_type=jnp.float32
    )
    grad_hidden_one = jnp.einsum(
        "ite,de->itd", grad_projected, weights[1], preferred_element_type=jnp.float32
    )
    grad_scale_one = plain_image_sums(grad_hidden_one * norm_one, full_length)
    grad_shift_one = plain_image_sums(grad_hidden_one, full_length)
    grad_tokens = grad_residual + plain_layer_back(
        grad_hidden_one * (1.0 + pieces[1]), norm_one, inverse_one
    )
    grad_mods = jnp.concatenate(
        [
            grad_shift_one,
            grad_scale_one,
            grad_gate_one,
            grad_shift_two,
            grad_scale_two,
            grad_gate_two,
        ],
        axis=-1,
    ).astype(jnp.bfloat16)
    cut = grad_mods.reshape(images, 2, n_fsdp, cols_ada)
    mine = lax.all_to_all(cut, COLS, split_axis=2, concat_axis=0, tiled=False)
    mine = lax.all_gather(mine.reshape(n_fsdp * images, 2, cols_ada), ROWS, axis=0, tiled=True)
    grad_b_ada = jnp.sum(mine.astype(jnp.float32), axis=(0, 1))
    grad_w_ada = jnp.einsum("ijd,ije->de", my_silu, mine, preferred_element_type=jnp.float32)
    back = jnp.einsum("ije,de->ijd", mine, w_ada, preferred_element_type=jnp.float32)
    back = lax.psum_scatter(back.reshape(n_dp, n_fsdp * images, 2, rows_ada), COLS, scatter_dimension=1, tiled=True)
    grad_silu = lax.all_to_all(back, ROWS, split_axis=0, concat_axis=3, tiled=True).reshape(images, 2, features)
    grad_cond = jax.vjp(jax.nn.silu, conds)[1](grad_silu)[0]
    image_rows = jnp.arange(images)[:, None]
    grad_masked = (
        jnp.zeros((images, full_length, features), jnp.float32)
        .at[image_rows, keep_index]
        .set(grad_tokens[:, full_length:])
    )
    def owned(grad):
        inner = lax.psum_scatter(grad.astype(jnp.bfloat16), ROWS, scatter_dimension=0, tiled=True)
        return lax.psum_scatter(inner, COLS, scatter_dimension=1, tiled=True).astype(jnp.float32)

    matrices = (grad_w_ada, owned(grad_w_qkv), owned(grad_w_out), owned(grad_w_fc1), owned(grad_w_fc2))
    sums = (grad_b_q, grad_b_v, grad_b_out, grad_b_fc1, grad_b_fc2)
    line = jnp.concatenate([g.reshape(n_fsdp, -1) for g in sums], axis=1)
    line = lax.psum(lax.psum_scatter(line, COLS, scatter_dimension=0, tiled=True), ROWS)[0]
    vectors, at = [grad_b_ada], 0
    for width in widths:
        vectors.append(line[at : at + width])
        at += width
    return (
        result[:, :full_length].astype(jnp.bfloat16),
        result[:, full_length:].astype(jnp.bfloat16),
        grad_tokens[:, :full_length],
        grad_masked,
        grad_cond[:, 0],
        grad_cond[:, 1],
        matrices[0],
        vectors[0],
        matrices[1],
        vectors[1],
        vectors[2],
        matrices[2],
        vectors[3],
        matrices[3],
        vectors[4],
        matrices[4],
        vectors[5],
    )


def solution(mesh):
    special = dict(mesh.shape) == {ROWS: 4, COLS: 8}
    return jax.shard_map(
        whole if special else general,
        mesh=mesh,
        in_specs=(
            P((ROWS, COLS), None, None),
            P((ROWS, COLS), None, None),
            P((ROWS, COLS), None),
            P((ROWS, COLS), None),
            P((ROWS, COLS), None),
            P(ROWS, COLS),
            P(COLS),
            P(ROWS, COLS),
            P(COLS),
            P(COLS),
            P(ROWS, COLS),
            P(COLS),
            P(ROWS, COLS),
            P(COLS),
            P(ROWS, COLS),
            P(COLS),
            P((ROWS, COLS), None, None),
            P((ROWS, COLS), None, None),
        ),
        out_specs=(
            P((ROWS, COLS), None, None),
            P((ROWS, COLS), None, None),
            P((ROWS, COLS), None, None),
            P((ROWS, COLS), None, None),
            P((ROWS, COLS), None),
            P((ROWS, COLS), None),
            P(ROWS, COLS),
            P(COLS),
            P(ROWS, COLS),
            P(COLS),
            P(COLS),
            P(ROWS, COLS),
            P(COLS),
            P(ROWS, COLS),
            P(COLS),
            P(ROWS, COLS),
            P(COLS),
        ),
        check_vma=False,
    )
```

```python
import functools
import math
import jax
import jax.numpy as jnp
from jax import lax
from jax.experimental import pallas as pl
from jax.experimental.pallas import tpu as pltpu
from jax.sharding import PartitionSpec as P


MESH = pl.DeviceIdType.MESH
ROWS, COLS = "dp", "fsdp"
F32, B16 = jnp.float32, jnp.bfloat16
D, HEADS, HEAD_DIM, SEQ, KEEP, TOK = 1152, 16, 72, 256, 128, 384
SCALE = 1.0 / math.sqrt(HEAD_DIM)
GELU_A, GELU_B = math.sqrt(2.0 / math.pi), 0.044715
MATS = ((1152, True, 32), (1152, True, 32), (1152, False, 32))
QO, FC1, FC2 = range(3)


def nn(a, b):
    return lax.dot_general(a, b, (((1,), (0,)), ((), ())), preferred_element_type=F32)


def nt(a, b):
    return lax.dot_general(a, b, (((1,), (1,)), ((), ())), preferred_element_type=F32)


def tn(a, b):
    return lax.dot_general(a, b, (((0,), (0,)), ((), ())), preferred_element_type=F32)


class Script:
    def __init__(self):
        self.steps = []

    def __getattr__(self, name):
        return lambda *args: self.steps.append((name, args))


class Place:
    def __init__(self):
        self.dp = dp = lax.axis_index(ROWS)
        self.f = f = lax.axis_index(COLS)
        self.z, self.c = f // 2, f % 2
        self.xn = dp + 1 - 2 * (dp % 2)
        self.yn = (dp + 2) % 4
        self.dg = 3 - dp
        self.sf = f + 1 - 2 * self.c
        z = self.z
        self.middle = (z == 1) | (z == 2)
        low = z < 2
        self.order = (z, z + 1 - 2 * (z % 2), jnp.where(low, 2, 1), jnp.where(low, 3, 0))
        self.x_dev, self.y_dev, self.d_dev, self.s_dev = (self.xn, f), (self.yn, f), (self.dg, f), (dp, self.sf)
        self.rows = [(self.dp + k) % 4 for k in (1, 2, 3)]
        self.cols = [(self.f + k) % 8 for k in range(1, 8)]

    def barrier(self):
        sem = pltpu.get_barrier_semaphore()
        for dev in [(r, self.f) for r in self.rows] + [(self.dp, c) for c in self.cols]:
            pl.semaphore_signal(sem, inc=1, device_id=dev, device_id_type=MESH)
        pl.semaphore_wait(sem, 10)


def remote(src, dst, send, recv, dev):
    return pltpu.make_async_remote_copy(src_ref=src, dst_ref=dst, send_sem=send, recv_sem=recv, device_id=dev, device_id_type=MESH)


def cut(ref, lo, n):
    return ref.at[pl.ds(lo, n)]


class Gather:
    SEMS = dict(rz=(4, 4), rx=(4, 4), ry=(4, 4), rd=(4, 4, 2), rs=(4, 4), so=(4, 2), sf=(4, 4), sx=(4, 4), sy=(4, 4), sd=(4, 4, 2),
                ss=(4, 4), loc=(4,), bx=(4,), by=(4,), bd=(4, 2), bz=(4, 4), cx=(4,), cy=(4,), cd=(4, 2), co=(4, 2), cf=(4, 4))

    def __init__(self, p, bufs, blks, sems):
        self.p, self.bufs, self.blks = p, bufs, blks
        for name, sem in zip(self.SEMS, sems, strict=True):
            setattr(self, name, sem)

    @classmethod
    def scratch(cls):
        return [pltpu.SemaphoreType.DMA(s) for s in cls.SEMS.values()]

    def a(self, m):
        return 144 - MATS[m][2]

    def split(self, m, j):
        a = self.a(m)
        h = (a // 32) * 16
        return (a - h, h) if j % 2 == 0 else (h, a - h)

    def slot(self, m, dp, zs):
        t = self.bufs[m]
        return t.at[zs, dp, self.p.c] if MATS[m][1] else t.at[dp, zs, self.p.c]

    def top(self, m, dp, zs):
        return cut(self.slot(m, dp, zs), 0, self.a(m))

    def low(self, m, dp, zs):
        return cut(self.slot(m, dp, zs), self.a(m), MATS[m][2])

    def low4(self, m, zs):
        t, rows = self.bufs[m], pl.ds(self.a(m), MATS[m][2])
        return t.at[zs, :, self.p.c, rows] if MATS[m][1] else t.at[:, zs, self.p.c, rows]

    def plane(self, m, zs, c):
        t = self.bufs[m]
        return t.at[zs, :, c] if MATS[m][1] else t.at[:, zs, c]

    def z_copies(self, m):
        p = self.p
        blk = cut(self.blks[m], 0, self.a(m))
        dst = self.top(m, p.dp, p.z)
        up = remote(blk, dst, self.so.at[m, 0], self.rz.at[m, p.z], (p.dp, p.f + 2))
        down = remote(blk, dst, self.so.at[m, 1], self.rz.at[m, p.z], (p.dp, p.f - 2))
        return up, down

    def bz_copies(self, m):
        p = self.p
        src = self.low4(m, p.z)
        up = remote(src, src, self.co.at[m, 0], self.bz.at[m, p.z], (p.dp, p.f + 2))
        down = remote(src, src, self.co.at[m, 1], self.bz.at[m, p.z], (p.dp, p.f - 2))
        return up, down

    def pass_on(self, m, zs):
        p = self.p
        src = self.top(m, p.dp, zs)
        return remote(src, src, self.sf.at[m, zs], self.rz.at[m, zs], (p.dp, p.f + jnp.where(zs < p.z, 2, -2)))

    def pass_low(self, m, zs):
        p = self.p
        src = self.low4(m, zs)
        return remote(src, src, self.cf.at[m, zs], self.bz.at[m, zs], (p.dp, p.f + jnp.where(zs < p.z, 2, -2)))

    def x_copy(self, m, src, zs):
        return remote(src, self.top(m, self.p.dp, zs), self.sx.at[m, zs], self.rx.at[m, zs], self.p.x_dev)

    def y_copy(self, m, src, zs):
        return remote(src, self.top(m, self.p.dp, zs), self.sy.at[m, zs], self.ry.at[m, zs], self.p.y_dev)

    def d_copy(self, m, j, zs, half):
        p = self.p
        a, b = self.split(m, j)
        lo, n = ((0, a), (a, b))[half]
        src = cut(self.slot(m, p.xn if half == 0 else p.yn, zs), lo, n)
        return remote(src, src, self.sd.at[m, zs, half], self.rd.at[m, zs, half], p.y_dev if half == 0 else p.x_dev)

    def bd_copy(self, m, half):
        p = self.p
        h = 16 * ((MATS[m][2] // 16 + 1) // 2)
        lo, n = ((0, h), (h, MATS[m][2] - h))[half]
        src = cut(self.slot(m, p.xn if half == 0 else p.yn, p.z), self.a(m) + lo, n)
        return remote(src, src, self.cd.at[m, half], self.bd.at[m, half], p.y_dev if half == 0 else p.x_dev)

    def s_copy(self, m, zs):
        src = self.plane(m, zs, self.p.c)
        return remote(src, src, self.ss.at[m, zs], self.rs.at[m, zs], self.p.s_dev)

    def ends(self, copies, act):
        p = self.p

        @pl.when(p.z < 3)
        def _():
            act(copies[0])

        @pl.when(p.z > 0)
        def _():
            act(copies[1])

    def got(self, ref, recv):
        remote(ref, ref, self.so.at[0, 0], recv, self.p.x_dev).wait_recv()

    def own(self, m):
        p = self.p
        self.ends(self.z_copies(m), lambda c: c.start())
        blk = cut(self.blks[m], 0, self.a(m))
        self.x_copy(m, blk, p.z).start()
        self.y_copy(m, blk, p.z).start()
        if not MATS[m][2]:
            pltpu.make_async_copy(self.blks[m], self.slot(m, p.dp, p.z), self.loc.at[m]).start()

    def bown(self, m):
        p = self.p
        pltpu.make_async_copy(self.blks[m], self.slot(m, p.dp, p.z), self.loc.at[m]).start()
        blk = cut(self.blks[m], self.a(m), MATS[m][2])
        dst = self.low(m, p.dp, p.z)
        remote(blk, dst, self.cx.at[m], self.bx.at[m], p.x_dev).start()
        remote(blk, dst, self.cy.at[m], self.by.at[m], p.y_dev).start()

    def arr(self, m, j):
        p = self.p
        zs = p.order[j]
        src = self.top(m, p.dp, zs)
        self.got(src, self.rz.at[m, zs])

        @pl.when(p.middle)
        def _():
            self.pass_on(m, zs).start()

        self.x_copy(m, src, zs).start()
        self.y_copy(m, src, zs).start()

    def cross(self, m, j):
        p = self.p
        zs = p.order[j]
        self.got(self.top(m, p.xn, zs), self.rx.at[m, zs])
        self.d_copy(m, j, zs, 0).start()
        self.got(self.top(m, p.yn, zs), self.ry.at[m, zs])
        self.d_copy(m, j, zs, 1).start()

    def bcross(self, m):
        p = self.p
        self.got(self.low(m, p.xn, p.z), self.bx.at[m])
        self.bd_copy(m, 0).start()
        self.got(self.low(m, p.yn, p.z), self.by.at[m])
        self.bd_copy(m, 1).start()

    def bz_(self, m):
        p = self.p
        h = 16 * ((MATS[m][2] // 16 + 1) // 2)
        for half, (lo, n) in enumerate(((0, h), (h, MATS[m][2] - h))):
            self.got(cut(self.slot(m, p.dg, p.z), self.a(m) + lo, n), self.bd.at[m, half])
        pltpu.make_async_copy(self.blks[m], self.slot(m, p.dp, p.z), self.loc.at[m]).wait()
        self.ends(self.bz_copies(m), lambda c: c.start())

    def barr(self, m, j):
        zs = self.p.order[j]
        self.got(self.low4(m, zs), self.bz.at[m, zs])

        @pl.when(self.p.middle)
        def _():
            self.pass_low(m, zs).start()

    def fin(self, m, j):
        p = self.p
        zs = p.order[j]
        a, b = self.split(m, j)
        for half, (lo, n) in enumerate(((0, a), (a, b))):
            self.got(cut(self.slot(m, p.dg, zs), lo, n), self.rd.at[m, zs, half])
        if j == 0 and not MATS[m][2]:
            pltpu.make_async_copy(self.blks[m], self.slot(m, p.dp, p.z), self.loc.at[m]).wait()
        self.s_copy(m, zs).start()

    def have(self, m):
        for j in range(4):
            zs = self.p.order[j]
            self.got(self.plane(m, zs, 1 - self.p.c), self.rs.at[m, zs])

    def drain(self):
        p = self.p
        for m in range(3):
            blk = cut(self.blks[m], 0, self.a(m))
            self.ends(self.z_copies(m), lambda c: c.wait_send())
            if MATS[m][2]:
                low = cut(self.blks[m], self.a(m), MATS[m][2])
                dst = self.low(m, p.dp, p.z)
                remote(low, dst, self.cx.at[m], self.bx.at[m], p.x_dev).wait_send()
                remote(low, dst, self.cy.at[m], self.by.at[m], p.y_dev).wait_send()
                self.bd_copy(m, 0).wait_send()
                self.bd_copy(m, 1).wait_send()
                self.ends(self.bz_copies(m), lambda c: c.wait_send())
            for j in range(4):
                zs = p.order[j]
                src = self.top(m, p.dp, zs)
                if j:

                    @pl.when(p.middle)
                    def _(m=m, zs=zs):
                        self.pass_on(m, zs).wait_send()
                        if MATS[m][2]:
                            self.pass_low(m, zs).wait_send()

                self.x_copy(m, src, zs).wait_send()
                self.y_copy(m, src, zs).wait_send()
                self.d_copy(m, j, zs, 0).wait_send()
                self.d_copy(m, j, zs, 1).wait_send()
                self.s_copy(m, zs).wait_send()


def stage(p, shard, got, send, recv):
    rows = shard.shape[0] // 2
    return remote(cut(shard, (1 - p.c) * rows, rows), got, send, recv, p.s_dev)


def join(p, shard, got, blk, at=0):
    rows, width = got.shape
    own = shard[pl.ds(pl.multiple_of(p.c * rows, 16), rows), :]
    other = got[...]
    first = p.c == 0
    blk[:, at : at + width] = jnp.where(first, own, other)
    blk[:, at + width : at + 2 * width] = jnp.where(first, other, own)


class Conditions:
    SEMS = dict(r1=(4,), s1=(4,), r2=(8,), s2=(8,), rb=(8,), sb=(8,), r3=(4,), s3=(4,), r4=(8,), s4=(8,))
    SHAPES = dict(sil4=(4, 2, 288), in1=(4, 2, 288), row8=(8, 288), in2=(8, 8, 288), pack=(1, D), inb=(8, 1, D), p3=(4, 16, 864),
                  in3=(4, 16, 864), m8=(8, 2, 864), in4=(8, 2, 864), mods=(6, 2, 1, D), bias=(8, 1, D), wide=(4, 1, D), qkvb=(4, 1, 864))

    @classmethod
    def scratch(cls):
        return [pltpu.VMEM(s, F32) for s in cls.SHAPES.values()] + [pltpu.SemaphoreType.DMA(s) for s in cls.SEMS.values()]

    def __init__(self, p, conds, w_ada, b_ada, biases, scratch):
        self.p, self.conds, self.w_ada, self.b_ada, self.biases = p, conds, w_ada, b_ada, biases
        for name, ref in zip(list(self.SHAPES) + list(self.SEMS), scratch, strict=True):
            setattr(self, name, ref)

    def over_dp(self, src_of, land, sem_s, sem_r):
        p = self.p
        return [remote(src_of(r), land.at[p.dp], sem_s.at[r], sem_r.at[p.dp], (r, p.f)) for r in p.rows]

    def over_f(self, src_of, land, sem_s, sem_r):
        p = self.p
        return [remote(src_of(c), land.at[p.f], sem_s.at[c], sem_r.at[p.f], (p.dp, c)) for c in p.cols]

    def copies(self, step):
        return {
            1: lambda: self.over_dp(lambda r: self.sil4.at[r], self.in1, self.s1, self.r1),
            2: lambda: self.over_f(lambda c: self.row8, self.in2, self.s2, self.r2),
            "b": lambda: self.over_f(lambda c: self.pack, self.inb, self.sb, self.rb),
            3: lambda: self.over_dp(lambda r: self.p3.at[r], self.in3, self.s3, self.r3),
            4: lambda: self.over_f(lambda c: self.m8.at[c], self.in4, self.s4, self.r4),
        }[step]()

    def send(self, step):
        for c in self.copies(step):
            c.start()

    def arrived(self, land, sem, peers):
        for q in peers:
            remote(land.at[q], land.at[q], self.s1.at[0], sem.at[q], self.p.x_dev).wait_recv()

    def begin(self):
        p = self.p
        at = 0
        for b in self.biases:
            n = b.shape[0]
            self.pack[:, at : at + n] = b[...].reshape(1, n).astype(F32)
            at += n
        self.send("b")
        self.inb[p.f] = self.pack[...]
        for s, cond in enumerate(self.conds):
            x = cond[...].astype(F32)
            y = (x / (1.0 + jnp.exp(-x))).astype(B16).astype(F32)
            for d in range(4):
                self.sil4[d, s : s + 1, :] = y[:, 288 * d : 288 * d + 288]
        self.send(1)
        self.in1[p.dp] = self.sil4[p.dp]

    def second(self):
        p = self.p
        self.arrived(self.in1, self.r1, p.rows)
        for d in range(4):
            self.row8[2 * d : 2 * d + 2, :] = self.in1[d]
        self.send(2)
        self.in2[p.f] = self.row8[...]

    def third(self):
        p = self.p
        self.arrived(self.in2, self.r2, p.cols)
        rows = self.in2[...].reshape(64, 288).astype(B16)
        part = nn(rows, self.w_ada[...])
        for d in range(4):
            for f in range(8):
                self.p3[d, 2 * f : 2 * f + 2, :] = part[8 * f + 2 * d : 8 * f + 2 * d + 2]
        self.send(3)
        self.in3[p.dp] = self.p3[p.dp]

    def fourth(self):
        p = self.p
        self.arrived(self.in3, self.r3, p.rows)
        total = self.in3[0] + self.in3[1] + self.in3[2] + self.in3[3] + self.b_ada[...].reshape(1, 864).astype(F32)
        for f in range(8):
            self.m8[f] = total[2 * f : 2 * f + 2]
        self.send(4)
        self.in4[p.f] = self.m8[p.f]

    def last(self):
        p = self.p
        self.arrived(self.in4, self.r4, p.cols)
        self.arrived(self.inb, self.rb, p.cols)
        for f in range(8):
            rows = self.in4[f]
            at = 864 * f
            while at < 864 * (f + 1):
                b = at // D
                end = min(864 * (f + 1), D * (b + 1))
                for s in range(2):
                    self.mods[b, s, :, at - D * b : end - D * b] = rows[s : s + 1, at - 864 * f : end - 864 * f]
                at = end
        for f in range(8):
            row = self.inb[f]
            for i, lo in enumerate((0, 144, 288, 1008)):
                self.bias[i, :, 144 * f : 144 * f + 144] = row[:, lo : lo + 144]
            half = 576 * (f % 2)
            self.wide[f // 2, :, half : half + 576] = row[:, 432:1008]
        line = jnp.concatenate([self.bias[0], jnp.zeros((1, D), F32), self.bias[1]], axis=1)
        for k in range(4):
            self.qkvb[k] = line[:, 864 * k : 864 * k + 864]

    def drain(self):
        for step in (1, 2, "b", 3, 4):
            for c in self.copies(step):
                c.wait_send()


def layer_stats(x):
    mean = jnp.mean(x, axis=-1, keepdims=True)
    centered = x - mean
    inv = lax.rsqrt(jnp.mean(centered * centered, axis=-1, keepdims=True) + 1e-6)
    return centered * inv, inv


def by_rows(body):
    def step(i, carry):
        body(pl.ds(pl.multiple_of(i * 128, 128), 128), i // 2)
        return carry

    lax.fori_loop(0, 3, step, 0)


def transpose_into(src, dst):
    for i in range(3):
        for k in range(9):
            t = src[128 * i : 128 * i + 128, 128 * k : 128 * k + 128].astype(F32).T.astype(B16)
            at = 128 * k
            while at < 128 * (k + 1):
                b = at // 144
                end = min(128 * (k + 1), 144 * (b + 1))
                dst[b, at - 144 * b : end - 144 * b, 128 * i : 128 * i + 128] = t[at - 128 * k : end - 128 * k]
                at = end


def pair_rows(p, mine, land, send, recv, loc):
    to_sib = [remote(mine.at[2 * k + (1 - p.c)], land.at[k, :, pl.ds(384, 384)], send.at[k], recv.at[k], p.s_dev) for k in range(4)]
    to_own = [pltpu.make_async_copy(mine.at[2 * k + p.c], land.at[k, :, pl.ds(0, 384)], loc.at[k]) for k in range(4)]
    return to_sib + to_own


class Bag:
    pass


def forward_steps(p, i, o, v, con):
    saves = []

    def save(pair):
        n = len(saves)
        saves.append(lambda: pltpu.make_async_copy(*pair(), v.ow.at[n]))
        saves[n]().start()

    waits = []

    def pairs(k, mine, land):
        waits.append(lambda: pair_rows(p, mine(), land, v.pt.at[k], v.pr.at[k], v.pl_.at[k]))
        for c in waits[-1]():
            c.start()

    loads = {}

    def load(name, k, slot, src, dst, sem):
        c = pltpu.make_async_copy(src, dst, sem)
        c.start()
        loads[name, k] = c

    def get_tokens():
        for n, (key, src, dst) in enumerate((("full", i.full, cut(v.tok, 0, SEQ)), ("masked", i.masked, v.masked), ("cot0", i.cot_full, cut(v.cot, 0, SEQ)), ("cot1", i.cot_masked, cut(v.cot, SEQ, KEEP)))):
            loads[key] = pltpu.make_async_copy(src.at[0], dst, v.lt.at[n])
            loads[key].start()

    def tokens():
        for key in ("full", "masked", "cot0", "cot1"):
            loads[key].wait()
        spread = (lax.broadcasted_iota(jnp.int32, (SEQ, KEEP), 0) == i.keep[...]).astype(B16)
        v.tok[SEQ:TOK] = tn(spread, v.masked[...]).astype(B16)
        save(lambda: (v.tok, o.tok))

    def norm1():
        def body(r, s):
            n, _ = layer_stats(v.tok[r, :].astype(F32))
            v.hid[r, :] = (n * (1.0 + con.mods[1, s]) + con.mods[0, s]).astype(B16)

        by_rows(body)

    def grads_in():
        v.gb[0:SEQ] = (con.mods[5, 0] * v.cot[0:SEQ].astype(F32)).astype(B16)
        v.gb[SEQ:TOK] = (con.mods[5, 1] * v.cot[SEQ:TOK].astype(F32)).astype(B16)
        save(lambda: (v.gb, o.gb))
        transpose_into(v.gb, v.gbt)
        pairs(0, lambda: v.gbt, o.gbp)

    def turn1():
        transpose_into(v.hid, v.h1t)
        pairs(1, lambda: v.h1t, o.h1p)

    def load_q(k):
        load("q", k, k % 2, o.t0.at[k], v.wq.at[k % 2], v.lq.at[k % 2])

    def qkv(k):
        loads["q", k].wait()
        y = (nn(v.hid[...], v.wq[k % 2, :, :, :, 0:864].reshape(D, 864)) + con.qkvb[k]).astype(B16)
        for h in range(12):
            v.qkv[12 * k + h] = y[:, 72 * h : 72 * h + 72]
        if k + 2 < 4:
            load_q(k + 2)
        if k == 3:
            pltpu.make_async_copy(v.qkv, o.qkv, v.oq.at[0]).start()

    def end_qkv():
        pltpu.make_async_copy(v.qkv, o.qkv, v.oq.at[0]).wait()

    def f_end():
        for s in saves:
            s().wait()
        for w in waits:
            for c in w():
                c.wait()

    def heads(k, n):
        def step(g, carry):
            parts = [(4 * g + u, lo, hi) for u in range(4) for lo, hi in ((0, SEQ), (SEQ, TOK))]
            scores = [nt(v.qkv[h, lo:hi], v.qkv[16 + h, lo:hi]) * SCALE for h, lo, hi in parts]
            exps = [jnp.exp(x - jnp.max(x, axis=-1, keepdims=True)) for x in scores]
            probs = [(e * (1.0 / jnp.sum(e, axis=-1, keepdims=True))).astype(B16) for e in exps]
            for (h, lo, hi), pr in zip(parts, probs):
                v.mixh[h, lo:hi] = nn(pr, v.qkv[32 + h, lo:hi]).astype(B16)
            return carry

        lax.fori_loop(k // 4, (k + n) // 4, step, 0)

    def mix():
        for h in range(HEADS):
            v.mixed[:, 72 * h : 72 * h + 72] = v.mixh[h]
        transpose_into(v.mixed, v.mxt)
        pairs(3, lambda: v.mxt, o.mxp)

    def load_o():
        for k in range(4):
            load("o", k, k, o.t0.at[k, :, :, :, pl.ds(768, 384)], v.wo.at[k], v.lo.at[k])

    def attend():
        for k in range(4):
            loads["o", k].wait()
            cols = slice(288 * k, 288 * k + 288)
            v.attn[:, cols] = nn(v.mixed[...], v.wo[k, :, :, :, 96:384].reshape(D, 288)) + con.bias[2, :, cols]

        def body(r, s):
            resid = v.tok[r, :].astype(F32) + con.mods[2, s] * v.attn[r, :]
            n, _ = layer_stats(resid)
            v.hid2[r, :] = (n * (1.0 + con.mods[4, s]) + con.mods[3, s]).astype(B16)

        by_rows(body)
        save(lambda: (v.attn, o.attn))

    def turn2():
        transpose_into(v.hid2, v.h2t)
        pairs(2, lambda: v.h2t, o.h2p)

    def load_1(k):
        load("1", k, k % 2, o.t2.at[k], v.w1.at[k % 2], v.l1.at[k % 2])

    def fc1(k):
        loads["1", k].wait()

        def tile(t, carry):
            lanes = pl.ds(pl.multiple_of(t * 384, 128), 384)
            u = nn(v.hid2[...], v.w1[k % 2, :, :, :, lanes].reshape(D, 384)) + con.wide[k, :, lanes]
            w = u * u
            th = jnp.tanh(GELU_A * u * (1.0 + GELU_B * w))
            v.act[k, :, lanes] = (0.5 * u * (1.0 + th)).astype(B16)
            v.dact[k, :, lanes] = (0.5 * (1.0 + th) + 0.5 * u * (1.0 - th * th) * (GELU_A * (1.0 + 3.0 * GELU_B * w))).astype(B16)
            return carry

        lax.fori_loop(0, 3, tile, 0)
        if k + 2 < 4:
            load_1(k + 2)
        save(lambda: (v.act.at[k], o.act.at[k, pl.ds(0, TOK)]))
        save(lambda: (v.dact.at[k], o.dact.at[k]))
        waits.append(lambda: [remote(v.act.at[k], o.act.at[k, pl.ds(TOK, TOK)], v.as_.at[k], v.ar.at[k], p.s_dev)])
        waits[-1]()[0].start()

    return dict(get_tokens=get_tokens, tokens=tokens, norm1=norm1, grads_in=grads_in, turn1=turn1, load_q=load_q, qkv=qkv, heads=heads, mix=mix, load_o=load_o,
                attend=attend, turn2=turn2, load_1=load_1, fc1=fc1, end_qkv=end_qkv, f_end=f_end)


LANES = (1152, 1152, 1152)
B_ROWS = (32, 32, 32)


class Scatter:
    SEMS = dict(sd=(4, 4, 2), rd=(4, 4, 2), sx=(4, 4), rx=(4, 4), sy=(4, 4), ry=(4, 4), sz=(4, 4), rz=(4, 5),
                cz=(4, 4), bz=(4, 5), cd=(4, 2), bd=(4, 2), cx=(4,), bx=(4,), cy=(4,), by=(4,))

    @classmethod
    def scratch(cls):
        out = []
        for m in range(3):
            b, n = B_ROWS[m], LANES[m]
            a = 144 - b
            out += [pltpu.VMEM(s, B16) for s in ((4, a, n), (4, a, n), (4, a, n), (5, a, n))]
            if b:
                out += [pltpu.VMEM(s, B16) for s in ((5, 4, b, n), (b, n), (b, n), (b, n))]
        return out + [pltpu.SemaphoreType.DMA(s) for s in cls.SEMS.values()]

    @classmethod
    def count(cls):
        return sum(8 if b else 4 for b in B_ROWS) + len(cls.SEMS)

    def __init__(self, p, r, refs):
        self.p, self.r = p, r
        refs = list(refs)
        self.ld, self.lx, self.ly, self.lz = [], [], [], []
        self.lbz, self.lbx, self.lby, self.lbd = {}, {}, {}, {}
        for m in range(3):
            for part in (self.ld, self.lx, self.ly, self.lz):
                part.append(refs.pop(0))
            if B_ROWS[m]:
                for part in (self.lbz, self.lbx, self.lby, self.lbd):
                    part[m] = refs.pop(0)
        for name in self.SEMS:
            setattr(self, name, refs.pop(0))

    def blk(self, m, dp, zs, lo, n):
        return self.r[m].at[dp, zs, pl.ds(lo, n), pl.ds(0, LANES[m])]

    def a(self, m):
        return 144 - B_ROWS[m]

    def half(self, m, j):
        a = self.a(m)
        h = (a // 32) * 16
        return a - h if j % 2 == 0 else h

    def got(self, ref, sem):
        remote(ref, ref, self.sd.at[0, 0, 0], sem, self.p.x_dev).wait_recv()

    def add(self, dst, *lands):
        y = dst[...].astype(F32)
        for land in lands:
            y = y + land[...].astype(F32)
        dst[...] = y.astype(B16)

    def c1(self, m, j):
        p, zs, a, h = self.p, self.p.order[j], self.a(m), self.half(m, j)
        one = remote(self.blk(m, p.dg, zs, 0, h), self.ld[m].at[zs, pl.ds(0, h)], self.sd.at[m, zs, 0], self.rd.at[m, zs, 0], p.x_dev)
        two = remote(self.blk(m, p.dg, zs, h, a - h), self.ld[m].at[zs, pl.ds(h, a - h)], self.sd.at[m, zs, 1], self.rd.at[m, zs, 1], p.y_dev)
        return one, two

    def c2(self, m, j):
        p, zs, a = self.p, self.p.order[j], self.a(m)
        y = remote(self.blk(m, p.yn, zs, 0, a), self.ly[m].at[zs], self.sy.at[m, zs], self.ry.at[m, zs], p.y_dev)
        x = remote(self.blk(m, p.xn, zs, 0, a), self.lx[m].at[zs], self.sx.at[m, zs], self.rx.at[m, zs], p.x_dev)
        return y, x

    def cz_(self, m, j):
        p, zs, a = self.p, self.p.order[j], self.a(m)
        up = zs > p.z
        slot = jnp.where(up, zs, jnp.where(zs == p.z - 1, 4, zs))
        return remote(self.blk(m, p.dp, zs, 0, a), self.lz[m].at[slot], self.sz.at[m, zs], self.rz.at[m, slot], (p.dp, p.f + jnp.where(up, 2, -2)))

    def cb(self, m, j):
        p, zs, a, b = self.p, self.p.order[j], self.a(m), B_ROWS[m]
        up = zs > p.z
        slot = jnp.where(up, zs, jnp.where(zs == p.z - 1, 4, zs))
        src = self.r[m].at[:, zs, pl.ds(a, b), pl.ds(0, LANES[m])]
        return remote(src, self.lbz[m].at[slot], self.cz.at[m, zs], self.bz.at[m, slot], (p.dp, p.f + jnp.where(up, 2, -2)))

    def cb2(self, m):
        p, a, b = self.p, self.a(m), B_ROWS[m]
        h = 16 * ((b // 16 + 1) // 2)
        one = remote(self.blk(m, p.dg, p.z, a, h), self.lbd[m].at[pl.ds(0, h)], self.cd.at[m, 0], self.bd.at[m, 0], p.x_dev)
        two = remote(self.blk(m, p.dg, p.z, a + h, b - h), self.lbd[m].at[pl.ds(h, b - h)], self.cd.at[m, 1], self.bd.at[m, 1], p.y_dev)
        return one, two

    def cb3(self, m):
        p, a, b = self.p, self.a(m), B_ROWS[m]
        y = remote(self.blk(m, p.yn, p.z, a, b), self.lby[m], self.cy.at[m], self.by.at[m], p.y_dev)
        x = remote(self.blk(m, p.xn, p.z, a, b), self.lbx[m], self.cx.at[m], self.bx.at[m], p.x_dev)
        return y, x

    def s1(self, m, j):
        for c in self.c1(m, j):
            c.start()

    def s2(self, m, j):
        p, zs, a, h = self.p, self.p.order[j], self.a(m), self.half(m, j)
        y, x = self.c2(m, j)
        land = self.ld[m].at[zs, pl.ds(0, h)]
        self.got(land, self.rd.at[m, zs, 0])
        self.add(self.blk(m, p.yn, zs, 0, h), land)
        y.start()
        land = self.ld[m].at[zs, pl.ds(h, a - h)]
        self.got(land, self.rd.at[m, zs, 1])
        self.add(self.blk(m, p.xn, zs, h, a - h), land)
        x.start()

    def s3(self, m, j):
        p, zs, a = self.p, self.p.order[j], self.a(m)
        self.got(self.lx[m].at[zs], self.rx.at[m, zs])
        self.got(self.ly[m].at[zs], self.ry.at[m, zs])
        self.add(self.blk(m, p.dp, zs, 0, a), self.lx[m].at[zs], self.ly[m].at[zs])

    def zt(self, m, j):
        p, zs, a = self.p, self.p.order[j], self.a(m)

        @pl.when(p.middle)
        def _():
            land = self.lz[m].at[zs]
            self.got(land, self.rz.at[m, zs])
            self.add(self.blk(m, p.dp, zs, 0, a), land)

        self.cz_(m, j).start()

    def both(self, act):
        @pl.when(self.p.z > 0)
        def _():
            act(self.p.z)

        @pl.when(self.p.z < 3)
        def _():
            act(4)

    def zf(self, m):
        p = self.p

        def take(slot):
            land = self.lz[m].at[slot]
            self.got(land, self.rz.at[m, slot])
            self.add(self.blk(m, p.dp, p.z, 0, self.a(m)), land)

        self.both(take)

    def b1(self, m, j):
        p, zs, a, b = self.p, self.p.order[j], self.a(m), B_ROWS[m]

        @pl.when(p.middle)
        def _():
            self.got(self.lbz[m].at[zs], self.bz.at[m, zs])
            for d in range(4):
                self.add(self.blk(m, d, zs, a, b), self.lbz[m].at[zs, d])

        self.cb(m, j).start()

    def bf(self, m):
        p, a, b = self.p, self.a(m), B_ROWS[m]

        def take(slot):
            self.got(self.lbz[m].at[slot], self.bz.at[m, slot])
            for d in range(4):
                self.add(self.blk(m, d, p.z, a, b), self.lbz[m].at[slot, d])

        self.both(take)
        for c in self.cb2(m):
            c.start()

    def b3(self, m):
        p, a, b = self.p, self.a(m), B_ROWS[m]
        h = 16 * ((b // 16 + 1) // 2)
        y, x = self.cb3(m)
        land = self.lbd[m].at[pl.ds(0, h)]
        self.got(land, self.bd.at[m, 0])
        self.add(self.blk(m, p.yn, p.z, a, h), land)
        y.start()
        land = self.lbd[m].at[pl.ds(h, b - h)]
        self.got(land, self.bd.at[m, 1])
        self.add(self.blk(m, p.xn, p.z, a + h, b - h), land)
        x.start()

    def b4(self, m):
        p, a, b = self.p, self.a(m), B_ROWS[m]
        self.got(self.lbx[m], self.bx.at[m])
        self.got(self.lby[m], self.by.at[m])
        self.add(self.blk(m, p.dp, p.z, a, b), self.lbx[m], self.lby[m])

    def sent(self, m):
        for j in range(4):
            for c in self.c1(m, j) + self.c2(m, j):
                c.wait_send()
            if j:
                self.cz_(m, j).wait_send()
                if B_ROWS[m]:
                    self.cb(m, j).wait_send()
        if B_ROWS[m]:
            for c in self.cb2(m) + self.cb3(m):
                c.wait_send()


class Back:
    SEMS = dict(r1=(8,), s1=(8,), r2=(4,), s2=(4,), rb=(4,), sb=(4,), r3=(8,), s3=(8,), r4=(4,), s4=(4,))
    SHAPES = dict(msg=(8, 4, D), in1=(8, 4, D), gm=(16, 864), in2=(4, 16, 864), bs=(1, D), inb=(4, 1, D), sil=(8, 8, 288), silr=(64, 288),
                  gmr=(64, 864), b8=(8, 8, 288), in3=(8, 8, 288), b4=(4, 2, 288), in4=(4, 2, 288))

    @classmethod
    def scratch(cls):
        return [pltpu.VMEM(s, F32) for s in cls.SHAPES.values()] + [pltpu.SemaphoreType.DMA(s) for s in cls.SEMS.values()]

    def __init__(self, p, gmods, gbias, w_ada, scratch):
        self.p, self.gmods, self.gbias, self.w_ada = p, gmods, gbias, w_ada
        for name, ref in zip(list(self.SHAPES) + list(self.SEMS), scratch, strict=True):
            setattr(self, name, ref)

    def over_dp(self, src_of, land, sem_s, sem_r):
        p = self.p
        return [remote(src_of(r), land.at[p.dp], sem_s.at[r], sem_r.at[p.dp], (r, p.f)) for r in p.rows]

    def over_f(self, src_of, land, sem_s, sem_r):
        p = self.p
        return [remote(src_of(c), land.at[p.f], sem_s.at[c], sem_r.at[p.f], (p.dp, c)) for c in p.cols]

    def copies(self, step):
        return {
            1: lambda: self.over_f(lambda c: self.msg.at[c], self.in1, self.s1, self.r1),
            2: lambda: self.over_dp(lambda r: self.gm, self.in2, self.s2, self.r2),
            "b": lambda: self.over_dp(lambda r: self.bs, self.inb, self.sb, self.rb),
            3: lambda: self.over_f(lambda c: self.b8.at[c], self.in3, self.s3, self.r3),
            4: lambda: self.over_dp(lambda r: self.b4.at[r], self.in4, self.s4, self.r4),
        }[step]()

    def send(self, step):
        for c in self.copies(step):
            c.start()

    def arrived(self, land, sem, peers):
        for q in peers:
            remote(land.at[q], land.at[q], self.s1.at[0], sem.at[q], self.p.x_dev).wait_recv()

    def begin(self):
        p = self.p
        for s in range(2):
            for f in range(8):
                at = 864 * f
                while at < 864 * (f + 1):
                    b = at // D
                    end = min(864 * (f + 1), D * (b + 1))
                    self.msg[f, s : s + 1, at - 864 * f : end - 864 * f] = self.gmods[b, s, :, at - D * b : end - D * b].astype(B16).astype(F32)
                    at = end
                self.msg[f, s : s + 1, 864:D] = jnp.zeros((1, D - 864), F32)
        for f in range(8):
            for i, lo in enumerate((0, 144, 288, 1008)):
                self.msg[f, 2:3, lo : lo + 144] = self.gbias[i, :, 144 * f : 144 * f + 144]
            half = 576 * (f % 2)
            self.msg[f, 2:3, 432:1008] = self.gbias[4 + f // 2, :, half : half + 576]
            self.msg[f, 3:4, :] = jnp.zeros((1, D), F32)
        self.send(1)
        self.in1[p.f] = self.msg[p.f]

    def second(self, sil):
        p = self.p
        self.arrived(self.in1, self.r1, p.cols)
        total = jnp.zeros((1, D), F32)
        for f in range(8):
            rows = self.in1[f]
            self.gm[2 * f : 2 * f + 2, :] = rows[0:2, 0:864]
            total = total + rows[2:3]
        self.bs[...] = total
        self.send(2)
        self.send("b")
        self.in2[p.dp] = self.gm[...]
        self.inb[p.dp] = self.bs[...]
        for f in range(8):
            for d in range(4):
                self.silr[16 * d + 2 * f : 16 * d + 2 * f + 2, :] = sil[f, 2 * d : 2 * d + 2]

    def third(self, out_w, out_b, out_biases):
        p = self.p
        self.arrived(self.in2, self.r2, p.rows)
        self.arrived(self.inb, self.rb, p.rows)
        gm = self.in2[...].reshape(64, 864)
        low = gm.astype(B16)
        back = nt(low, self.w_ada[...])
        for f in range(8):
            for d in range(4):
                self.b8[f, 2 * d : 2 * d + 2, :] = back[16 * d + 2 * f : 16 * d + 2 * f + 2]
        self.send(3)
        self.in3[p.f] = self.b8[p.f]
        out_b[...] = jnp.sum(gm, axis=0, keepdims=True)
        out_w[...] = tn(self.silr[...].astype(B16), low)
        row = self.inb[0] + self.inb[1] + self.inb[2] + self.inb[3]
        for ref, lo in zip(out_biases, (0, 144, 288, 432, 1008), strict=True):
            ref[...] = row[:, lo : lo + ref.shape[1]]

    def fourth(self):
        p = self.p
        self.arrived(self.in3, self.r3, p.cols)
        total = self.in3[0]
        for f in range(1, 8):
            total = total + self.in3[f]
        for d in range(4):
            self.b4[d] = total[2 * d : 2 * d + 2]
        self.send(4)
        self.in4[p.dp] = self.b4[p.dp]

    def last(self, conds, outs):
        p = self.p
        self.arrived(self.in4, self.r4, p.rows)
        for s in range(2):
            x = conds[s][...].astype(F32)
            sig = 1.0 / (1.0 + jnp.exp(-x))
            slope = sig * (1.0 + x * (1.0 - sig))
            for d in range(4):
                outs[s][:, 288 * d : 288 * d + 288] = self.in4[d, s : s + 1, :] * slope[:, 288 * d : 288 * d + 288]

    def drain(self):
        for step in (1, 2, "b", 3, 4):
            for c in self.copies(step):
                c.wait_send()


def backward_steps(p, i, o, v, con, back):
    loads, ends = {}, []
    count = dict(ld=0, ws=0)

    def load(key, src, dst):
        c = pltpu.make_async_copy(src, dst, v.ld.at[count["ld"] % 24])
        count["ld"] += 1
        c.start()
        loads[key] = c

    def save(src, dst):
        c = pltpu.make_async_copy(src, dst, v.ws.at[count["ws"]])
        count["ws"] += 1
        c.start()
        return c

    pending = {}

    by_dp = (p.dg, p.yn, p.xn, p.dp)
    by_z = p.order[::-1]

    def load_gbp():
        load("gbp", o.gbp, v.gbp)

    def load_act(n):
        load(("actp", n), o.act.at[by_dp[n]], v.actp.at[n % 2])

    def grad_fc2(n):
        if n == 0:
            loads["gbp"].wait()
        loads["actp", n].wait()
        dp = by_dp[n]

        y = nn(v.gbp[...].reshape(576, 768), v.actp[n % 2]).astype(B16)
        for z in range(4):
            v.r_big[dp, z] = y[144 * z : 144 * z + 144]
        if n + 2 < 4:
            load_act(n + 2)

    def load_mlp(k):
        s = k % 2
        if k == 0:
            load("gb", o.gb, v.gb)
        load(("w2", k), o.t3.at[k], v.w2.at[s])
        if k == 0:
            load_w1(k)
        load(("dact", k), o.dact.at[k], v.dact.at[s])

    def load_w1(k):
        load(("w1", k), o.t2.at[k], v.w1.at[0])

    def mlp(k):
        s = k % 2
        if k == 0:
            loads["gb"].wait()
        loads["w2", k].wait()
        loads["dact", k].wait()
        if k >= 2:
            c, w = pending.pop(("gup", k - 2))
            c.wait_send()
            w.wait()

        gu = (nn(v.gb[...], v.w2[s].reshape(D, D)) * v.dact[s].astype(F32)).astype(B16)
        v.gup[s] = gu
        v.gbias[4 + k] = jnp.sum(gu.astype(F32), axis=0, keepdims=True)
        c = remote(v.gup.at[s], o.gupp.at[k, pl.ds(TOK, TOK)], v.gs.at[k], v.gr.at[k], p.s_dev)
        c.start()
        pending["gup", k] = (c, save(v.gup.at[s], o.gupp.at[k, pl.ds(0, TOK)]))
        loads["w1", k].wait()

        two = nt(v.gup[s], v.w1[0].reshape(D, D))
        v.gh2[...] = two if k == 0 else v.gh2[...] + two
        if k + 1 < 4:
            load_w1(k + 1)
        if k + 2 < 4:
            load_mlp(k + 2)

    def end_mlp():
        for k in (2, 3):
            c, w = pending.pop(("gup", k))
            c.wait_send()
            w.wait()

    def load_g():
        load("h2p", o.h2p, v.h2p)
        for n in range(2):
            load_gup(n)

    def load_gup(n):
        if n == 0:
            for k in range(4):
                sib = o.gupp.at[k, pl.ds(TOK, TOK)]
                remote(sib, sib, v.gs.at[k], v.gr.at[k], p.s_dev).wait_recv()
        load(("gupv", n), o.gupp.at[by_z[n]], v.gupv.at[n % 2])

    def grad_fc1(n):
        if n == 0:
            loads["h2p"].wait()
        loads["gupv", n].wait()
        z = by_z[n]

        y = nn(v.h2p[...].reshape(576, 768), v.gupv[n % 2]).astype(B16)
        for d in range(4):
            v.r_fc1[d, z] = y[144 * d : 144 * d + 144]
        if n + 2 < 4:
            load_gup(n + 2)

    def load_x():
        for n in range(2):
            load_branch(n)
        load_n()

    def load_branch(k):
        load(("w2", k), o.t3.at[k], v.w2.at[k % 2])
        load(("act", k), o.act.at[k, pl.ds(0, TOK)], v.acto.at[k % 2])

    def branch(k):
        loads["w2", k].wait()
        loads["act", k].wait()
        one = nt(v.acto[k % 2], v.w2[k % 2].reshape(D, D))
        v.branch[...] = one if k == 0 else v.branch[...] + one
        if k + 2 < 4:
            load_branch(k + 2)

    def result():
        for key in ("tok", "attn", "cot0", "cot1"):
            loads[key].wait()

        def body(r, s):
            branch = v.branch[r, :] + con.bias[3]
            v.res[r, :] = (v.tok[r, :].astype(F32) + con.mods[2, s] * v.attn[r, :] + con.mods[5, s] * branch).astype(B16)
            v.gmods[5, s] += jnp.sum(v.cot[r, :].astype(F32) * branch, axis=0, keepdims=True)

        by_rows(body)
        pltpu.make_async_copy(v.res, o.result, v.fs.at[0]).start()

    def end_result():
        pltpu.make_async_copy(v.res, o.result, v.fs.at[0]).wait()

    def load_n():
        load("cot0", i.cot_full.at[0], cut(v.cot, 0, SEQ))
        load("cot1", i.cot_masked.at[0], cut(v.cot, SEQ, KEEP))
        load("tok", o.tok, v.tok)
        load("attn", o.attn, v.attn)

    def norm2():
        for key in ("tok", "attn", "cot0", "cot1"):
            loads[key].wait()
        zero = jnp.zeros((1, D), F32)
        for b in range(6):
            for s in range(2):
                v.gmods[b, s] = zero
        v.gbias[2] = zero
        v.gbias[3] = zero

        def body(r, s):
            tok = v.tok[r, :].astype(F32)
            attn = v.attn[r, :]
            resid = tok + con.mods[2, s] * attn
            n, inv = layer_stats(resid)
            cot = v.cot[r, :].astype(F32)
            gh = v.gh2[r, :]
            v.gmods[4, s] += jnp.sum(gh * n, axis=0, keepdims=True)
            v.gmods[3, s] += jnp.sum(gh, axis=0, keepdims=True)
            u = gh * (1.0 + con.mods[4, s])
            gres = cot + inv * (u - jnp.mean(u, axis=-1, keepdims=True) - n * jnp.mean(u * n, axis=-1, keepdims=True))
            v.gres[r, :] = gres
            v.gmods[2, s] += jnp.sum(gres * attn, axis=0, keepdims=True)
            ga = (con.mods[2, s] * gres).astype(B16)
            v.ga[r, :] = ga
            v.gbias[2] += jnp.sum(ga.astype(F32), axis=0, keepdims=True)
            v.gbias[3] += jnp.sum(v.gb[r, :].astype(F32), axis=0, keepdims=True)

        by_rows(body)

    def load_o():
        for k in range(4):
            load(("wo", k), o.t0.at[k, :, :, :, pl.ds(768, 384)], v.wo.at[k])

    def give_a():
        remote(v.ga, cut(o.gap, TOK, TOK), v.ps.at[0], v.gpr.at[0], p.s_dev).start()
        pltpu.make_async_copy(v.ga, cut(o.gap, 0, TOK), v.pb.at[0]).start()

    def load_m():
        load("mxp", o.mxp, v.mxp)
        remote(v.ga, cut(o.gap, TOK, TOK), v.ps.at[0], v.gpr.at[0], p.s_dev).wait()
        pltpu.make_async_copy(v.ga, cut(o.gap, 0, TOK), v.pb.at[0]).wait()
        load("gap", o.gap, v.gapv)

    def grad_mixed():
        y = jnp.zeros((TOK, D), F32)
        for k in range(4):
            loads["wo", k].wait()
            y = y + nt(v.ga[:, 288 * k : 288 * k + 288], v.wo[k, :, :, :, 96:384].reshape(D, 288))
        y = y.astype(B16)
        for h in range(HEADS):
            v.gmh[h] = y[:, 72 * h : 72 * h + 72]

    def grad_out():
        loads["mxp"].wait()
        loads["gap"].wait()
        y = nn(v.mxp[...].reshape(576, 768), v.gapv[...]).astype(B16)
        for d in range(4):
            for z in range(4):
                v.r_big[d, z, :, 864:1152] = y[144 * d : 144 * d + 144, 288 * z : 288 * z + 288]

    def load_q():
        load("qkv", o.qkv, v.qkv)
        load("tok", o.tok, v.tok)
        load("h1p", o.h1p, v.h1p)
        for k in range(2):
            load_wq(k)

    def load_wq(k):
        load(("wq", k), o.t0.at[k], v.wq.at[k % 2])

    def heads(k, n):
        if k == 0:
            loads["qkv"].wait()

        def step(g, carry):
            parts = [(4 * g + u, lo, hi) for u in range(4) for lo, hi in ((0, SEQ), (SEQ, TOK))]
            qs, ks, vs = ([v.qkv[16 * n + h, lo:hi] for h, lo, hi in parts] for n in range(3))
            gs = [v.gmh[h, lo:hi] for h, lo, hi in parts]
            scores = [nt(key, q) * SCALE for q, key in zip(qs, ks)]
            gps = [nt(val, gm) for val, gm in zip(vs, gs)]
            exps = [jnp.exp(x - jnp.max(x, axis=0, keepdims=True)) for x in scores]
            probs = [e * (1.0 / jnp.sum(e, axis=0, keepdims=True)) for e in exps]
            gsc = [(pr * (gp - jnp.sum(pr * gp, axis=0, keepdims=True))).astype(B16) for pr, gp in zip(probs, gps)]
            for (h, lo, hi), pr, gc, q, key, gm in zip(parts, probs, gsc, qs, ks, gs):
                v.qkv[32 + h, lo:hi] = nn(pr.astype(B16), gm).astype(B16)
                v.qkv[h, lo:hi] = (tn(gc, key) * SCALE).astype(B16)
                v.qkv[16 + h, lo:hi] = (nn(gc, q) * SCALE).astype(B16)
            return carry

        lax.fori_loop(k // 4, (k + n) // 4, step, 0)

    def grad_h1(k):
        s = k % 2
        if k >= 2:
            c, w = pending.pop(("gq", k - 2))
            c.wait_send()
            w.wait()
        for h in range(12):
            v.gq[s, :, 72 * h : 72 * h + 72] = v.qkv[12 * k + h]
        c = remote(v.gq.at[s], o.gqp.at[k, pl.ds(TOK, TOK)], v.qs.at[k], v.qr.at[k], p.s_dev)
        c.start()
        pending["gq", k] = (c, save(v.gq.at[s], o.gqp.at[k, pl.ds(0, TOK)]))
        if k != 2:
            total = jnp.sum(v.gq[s].astype(F32), axis=0, keepdims=True)
        else:
            total = jnp.sum(v.gq[s, :, 576:864].astype(F32), axis=0, keepdims=True)
        if k == 0:
            v.gbias[0, :, 0:864] = total
        elif k == 1:
            v.gbias[0, :, 864:D] = total[:, 0:288]
        elif k == 2:
            v.gbias[1, :, 0:288] = total
        else:
            v.gbias[1, :, 288:D] = total
        loads["wq", k].wait()

        y = nt(v.gq[s], v.wq[s, :, :, :, 0:864].reshape(D, 864))
        v.gh1[...] = y if k == 0 else v.gh1[...] + y
        if k + 2 < 4:
            load_wq(k + 2)

    def load_gq(n):
        if n == 0:
            for k in range(4):
                sib = o.gqp.at[k, pl.ds(TOK, TOK)]
                remote(sib, sib, v.qs.at[k], v.qr.at[k], p.s_dev).wait_recv()
            for k in (2, 3):
                c, w = pending.pop(("gq", k))
                c.wait_send()
                w.wait()
        load(("gqv", n), o.gqp.at[by_z[n]], v.gqv.at[n % 2])

    def grad_qkv(n):
        if n == 0:
            loads["h1p"].wait()
        loads["gqv", n].wait()
        y = nn(v.h1p[...].reshape(576, 768), v.gqv[n % 2]).astype(B16)
        for d in range(4):
            v.r_big[d, by_z[n], :, 0:864] = y[144 * d : 144 * d + 144]
        if n + 2 < 4:
            load_gq(n + 2)

    def norm1():
        loads["tok"].wait()

        def body(r, s):
            n, inv = layer_stats(v.tok[r, :].astype(F32))
            gh = v.gh1[r, :]
            v.gmods[1, s] += jnp.sum(gh * n, axis=0, keepdims=True)
            v.gmods[0, s] += jnp.sum(gh, axis=0, keepdims=True)
            u = gh * (1.0 + con.mods[1, s])
            v.gres[r, :] += inv * (u - jnp.mean(u, axis=-1, keepdims=True) - n * jnp.mean(u * n, axis=-1, keepdims=True))

        by_rows(body)

    def put_full():
        pltpu.make_async_copy(cut(v.gres, 0, SEQ), o.gfull, v.fs.at[3]).start()

    def end_full():
        pltpu.make_async_copy(cut(v.gres, 0, SEQ), o.gfull, v.fs.at[3]).wait()

    def spread():
        hot = (lax.broadcasted_iota(jnp.int32, (SEQ, KEEP), 0) == i.keep[...]).astype(F32)
        v.spr[...] = lax.dot_general(hot, v.gres[SEQ:TOK], (((1,), (0,)), ((), ())), precision=lax.Precision.HIGHEST, preferred_element_type=F32)
        pltpu.make_async_copy(v.spr, o.gmasked, v.fs.at[1]).start()

    def end_spread():
        pltpu.make_async_copy(v.spr, o.gmasked, v.fs.at[1]).wait()

    def put(n, src, dst):
        return pltpu.make_async_copy(src, dst, v.fo.at[n])

    def finals(n):
        return put(n, v.part[n].at[0], (o.gw_fc1, o.gw_qkv, o.gw_out)[n].at[p.c])

    def swaps(n):
        return remote(v.part[n].at[1], (o.gw_fc1, o.gw_qkv, o.gw_out)[n].at[p.c], v.xs.at[n], v.xr.at[n], p.s_dev)

    def swap(block, width, n):
        first = p.c == 0
        lo, hi = block[:, 0:width], block[:, width : 2 * width]
        v.part[n][1] = jnp.where(first, hi, lo)
        v.part[n][0] = jnp.where(first, lo, hi)
        finals(n).start()
        swaps(n).start()

    def end_swap(n):
        finals(n).wait()
        swaps(n).wait_send()
        land = (o.gw_fc1, o.gw_qkv, o.gw_out)[n].at[1 - p.c]
        remote(land, land, v.xs.at[n], v.xr.at[n], p.s_dev).wait_recv()

    def out_fc2():
        put(3, v.r_big.at[p.dp, p.z], o.gw_fc2).start()

    def end_fc2():
        put(3, v.r_big.at[p.dp, p.z], o.gw_fc2).wait()

    def out_fc1():
        swap(v.r_fc1[p.dp, p.z], 576, 0)

    def out_qo():
        swap(v.r_big[p.dp, p.z, :, 0:864], 432, 1)
        swap(v.r_big[p.dp, p.z, :, 864:1152], 144, 2)

    def end_fc1():
        end_swap(0)

    def end_qo():
        end_swap(1)
        end_swap(2)

    def back_second():
        back.second(con.in2)

    def back_third():
        back.third(v.gwa, o.gb_ada, (o.gb_q, o.gb_v, o.gb_out, o.gb_fc1, o.gb_fc2))

        pltpu.make_async_copy(v.gwa, o.gw_ada, v.fs.at[2]).start()

    def end_ada():
        pltpu.make_async_copy(v.gwa, o.gw_ada, v.fs.at[2]).wait()

    def back_last():
        back.last((i.cond_full, i.cond_masked), (o.gc_full, o.gc_masked))

    table = {n: f for n, f in locals().items() if callable(f)}
    table.update(back_begin=back.begin, back_fourth=back.fourth)
    return table


STAGE = dict(got_q=((144, 432), B16), got_1=((144, 576), B16), got_o=((144, 144), B16), w_out=((288, 144), B16), bq=((144, 1152), B16), b1=((144, 1152), B16),
             gmods=((6, 2, 1, D), F32), gbias=((8, 1, D), F32), part1=((2, 144, 576), B16), partq=((2, 144, 432), B16), parto=((2, 144, 144), B16))
SIGNALS = dict(st=(3,), rt=(3,), lq=(2,), lo=(4,), l1=(2,), lt=(4,), pt=(4, 4), pr=(4, 4), pl_=(4, 4), as_=(4,), ar=(4,), ow=(16,), oq=(1,),
               ld=(24,), ws=(24,), gs=(4,), gr=(4,), qs=(4,), qr=(4,), ps=(4,), pb=(4,), gpr=(4,), xs=(3,), xr=(3,), fs=(4,), fo=(4,))
SCOPE_P = dict(hid=((TOK, D), B16), hid2=((TOK, D), B16), tok=((TOK, D), B16), h1t=((8, 144, TOK), B16), h2t=((8, 144, TOK), B16), gbt=((8, 144, TOK), B16), mxt=((8, 144, TOK), B16),
           gb=((TOK, D), B16), mixed=((TOK, D), B16), attn=((TOK, D), F32), act=((4, TOK, D), B16), dact=((4, TOK, D), B16))
SCOPE_I = dict(masked=((SEQ, D), B16), cot=((TOK, D), B16))
SCOPE_H = dict(qkv=((48, TOK, HEAD_DIM), B16), mixh=((HEADS, TOK, HEAD_DIM), B16), wq=((2, 4, 2, 144, D), B16))
SCOPE_U = dict(wo=((4, 4, 2, 144, 384), B16), w1=((2, 4, 2, 144, D), B16))
SCOPE_R = dict(r_big=((4, 4, 144, D), B16), r_fc1=((4, 4, 144, D), B16), gres=((TOK, D), F32), ga=((TOK, D), B16))
SCOPE_M = dict(gb=((TOK, D), B16), gh2=((TOK, D), F32))
SCOPE_W = dict(gbp=((4, 144, 768), B16), actp=((2, 2 * TOK, D), B16), w2=((2, 4, 2, 144, D), B16), w1=((1, 4, 2, 144, D), B16),
           dact=((2, TOK, D), B16), gup=((2, TOK, D), B16))
SCOPE_G = dict(h2p=((4, 144, 768), B16), gupv=((2, 2 * TOK, D), B16))
SCOPE_N = dict(tok=((TOK, D), B16), attn=((TOK, D), F32), cot=((TOK, D), B16))
SCOPE_X = dict(w2=((2, 4, 2, 144, D), B16), acto=((2, TOK, D), B16), branch=((TOK, D), F32), tok=((TOK, D), B16), attn=((TOK, D), F32), cot=((TOK, D), B16), res=((TOK, D), B16))
SCOPE_S = dict(spr=((SEQ, D), F32), gwa=((288, 864), F32))
SCOPE_A = dict(gmh=((HEADS, TOK, HEAD_DIM), B16))
SCOPE_B = dict(wo=((4, 4, 2, 144, 384), B16))
SCOPE_O = dict(gapv=((2 * TOK, D), B16), mxp=((4, 144, 768), B16))
SCOPE_Q = dict(qkv=((48, TOK, HEAD_DIM), B16), wq=((2, 4, 2, 144, D), B16), gq=((2, TOK, 864), B16),
           gqv=((2, 2 * TOK, 864), B16), h1p=((4, 144, 768), B16), gh1=((TOK, D), F32), tok=((TOK, D), B16))
INS_V = dict(keep=0, cond_full=0, cond_masked=0, w_ada=0, b_ada=0, b_q=0, b_v=0, b_out=0, b_fc1=0, b_fc2=0, w_qkv=0, w_out=0, w_fc1=0, w_fc2=0)
INS_A = dict(full=0, masked=0, cot_full=0, cot_masked=0)
OUT_V = dict(gc_full=((1, D), F32), gc_masked=((1, D), F32), gb_ada=((1, 864), F32), gb_q=((1, 144), F32), gb_v=((1, 144), F32),
             gb_out=((1, 144), F32), gb_fc1=((1, 576), F32), gb_fc2=((1, 144), F32))
OUT_A = dict(
    result=((TOK, D), B16), gfull=((SEQ, D), F32), gmasked=((SEQ, D), F32), gw_ada=((288, 864), F32), gw_qkv=((2, 144, 432), B16),
    gw_out=((2, 144, 144), B16), gw_fc1=((2, 144, 576), B16), gw_fc2=((144, D), B16),
    t0=((4, 4, 2, 144, D), B16), t2=((4, 4, 2, 144, D), B16), t3=((4, 4, 2, 144, D), B16),
    tok=((TOK, D), B16), qkv=((48, TOK, HEAD_DIM), B16), attn=((TOK, D), F32),
    mxp=((4, 144, 768), B16), h1p=((4, 144, 768), B16), h2p=((4, 144, 768), B16), gbp=((4, 144, 768), B16), act=((4, 2 * TOK, D), B16), dact=((4, TOK, D), B16), gb=((TOK, D), B16),
    gupp=((4, 2 * TOK, D), B16), gqp=((4, 2 * TOK, 864), B16), gap=((2 * TOK, D), B16),
)


def block_kernel(events, *refs):
    i, o, v = Bag(), Bag(), Bag()
    refs = list(refs)
    for bag, names in ((i, INS_V), (i, INS_A), (o, OUT_V), (o, OUT_A), (v, STAGE), (v, SIGNALS)):
        for n in names:
            setattr(bag, n, refs.pop(0))
    v.part = (v.part1, v.partq, v.parto)
    p = Place()
    con_refs = [refs.pop(0) for _ in range(len(Conditions.SHAPES) + len(Conditions.SEMS))]
    back_refs = [refs.pop(0) for _ in range(len(Back.SHAPES) + len(Back.SEMS))]
    sc_refs = [refs.pop(0) for _ in range(Scatter.count())]
    con = Conditions(p, (i.cond_full, i.cond_masked), i.w_ada, i.b_ada, (i.b_q, i.b_v, i.b_out, i.b_fc1, i.b_fc2), con_refs)
    back = Back(p, v.gmods, v.gbias, i.w_ada, back_refs)
    sc = Scatter(p, None, sc_refs)
    g = Gather(p, (o.t0, o.t2, o.t3), (v.bq, v.b1, i.w_fc2), refs)
    f_table = forward_steps(p, i, o, v, con)
    table = backward_steps(p, i, o, v, con, back)
    f_table.update(second=con.second, third=con.third, fourth=con.fourth, last=con.last, begin=con.begin)
    table.update({"f_" + n.removeprefix("f_"): f for n, f in f_table.items()})
    table.update(own=g.own, bown=g.bown, arr=g.arr, cross=g.cross, bcross=g.bcross, bz=g.bz_, barr=g.barr, fin=g.fin, have=g.have)
    table.update(s1=sc.s1, s2=sc.s2, s3=sc.s3, zt=sc.zt, zf=sc.zf, b1=sc.b1, bf=sc.bf, b3=sc.b3, b4=sc.b4, sent=sc.sent)

    def stages(n):
        return stage(p, (i.w_qkv, v.w_out, i.w_fc1)[n], (v.got_q, v.got_o, v.got_1)[n], v.st.at[n], v.rt.at[n])

    def join_q():
        stages(0).wait_recv()
        join(p, i.w_qkv, v.got_q, v.bq)
        stages(1).wait_recv()
        join(p, v.w_out, v.got_o, v.bq, 864)

    def join_1():
        stages(2).wait_recv()
        join(p, i.w_fc1, v.got_1, v.b1)

    table.update(join_q=join_q, join_1=join_1)

    def run(queue):
        for name, args in queue:
            if args and isinstance(args[0], dict):
                spec = args[0]

                def scope(*inner, spec=spec):
                    for n, ref in zip(spec, inner, strict=True):
                        setattr(v, n, ref)
                    if spec is SCOPE_R:
                        sc.r = (v.r_big, v.r_fc1, v.r_big)
                    run(queue)

                pl.run_scoped(scope, *[pltpu.VMEM(s, d) for s, d in spec.values()])
            elif name not in table:
                return
            else:
                table[name](*args)

    v.w_out[...] = i.w_out[...].astype(F32).T.astype(B16)
    p.barrier()
    for n in range(3):
        stages(n).start()
    run(iter(events))
    for n in range(3):
        stages(n).wait_send()
    con.drain()
    back.drain()
    g.drain()


def block_events():
    e = Script()
    e.bown(FC2)
    e.join_q()
    e.bown(QO)
    e.own(QO)
    e.join_1()
    e.bcross(QO)
    e.bown(FC1)
    e.own(FC1)
    e.bcross(FC2)
    e.open(SCOPE_P)
    e.open(SCOPE_I)
    e.f_get_tokens()
    e.arr(QO, 1)
    e.f_begin()
    e.bz(QO)
    e.cross(QO, 0)
    e.f_second()
    e.arr(QO, 2)
    e.arr(QO, 3)
    e.f_tokens()
    e.barr(QO, 1)
    e.barr(QO, 2)
    e.f_third()
    e.cross(QO, 2)
    e.fin(QO, 0)
    e.f_fourth()
    e.barr(QO, 3)
    e.bcross(FC1)
    e.f_last()
    e.cross(QO, 3)
    e.cross(QO, 1)
    e.f_norm1()
    e.arr(FC1, 2)
    e.bz(FC1)
    e.f_grads_in()
    e.fin(QO, 1)
    e.arr(FC1, 1)
    e.cross(FC1, 2)
    e.close()
    e.f_turn1()
    e.fin(QO, 2)
    e.cross(FC1, 0)
    e.open(SCOPE_H)
    e.arr(FC1, 3)
    e.cross(FC1, 1)
    e.fin(QO, 3)
    e.barr(FC1, 2)
    e.own(FC2)
    e.have(QO)
    e.f_load_q(0)
    e.fin(FC1, 0)
    e.barr(FC1, 1)
    e.fin(FC1, 2)
    e.bz(FC2)
    e.f_load_q(1)
    e.f_qkv(0)
    e.f_qkv(1)
    e.f_qkv(2)
    e.f_qkv(3)
    e.f_heads(0, 4)
    e.f_heads(4, 4)
    e.cross(FC1, 3)
    e.fin(FC1, 1)
    e.f_heads(8, 4)
    e.f_heads(12, 4)
    e.arr(FC2, 1)
    e.cross(FC2, 0)
    e.f_mix()
    e.barr(FC1, 3)
    e.f_end_qkv()
    e.close()
    e.open(SCOPE_U)
    e.fin(FC1, 3)
    e.f_load_o()
    e.f_attend()
    e.f_turn2()
    e.arr(FC2, 2)
    e.have(FC1)
    e.f_load_1(0)
    e.f_load_1(1)
    e.f_fc1(0)
    e.cross(FC2, 1)
    e.arr(FC2, 3)
    e.f_fc1(1)
    e.fin(FC2, 0)
    e.barr(FC2, 1)
    e.cross(FC2, 2)
    e.barr(FC2, 2)
    e.f_fc1(2)
    e.fin(FC2, 1)
    e.f_fc1(3)
    e.barr(FC2, 3)
    e.close()
    e.cross(FC2, 3)
    e.fin(FC2, 2)
    e.f_end()
    e.close()
    e.open(SCOPE_R)
    e.open(SCOPE_M)
    e.open(SCOPE_W)
    e.load_gbp()
    e.load_act(0)
    e.load_act(1)
    e.grad_fc2(0)
    e.fin(FC2, 3)
    e.s1(FC2, 2)
    e.s1(FC2, 1)
    e.grad_fc2(1)
    e.s1(FC2, 3)
    e.grad_fc2(2)
    e.grad_fc2(3)
    e.b1(FC2, 3)
    e.s2(FC2, 2)
    e.have(FC2)
    e.s1(FC2, 0)
    e.load_mlp(0)
    e.load_mlp(1)
    e.mlp(0)
    e.b1(FC2, 2)
    e.s2(FC2, 3)
    e.s2(FC2, 1)
    e.b1(FC2, 1)
    e.mlp(1)
    e.mlp(2)
    e.mlp(3)
    e.s3(FC2, 3)
    e.zt(FC2, 3)
    e.end_mlp()
    e.close()
    e.s2(FC2, 0)
    e.open(SCOPE_N)
    e.load_n()
    e.norm2()
    e.give_a()
    e.close()
    e.close()
    e.s3(FC2, 1)
    e.zt(FC2, 1)
    e.s3(FC2, 2)
    e.bf(FC2)
    e.open(SCOPE_G)
    e.load_g()
    e.grad_fc1(0)
    e.grad_fc1(1)
    e.s1(FC1, 2)
    e.b3(FC2)
    e.zt(FC2, 2)
    e.s3(FC2, 0)
    e.grad_fc1(2)
    e.grad_fc1(3)
    e.s1(FC1, 1)
    e.close()
    e.open(SCOPE_A)
    e.open(SCOPE_B)
    e.load_o()
    e.grad_mixed()
    e.b1(FC1, 3)
    e.s1(FC1, 0)
    e.close()
    e.open(SCOPE_Q)
    e.b4(FC2)
    e.s2(FC1, 2)
    e.s1(FC1, 3)
    e.zf(FC2)
    e.out_fc2()
    e.load_q()
    e.end_fc2()
    e.sent(FC2)
    e.open(SCOPE_O)
    e.load_m()
    e.grad_out()
    e.close()
    e.b1(FC1, 2)
    e.heads(0, 4)
    e.heads(4, 4)
    e.b1(FC1, 1)
    e.heads(8, 4)
    e.s2(FC1, 3)
    e.s2(FC1, 0)
    e.s3(FC1, 2)
    e.s2(FC1, 1)
    e.heads(12, 4)
    e.grad_h1(0)
    e.zt(FC1, 2)
    e.grad_h1(1)
    e.s3(FC1, 3)
    e.grad_h1(2)
    e.zt(FC1, 3)
    e.grad_h1(3)
    e.load_gq(0)
    e.load_gq(1)
    e.grad_qkv(0)
    e.b1(QO, 3)
    e.s1(QO, 3)
    e.grad_qkv(1)
    e.grad_qkv(2)
    e.s1(QO, 2)
    e.bf(FC1)
    e.grad_qkv(3)
    e.s1(QO, 1)
    e.norm1()
    e.b1(QO, 2)
    e.put_full()
    e.s2(QO, 3)
    e.s2(QO, 2)
    e.b1(QO, 1)
    e.s1(QO, 0)
    e.close()
    e.close()
    e.open(SCOPE_X)
    e.load_x()
    e.s3(FC1, 1)
    e.branch(0)
    e.branch(1)
    e.branch(2)
    e.branch(3)
    e.result()
    e.s2(QO, 1)
    e.end_result()
    e.s3(QO, 3)
    e.close()
    e.zt(QO, 3)
    e.s3(FC1, 0)
    e.b3(FC1)
    e.zt(FC1, 1)
    e.open(SCOPE_S)
    e.back_begin()
    e.back_second()
    e.back_third()
    e.s3(QO, 2)
    e.bf(QO)
    e.zt(QO, 2)
    e.s2(QO, 0)
    e.zf(FC1)
    e.b4(FC1)
    e.s3(QO, 1)
    e.zt(QO, 1)
    e.back_fourth()
    e.spread()
    e.b3(QO)
    e.out_fc1()
    e.back_last()
    e.sent(FC1)
    e.end_full()
    e.s3(QO, 0)
    e.end_spread()
    e.end_fc1()
    e.zf(QO)
    e.b4(QO)
    e.end_ada()
    e.close()
    e.sent(QO)
    e.out_qo()
    e.end_qo()
    e.close()
    return e.steps


def block(events, args):
    V, A = pl.BlockSpec(memory_space=pltpu.VMEM), pl.BlockSpec(memory_space=pl.ANY)
    outs = {**OUT_V, **OUT_A}
    got = pl.pallas_call(
        functools.partial(block_kernel, events),
        out_shape=[jax.ShapeDtypeStruct(s, d) for s, d in outs.values()],
        in_specs=[V] * len(INS_V) + [A] * len(INS_A),
        out_specs=[V] * len(OUT_V) + [A] * len(OUT_A),
        scratch_shapes=[pltpu.VMEM(s, d) for s, d in STAGE.values()] + [pltpu.SemaphoreType.DMA(s) for s in SIGNALS.values()]
        + Conditions.scratch() + Back.scratch() + Scatter.scratch() + Gather.scratch(),
        compiler_params=pltpu.CompilerParams(collective_id=0, has_side_effects=True, vmem_limit_bytes=62 * 2**20),
        name="block",
    )(*args)
    return dict(zip(outs, got, strict=True))


FINAL_A = dict(result=((TOK, D), B16), gfull=((SEQ, D), F32), gmasked=((SEQ, D), F32), gw_ada=((288, 864), F32))
FINAL_V = dict(gw_qkv=(2, 144, 432), gw_out=(2, 144, 144), gw_fc1=(2, 144, 576), gw_fc2=(144, D))


def final_kernel(result, gfull, gmasked, gw_ada, *refs):
    blocks, refs = refs[:4], refs[4:]
    small, refs = refs[:8], refs[8:]
    outs, sem = refs[:-1], refs[-1]
    moves = ((cut(result, 0, SEQ), outs[0].at[0]), (cut(result, SEQ, KEEP), outs[1].at[0]), (gfull, outs[2].at[0]), (gmasked, outs[3].at[0]), (gw_ada, outs[4]))
    copies = [pltpu.make_async_copy(src, dst, sem.at[n]) for n, (src, dst) in enumerate(moves)]
    for c in copies:
        c.start()
    for n, (src, dst) in enumerate(zip(blocks, outs[5:9], strict=True)):
        y = src[...].astype(F32)
        dst[...] = y.reshape(288, 144).T if n == 1 else y
    for src, dst in zip(small, outs[9:], strict=True):
        dst[...] = src[...].reshape(dst.shape)
    for c in copies:
        c.wait()


def whole(full_input, masked_input, keep_index, cond_full, cond_masked, w_ada, b_ada, w_qkv, b_q, b_v, w_out, b_out, w_fc1, b_fc1, w_fc2, b_fc2, cot_full, cot_masked):
    g = block(block_events(), (keep_index, cond_full, cond_masked, w_ada, b_ada, b_q, b_v, b_out, b_fc1, b_fc2, w_qkv, w_out.T, w_fc1, w_fc2.T, full_input, masked_input, cot_full, cot_masked))
    V, A = pl.BlockSpec(memory_space=pltpu.VMEM), pl.BlockSpec(memory_space=pl.ANY)
    shapes = [((1, SEQ, D), B16), ((1, KEEP, D), B16), ((1, SEQ, D), F32), ((1, SEQ, D), F32), ((288, 864), F32)]
    shapes += [((144, 288) if n == 1 else s, F32) for n, s in enumerate(FINAL_V.values())]
    shapes += [((1, D), F32)] * 2 + [(s, F32) for s in ((864,), (144,), (144,), (144,), (576,), (144,))]
    out = pl.pallas_call(
        final_kernel,
        out_shape=[jax.ShapeDtypeStruct(s, d) for s, d in shapes],
        in_specs=[V] * 16,
        out_specs=[A] * 5 + [V] * (len(shapes) - 5),
        scratch_shapes=[pltpu.SemaphoreType.DMA((5,))],
        name="results",
    )(*[g[n] for n in FINAL_A], *[g[n] for n in FINAL_V], *[g[n] for n in OUT_V])
    out_full, out_masked, gfull, gmasked, gw_ada, gw_qkv, gw_out, gw_fc1, gw_fc2, gc_full, gc_masked, gb_ada, gb_q, gb_v, gb_out, gb_fc1, gb_fc2 = out
    return (
        out_full, out_masked, gfull, gmasked, gc_full, gc_masked, gw_ada, gb_ada, gw_qkv.reshape(288, 432), gb_q, gb_v, gw_out.T, gb_out,
        gw_fc1.reshape(288, 576), gb_fc1, gw_fc2.T, gb_fc2,
    )


def plain_layer_stats(values):
    centered = values - jnp.mean(values, axis=-1, keepdims=True)
    inverse = lax.rsqrt(jnp.mean(centered * centered, axis=-1, keepdims=True) + 1e-06)
    return (centered * inverse, inverse)


def plain_layer_back(upstream, normed, inverse):
    return inverse * (
        upstream
        - jnp.mean(upstream, axis=-1, keepdims=True)
        - normed * jnp.mean(upstream * normed, axis=-1, keepdims=True)
    )


def plain_gelu_tanh(values):
    return jax.nn.gelu(values, approximate=True)


def plain_expand_mods(piece, full_length, kept_length):
    head_part = jnp.broadcast_to(piece[:, 0:1], (piece.shape[0], full_length, piece.shape[2]))
    tail_part = jnp.broadcast_to(piece[:, 1:2], (piece.shape[0], kept_length, piece.shape[2]))
    return jnp.concatenate([head_part, tail_part], axis=1)


def plain_image_sums(values, full_length):
    return jnp.stack(
        [jnp.sum(values[:, :full_length], axis=1), jnp.sum(values[:, full_length:], axis=1)], axis=1
    )


def plain_forward_pass(tokens, mods, weights, biases, full_length):
    images, length, features = tokens.shape
    head_count = features // HEAD_DIM
    pieces = [
        plain_expand_mods(
            mods[:, :, column * features : (column + 1) * features],
            full_length,
            length - full_length,
        )
        for column in range(6)
    ]
    norm_one, inverse_one = plain_layer_stats(tokens)
    hidden_one = (norm_one * (1.0 + pieces[1]) + pieces[0]).astype(jnp.bfloat16)
    bias_all = jnp.concatenate([biases[1], jnp.zeros((features,), jnp.bfloat16), biases[2]]).astype(
        jnp.float32
    )
    projected = (
        jnp.einsum("itd,de->ite", hidden_one, weights[1], preferred_element_type=jnp.float32)
        + bias_all
    )
    projected = projected.astype(jnp.bfloat16).reshape(images, length, 3, head_count, HEAD_DIM)
    query_rows = projected[:, :, 0]
    key_rows = projected[:, :, 1]
    value_rows = projected[:, :, 2]
    scale_factor = 1.0 / math.sqrt(HEAD_DIM)
    scores = (
        jnp.einsum("iqhc,ikhc->ihqk", query_rows, key_rows, preferred_element_type=jnp.float32)
        * scale_factor
    )
    marker = jnp.arange(length) >= full_length
    same_image = marker[:, None] == marker[None, :]
    scores = jnp.where(same_image, scores, -1e30)
    row_max = jnp.max(scores, axis=-1, keepdims=True)
    exponent = jnp.exp(scores - row_max)
    attention = exponent / jnp.sum(exponent, axis=-1, keepdims=True)
    attention_low = attention.astype(jnp.bfloat16)
    mixed = jnp.einsum(
        "ihqk,ikhc->iqhc", attention_low, value_rows, preferred_element_type=jnp.float32
    )
    mixed = mixed.astype(jnp.bfloat16).reshape(images, length, features)
    attn_out = jnp.einsum(
        "itd,de->ite", mixed, weights[2], preferred_element_type=jnp.float32
    ) + biases[3].astype(jnp.float32)
    residual = tokens + pieces[2] * attn_out
    norm_two, inverse_two = plain_layer_stats(residual)
    hidden_two = (norm_two * (1.0 + pieces[4]) + pieces[3]).astype(jnp.bfloat16)
    upper = jnp.einsum(
        "itd,df->itf", hidden_two, weights[3], preferred_element_type=jnp.float32
    ) + biases[4].astype(jnp.float32)
    activated = plain_gelu_tanh(upper).astype(jnp.bfloat16)
    branch = jnp.einsum(
        "itf,fd->itd", activated, weights[4], preferred_element_type=jnp.float32
    ) + biases[5].astype(jnp.float32)
    result = residual + pieces[5] * branch
    return (
        result,
        pieces,
        norm_one,
        inverse_one,
        hidden_one,
        query_rows,
        key_rows,
        value_rows,
        attention,
        attention_low,
        mixed,
        attn_out,
        norm_two,
        inverse_two,
        hidden_two,
        upper,
        activated,
        branch,
    )


def general(
    full_input,
    masked_input,
    keep_index,
    cond_full,
    cond_masked,
    w_ada,
    b_ada,
    w_qkv,
    b_q,
    b_v,
    w_out,
    b_out,
    w_fc1,
    b_fc1,
    w_fc2,
    b_fc2,
    cot_full,
    cot_masked,
):
    def columns(shard):
        return lax.all_gather(lax.all_gather(shard, ROWS, axis=0, tiled=True), COLS, axis=1, tiled=True)

    weights = (None, columns(w_qkv), columns(w_out), columns(w_fc1), columns(w_fc2))
    widths = [b.shape[0] for b in (b_q, b_v, b_out, b_fc1, b_fc2)]
    packed = lax.all_gather(jnp.concatenate([b_q, b_v, b_out, b_fc1, b_fc2]), COLS, axis=0, tiled=False)
    biases, at = [None], 0
    for width in widths:
        biases.append(packed[:, at : at + width].reshape(-1))
        at += width
    full_length = full_input.shape[1]
    images = full_input.shape[0]
    features = full_input.shape[2]
    picked = jnp.take_along_axis(masked_input, keep_index[:, :, None], axis=1)
    tokens = jnp.concatenate([full_input, picked], axis=1).astype(jnp.float32)
    conds = jnp.stack([cond_full, cond_masked], axis=1).astype(jnp.float32)
    silu_low = jax.nn.silu(conds).astype(jnp.bfloat16)
    n_dp, n_fsdp = lax.axis_size(ROWS), lax.axis_size(COLS)
    rows_ada, cols_ada = w_ada.shape
    every_silu = lax.all_gather(silu_low, (ROWS, COLS), axis=0, tiled=True)
    my_silu = lax.dynamic_slice_in_dim(every_silu, lax.axis_index(ROWS) * rows_ada, rows_ada, axis=2)
    part = jnp.einsum("ijd,de->ije", my_silu, w_ada, preferred_element_type=jnp.float32)
    part = lax.psum_scatter(part, ROWS, scatter_dimension=0, tiled=True)
    part = part + b_ada.astype(jnp.float32)
    mods = lax.all_to_all(part, COLS, split_axis=0, concat_axis=2, tiled=True)
    (
        result,
        pieces,
        norm_one,
        inverse_one,
        hidden_one,
        query_rows,
        key_rows,
        value_rows,
        attention,
        attention_low,
        mixed,
        attn_out,
        norm_two,
        inverse_two,
        hidden_two,
        upper,
        activated,
        branch,
    ) = plain_forward_pass(tokens, mods, weights, biases, full_length)
    length = tokens.shape[1]
    head_count = features // HEAD_DIM
    scale_factor = 1.0 / math.sqrt(HEAD_DIM)
    grad_result = jnp.concatenate([cot_full, cot_masked], axis=1).astype(jnp.float32)
    grad_gate_two = plain_image_sums(grad_result * branch, full_length)
    grad_branch = (pieces[5] * grad_result).astype(jnp.bfloat16)
    grad_b_fc2 = jnp.sum(grad_branch.astype(jnp.float32), axis=(0, 1))
    grad_w_fc2 = jnp.einsum(
        "itf,itd->fd", activated, grad_branch, preferred_element_type=jnp.float32
    )
    grad_act = jnp.einsum(
        "itd,fd->itf", grad_branch, weights[4], preferred_element_type=jnp.float32
    )
    grad_upper = jax.vjp(plain_gelu_tanh, upper)[1](grad_act)[0].astype(jnp.bfloat16)
    grad_b_fc1 = jnp.sum(grad_upper.astype(jnp.float32), axis=(0, 1))
    grad_w_fc1 = jnp.einsum(
        "itd,itf->df", hidden_two, grad_upper, preferred_element_type=jnp.float32
    )
    grad_hidden_two = jnp.einsum(
        "itf,df->itd", grad_upper, weights[3], preferred_element_type=jnp.float32
    )
    grad_scale_two = plain_image_sums(grad_hidden_two * norm_two, full_length)
    grad_shift_two = plain_image_sums(grad_hidden_two, full_length)
    grad_residual = grad_result + plain_layer_back(
        grad_hidden_two * (1.0 + pieces[4]), norm_two, inverse_two
    )
    grad_gate_one = plain_image_sums(grad_residual * attn_out, full_length)
    grad_attn = (pieces[2] * grad_residual).astype(jnp.bfloat16)
    grad_b_out = jnp.sum(grad_attn.astype(jnp.float32), axis=(0, 1))
    grad_w_out = jnp.einsum("itd,ite->de", mixed, grad_attn, preferred_element_type=jnp.float32)
    grad_mixed = jnp.einsum(
        "ite,de->itd", grad_attn, weights[2], preferred_element_type=jnp.float32
    )
    grad_mixed = grad_mixed.astype(jnp.bfloat16).reshape(images, length, head_count, HEAD_DIM)
    grad_attention = jnp.einsum(
        "iqhc,ikhc->ihqk", grad_mixed, value_rows, preferred_element_type=jnp.float32
    )
    grad_values = jnp.einsum(
        "ihqk,iqhc->ikhc", attention_low, grad_mixed, preferred_element_type=jnp.float32
    )
    grad_scores = attention * (
        grad_attention - jnp.sum(attention * grad_attention, axis=-1, keepdims=True)
    )
    grad_scores = grad_scores.astype(jnp.bfloat16)
    grad_queries = (
        jnp.einsum("ihqk,ikhc->iqhc", grad_scores, key_rows, preferred_element_type=jnp.float32)
        * scale_factor
    )
    grad_keys = (
        jnp.einsum("ihqk,iqhc->ikhc", grad_scores, query_rows, preferred_element_type=jnp.float32)
        * scale_factor
    )
    grad_projected = jnp.stack([grad_queries, grad_keys, grad_values], axis=2)
    grad_projected = grad_projected.reshape(images, length, 3 * features).astype(jnp.bfloat16)
    grad_b_q = jnp.sum(grad_projected[:, :, :features].astype(jnp.float32), axis=(0, 1))
    grad_b_v = jnp.sum(grad_projected[:, :, 2 * features :].astype(jnp.float32), axis=(0, 1))
    grad_w_qkv = jnp.einsum(
        "itd,ite->de", hidden_one, grad_projected, preferred_element_type=jnp.float32
    )
    grad_hidden_one = jnp.einsum(
        "ite,de->itd", grad_projected, weights[1], preferred_element_type=jnp.float32
    )
    grad_scale_one = plain_image_sums(grad_hidden_one * norm_one, full_length)
    grad_shift_one = plain_image_sums(grad_hidden_one, full_length)
    grad_tokens = grad_residual + plain_layer_back(
        grad_hidden_one * (1.0 + pieces[1]), norm_one, inverse_one
    )
    grad_mods = jnp.concatenate(
        [
            grad_shift_one,
            grad_scale_one,
            grad_gate_one,
            grad_shift_two,
            grad_scale_two,
            grad_gate_two,
        ],
        axis=-1,
    ).astype(jnp.bfloat16)
    cut = grad_mods.reshape(images, 2, n_fsdp, cols_ada)
    mine = lax.all_to_all(cut, COLS, split_axis=2, concat_axis=0, tiled=False)
    mine = lax.all_gather(mine.reshape(n_fsdp * images, 2, cols_ada), ROWS, axis=0, tiled=True)
    grad_b_ada = jnp.sum(mine.astype(jnp.float32), axis=(0, 1))
    grad_w_ada = jnp.einsum("ijd,ije->de", my_silu, mine, preferred_element_type=jnp.float32)
    back = jnp.einsum("ije,de->ijd", mine, w_ada, preferred_element_type=jnp.float32)
    back = lax.psum_scatter(back.reshape(n_dp, n_fsdp * images, 2, rows_ada), COLS, scatter_dimension=1, tiled=True)
    grad_silu = lax.all_to_all(back, ROWS, split_axis=0, concat_axis=3, tiled=True).reshape(images, 2, features)
    grad_cond = jax.vjp(jax.nn.silu, conds)[1](grad_silu)[0]
    image_rows = jnp.arange(images)[:, None]
    grad_masked = (
        jnp.zeros((images, full_length, features), jnp.float32)
        .at[image_rows, keep_index]
        .set(grad_tokens[:, full_length:])
    )
    def owned(grad):
        inner = lax.psum_scatter(grad.astype(jnp.bfloat16), ROWS, scatter_dimension=0, tiled=True)
        return lax.psum_scatter(inner, COLS, scatter_dimension=1, tiled=True).astype(jnp.float32)

    matrices = (grad_w_ada, owned(grad_w_qkv), owned(grad_w_out), owned(grad_w_fc1), owned(grad_w_fc2))
    sums = (grad_b_q, grad_b_v, grad_b_out, grad_b_fc1, grad_b_fc2)
    line = jnp.concatenate([g.reshape(n_fsdp, -1) for g in sums], axis=1)
    line = lax.psum(lax.psum_scatter(line, COLS, scatter_dimension=0, tiled=True), ROWS)[0]
    vectors, at = [grad_b_ada], 0
    for width in widths:
        vectors.append(line[at : at + width])
        at += width
    return (
        result[:, :full_length].astype(jnp.bfloat16),
        result[:, full_length:].astype(jnp.bfloat16),
        grad_tokens[:, :full_length],
        grad_masked,
        grad_cond[:, 0],
        grad_cond[:, 1],
        matrices[0],
        vectors[0],
        matrices[1],
        vectors[1],
        vectors[2],
        matrices[2],
        vectors[3],
        matrices[3],
        vectors[4],
        matrices[4],
        vectors[5],
    )


def solution(mesh):
    special = dict(mesh.shape) == {ROWS: 4, COLS: 8}
    return jax.shard_map(
        whole if special else general,
        mesh=mesh,
        in_specs=(
            P((ROWS, COLS), None, None),
            P((ROWS, COLS), None, None),
            P((ROWS, COLS), None),
            P((ROWS, COLS), None),
            P((ROWS, COLS), None),
            P(ROWS, COLS),
            P(COLS),
            P(ROWS, COLS),
            P(COLS),
            P(COLS),
            P(ROWS, COLS),
            P(COLS),
            P(ROWS, COLS),
            P(COLS),
            P(ROWS, COLS),
            P(COLS),
            P((ROWS, COLS), None, None),
            P((ROWS, COLS), None, None),
        ),
        out_specs=(
            P((ROWS, COLS), None, None),
            P((ROWS, COLS), None, None),
            P((ROWS, COLS), None, None),
            P((ROWS, COLS), None, None),
            P((ROWS, COLS), None),
            P((ROWS, COLS), None),
            P(ROWS, COLS),
            P(COLS),
            P(ROWS, COLS),
            P(COLS),
            P(COLS),
            P(ROWS, COLS),
            P(COLS),
            P(ROWS, COLS),
            P(COLS),
            P(ROWS, COLS),
            P(COLS),
        ),
        check_vma=False,
    )
```

```python
import functools
import math
import jax
import jax.numpy as jnp
from jax import lax
from jax.experimental import pallas as pl
from jax.experimental.pallas import tpu as pltpu
from jax.sharding import PartitionSpec as P


MESH = pl.DeviceIdType.MESH
ROWS, COLS = "dp", "fsdp"
F32, B16 = jnp.float32, jnp.bfloat16
D, HEADS, HEAD_DIM, SEQ, KEEP, TOK = 1152, 16, 72, 256, 128, 384
SCALE = 1.0 / math.sqrt(HEAD_DIM)
GELU_A, GELU_B = math.sqrt(2.0 / math.pi), 0.044715
MATS = ((1152, True, 32), (1152, True, 32), (1152, False, 32))
QO, FC1, FC2 = range(3)


def nn(a, b):
    return lax.dot_general(a, b, (((1,), (0,)), ((), ())), preferred_element_type=F32)


def nt(a, b):
    return lax.dot_general(a, b, (((1,), (1,)), ((), ())), preferred_element_type=F32)


def tn(a, b):
    return lax.dot_general(a, b, (((0,), (0,)), ((), ())), preferred_element_type=F32)


class Script:
    def __init__(self):
        self.steps = []

    def __getattr__(self, name):
        return lambda *args: self.steps.append((name, args))


class Place:
    def __init__(self):
        self.dp = dp = lax.axis_index(ROWS)
        self.f = f = lax.axis_index(COLS)
        self.z, self.c = f // 2, f % 2
        self.xn = dp + 1 - 2 * (dp % 2)
        self.yn = (dp + 2) % 4
        self.dg = 3 - dp
        self.sf = f + 1 - 2 * self.c
        z = self.z
        self.middle = (z == 1) | (z == 2)
        low = z < 2
        self.order = (z, z + 1 - 2 * (z % 2), jnp.where(low, 2, 1), jnp.where(low, 3, 0))
        self.x_dev, self.y_dev, self.d_dev, self.s_dev = (self.xn, f), (self.yn, f), (self.dg, f), (dp, self.sf)
        self.rows = [(self.dp + k) % 4 for k in (1, 2, 3)]
        self.cols = [(self.f + k) % 8 for k in range(1, 8)]

    def barrier(self):
        sem = pltpu.get_barrier_semaphore()
        for dev in [(r, self.f) for r in self.rows] + [(self.dp, c) for c in self.cols]:
            pl.semaphore_signal(sem, inc=1, device_id=dev, device_id_type=MESH)
        pl.semaphore_wait(sem, 10)


def remote(src, dst, send, recv, dev):
    return pltpu.make_async_remote_copy(src_ref=src, dst_ref=dst, send_sem=send, recv_sem=recv, device_id=dev, device_id_type=MESH)


def cut(ref, lo, n):
    return ref.at[pl.ds(lo, n)]


class Gather:
    SEMS = dict(rz=(4, 4), rx=(4, 4), ry=(4, 4), rd=(4, 4, 2), rs=(4, 4), so=(4, 2), sf=(4, 4), sx=(4, 4), sy=(4, 4), sd=(4, 4, 2),
                ss=(4, 4), loc=(4,), bx=(4,), by=(4,), bd=(4, 2), bz=(4, 4), cx=(4,), cy=(4,), cd=(4, 2), co=(4, 2), cf=(4, 4))

    def __init__(self, p, bufs, blks, sems):
        self.p, self.bufs, self.blks = p, bufs, blks
        for name, sem in zip(self.SEMS, sems, strict=True):
            setattr(self, name, sem)

    @classmethod
    def scratch(cls):
        return [pltpu.SemaphoreType.DMA(s) for s in cls.SEMS.values()]

    def a(self, m):
        return 144 - MATS[m][2]

    def split(self, m, j):
        a = self.a(m)
        h = (a // 32) * 16
        return (a - h, h) if j % 2 == 0 else (h, a - h)

    def slot(self, m, dp, zs):
        t = self.bufs[m]
        return t.at[zs, dp, self.p.c] if MATS[m][1] else t.at[dp, zs, self.p.c]

    def top(self, m, dp, zs):
        return cut(self.slot(m, dp, zs), 0, self.a(m))

    def low(self, m, dp, zs):
        return cut(self.slot(m, dp, zs), self.a(m), MATS[m][2])

    def low4(self, m, zs):
        t, rows = self.bufs[m], pl.ds(self.a(m), MATS[m][2])
        return t.at[zs, :, self.p.c, rows] if MATS[m][1] else t.at[:, zs, self.p.c, rows]

    def plane(self, m, zs, c):
        t = self.bufs[m]
        return t.at[zs, :, c] if MATS[m][1] else t.at[:, zs, c]

    def z_copies(self, m):
        p = self.p
        blk = cut(self.blks[m], 0, self.a(m))
        dst = self.top(m, p.dp, p.z)
        up = remote(blk, dst, self.so.at[m, 0], self.rz.at[m, p.z], (p.dp, p.f + 2))
        down = remote(blk, dst, self.so.at[m, 1], self.rz.at[m, p.z], (p.dp, p.f - 2))
        return up, down

    def bz_copies(self, m):
        p = self.p
        src = self.low4(m, p.z)
        up = remote(src, src, self.co.at[m, 0], self.bz.at[m, p.z], (p.dp, p.f + 2))
        down = remote(src, src, self.co.at[m, 1], self.bz.at[m, p.z], (p.dp, p.f - 2))
        return up, down

    def pass_on(self, m, zs):
        p = self.p
        src = self.top(m, p.dp, zs)
        return remote(src, src, self.sf.at[m, zs], self.rz.at[m, zs], (p.dp, p.f + jnp.where(zs < p.z, 2, -2)))

    def pass_low(self, m, zs):
        p = self.p
        src = self.low4(m, zs)
        return remote(src, src, self.cf.at[m, zs], self.bz.at[m, zs], (p.dp, p.f + jnp.where(zs < p.z, 2, -2)))

    def x_copy(self, m, src, zs):
        return remote(src, self.top(m, self.p.dp, zs), self.sx.at[m, zs], self.rx.at[m, zs], self.p.x_dev)

    def y_copy(self, m, src, zs):
        return remote(src, self.top(m, self.p.dp, zs), self.sy.at[m, zs], self.ry.at[m, zs], self.p.y_dev)

    def d_copy(self, m, j, zs, half):
        p = self.p
        a, b = self.split(m, j)
        lo, n = ((0, a), (a, b))[half]
        src = cut(self.slot(m, p.xn if half == 0 else p.yn, zs), lo, n)
        return remote(src, src, self.sd.at[m, zs, half], self.rd.at[m, zs, half], p.y_dev if half == 0 else p.x_dev)

    def bd_copy(self, m, half):
        p = self.p
        h = 16 * ((MATS[m][2] // 16 + 1) // 2)
        lo, n = ((0, h), (h, MATS[m][2] - h))[half]
        src = cut(self.slot(m, p.xn if half == 0 else p.yn, p.z), self.a(m) + lo, n)
        return remote(src, src, self.cd.at[m, half], self.bd.at[m, half], p.y_dev if half == 0 else p.x_dev)

    def s_copy(self, m, zs):
        src = self.plane(m, zs, self.p.c)
        return remote(src, src, self.ss.at[m, zs], self.rs.at[m, zs], self.p.s_dev)

    def ends(self, copies, act):
        p = self.p

        @pl.when(p.z < 3)
        def _():
            act(copies[0])

        @pl.when(p.z > 0)
        def _():
            act(copies[1])

    def got(self, ref, recv):
        remote(ref, ref, self.so.at[0, 0], recv, self.p.x_dev).wait_recv()

    def own(self, m):
        p = self.p
        self.ends(self.z_copies(m), lambda c: c.start())
        blk = cut(self.blks[m], 0, self.a(m))
        self.x_copy(m, blk, p.z).start()
        self.y_copy(m, blk, p.z).start()
        if not MATS[m][2]:
            pltpu.make_async_copy(self.blks[m], self.slot(m, p.dp, p.z), self.loc.at[m]).start()

    def bown(self, m):
        p = self.p
        pltpu.make_async_copy(self.blks[m], self.slot(m, p.dp, p.z), self.loc.at[m]).start()
        blk = cut(self.blks[m], self.a(m), MATS[m][2])
        dst = self.low(m, p.dp, p.z)
        remote(blk, dst, self.cx.at[m], self.bx.at[m], p.x_dev).start()
        remote(blk, dst, self.cy.at[m], self.by.at[m], p.y_dev).start()

    def arr(self, m, j):
        p = self.p
        zs = p.order[j]
        src = self.top(m, p.dp, zs)
        self.got(src, self.rz.at[m, zs])

        @pl.when(p.middle)
        def _():
            self.pass_on(m, zs).start()

        self.x_copy(m, src, zs).start()
        self.y_copy(m, src, zs).start()

    def cross(self, m, j):
        p = self.p
        zs = p.order[j]
        self.got(self.top(m, p.xn, zs), self.rx.at[m, zs])
        self.d_copy(m, j, zs, 0).start()
        self.got(self.top(m, p.yn, zs), self.ry.at[m, zs])
        self.d_copy(m, j, zs, 1).start()

    def bcross(self, m):
        p = self.p
        self.got(self.low(m, p.xn, p.z), self.bx.at[m])
        self.bd_copy(m, 0).start()
        self.got(self.low(m, p.yn, p.z), self.by.at[m])
        self.bd_copy(m, 1).start()

    def bz_(self, m):
        p = self.p
        h = 16 * ((MATS[m][2] // 16 + 1) // 2)
        for half, (lo, n) in enumerate(((0, h), (h, MATS[m][2] - h))):
            self.got(cut(self.slot(m, p.dg, p.z), self.a(m) + lo, n), self.bd.at[m, half])
        pltpu.make_async_copy(self.blks[m], self.slot(m, p.dp, p.z), self.loc.at[m]).wait()
        self.ends(self.bz_copies(m), lambda c: c.start())

    def barr(self, m, j):
        zs = self.p.order[j]
        self.got(self.low4(m, zs), self.bz.at[m, zs])

        @pl.when(self.p.middle)
        def _():
            self.pass_low(m, zs).start()

    def fin(self, m, j):
        p = self.p
        zs = p.order[j]
        a, b = self.split(m, j)
        for half, (lo, n) in enumerate(((0, a), (a, b))):
            self.got(cut(self.slot(m, p.dg, zs), lo, n), self.rd.at[m, zs, half])
        if j == 0 and not MATS[m][2]:
            pltpu.make_async_copy(self.blks[m], self.slot(m, p.dp, p.z), self.loc.at[m]).wait()
        self.s_copy(m, zs).start()

    def have(self, m):
        for j in range(4):
            zs = self.p.order[j]
            self.got(self.plane(m, zs, 1 - self.p.c), self.rs.at[m, zs])

    def drain(self):
        p = self.p
        for m in range(3):
            blk = cut(self.blks[m], 0, self.a(m))
            self.ends(self.z_copies(m), lambda c: c.wait_send())
            if MATS[m][2]:
                low = cut(self.blks[m], self.a(m), MATS[m][2])
                dst = self.low(m, p.dp, p.z)
                remote(low, dst, self.cx.at[m], self.bx.at[m], p.x_dev).wait_send()
                remote(low, dst, self.cy.at[m], self.by.at[m], p.y_dev).wait_send()
                self.bd_copy(m, 0).wait_send()
                self.bd_copy(m, 1).wait_send()
                self.ends(self.bz_copies(m), lambda c: c.wait_send())
            for j in range(4):
                zs = p.order[j]
                src = self.top(m, p.dp, zs)
                if j:

                    @pl.when(p.middle)
                    def _(m=m, zs=zs):
                        self.pass_on(m, zs).wait_send()
                        if MATS[m][2]:
                            self.pass_low(m, zs).wait_send()

                self.x_copy(m, src, zs).wait_send()
                self.y_copy(m, src, zs).wait_send()
                self.d_copy(m, j, zs, 0).wait_send()
                self.d_copy(m, j, zs, 1).wait_send()
                self.s_copy(m, zs).wait_send()


def stage(p, shard, got, send, recv):
    rows = shard.shape[0] // 2
    return remote(cut(shard, (1 - p.c) * rows, rows), got, send, recv, p.s_dev)


def join(p, shard, got, blk, at=0):
    rows, width = got.shape
    own = shard[pl.ds(pl.multiple_of(p.c * rows, 16), rows), :]
    other = got[...]
    first = p.c == 0
    blk[:, at : at + width] = jnp.where(first, own, other)
    blk[:, at + width : at + 2 * width] = jnp.where(first, other, own)


class Conditions:
    SEMS = dict(r1=(4,), s1=(4,), r2=(8,), s2=(8,), rb=(8,), sb=(8,), r3=(4,), s3=(4,), r4=(8,), s4=(8,))
    SHAPES = dict(sil4=(4, 2, 288), in1=(4, 2, 288), row8=(8, 288), in2=(8, 8, 288), pack=(1, D), inb=(8, 1, D), p3=(4, 16, 864),
                  in3=(4, 16, 864), m8=(8, 2, 864), in4=(8, 2, 864), mods=(6, 2, 1, D), bias=(8, 1, D), wide=(4, 1, D), qkvb=(4, 1, 864))

    @classmethod
    def scratch(cls):
        return [pltpu.VMEM(s, F32) for s in cls.SHAPES.values()] + [pltpu.SemaphoreType.DMA(s) for s in cls.SEMS.values()]

    def __init__(self, p, conds, w_ada, b_ada, biases, scratch):
        self.p, self.conds, self.w_ada, self.b_ada, self.biases = p, conds, w_ada, b_ada, biases
        for name, ref in zip(list(self.SHAPES) + list(self.SEMS), scratch, strict=True):
            setattr(self, name, ref)

    def over_dp(self, src_of, land, sem_s, sem_r):
        p = self.p
        return [remote(src_of(r), land.at[p.dp], sem_s.at[r], sem_r.at[p.dp], (r, p.f)) for r in p.rows]

    def over_f(self, src_of, land, sem_s, sem_r):
        p = self.p
        return [remote(src_of(c), land.at[p.f], sem_s.at[c], sem_r.at[p.f], (p.dp, c)) for c in p.cols]

    def copies(self, step):
        return {
            1: lambda: self.over_dp(lambda r: self.sil4.at[r], self.in1, self.s1, self.r1),
            2: lambda: self.over_f(lambda c: self.row8, self.in2, self.s2, self.r2),
            "b": lambda: self.over_f(lambda c: self.pack, self.inb, self.sb, self.rb),
            3: lambda: self.over_dp(lambda r: self.p3.at[r], self.in3, self.s3, self.r3),
            4: lambda: self.over_f(lambda c: self.m8.at[c], self.in4, self.s4, self.r4),
        }[step]()

    def send(self, step):
        for c in self.copies(step):
            c.start()

    def arrived(self, land, sem, peers):
        for q in peers:
            remote(land.at[q], land.at[q], self.s1.at[0], sem.at[q], self.p.x_dev).wait_recv()

    def begin(self):
        p = self.p
        at = 0
        for b in self.biases:
            n = b.shape[0]
            self.pack[:, at : at + n] = b[...].reshape(1, n).astype(F32)
            at += n
        self.send("b")
        self.inb[p.f] = self.pack[...]
        for s, cond in enumerate(self.conds):
            x = cond[...].astype(F32)
            y = (x / (1.0 + jnp.exp(-x))).astype(B16).astype(F32)
            for d in range(4):
                self.sil4[d, s : s + 1, :] = y[:, 288 * d : 288 * d + 288]
        self.send(1)
        self.in1[p.dp] = self.sil4[p.dp]

    def second(self):
        p = self.p
        self.arrived(self.in1, self.r1, p.rows)
        for d in range(4):
            self.row8[2 * d : 2 * d + 2, :] = self.in1[d]
        self.send(2)
        self.in2[p.f] = self.row8[...]

    def third(self):
        p = self.p
        self.arrived(self.in2, self.r2, p.cols)
        rows = self.in2[...].reshape(64, 288).astype(B16)
        part = nn(rows, self.w_ada[...])
        for d in range(4):
            for f in range(8):
                self.p3[d, 2 * f : 2 * f + 2, :] = part[8 * f + 2 * d : 8 * f + 2 * d + 2]
        self.send(3)
        self.in3[p.dp] = self.p3[p.dp]

    def fourth(self):
        p = self.p
        self.arrived(self.in3, self.r3, p.rows)
        total = self.in3[0] + self.in3[1] + self.in3[2] + self.in3[3] + self.b_ada[...].reshape(1, 864).astype(F32)
        for f in range(8):
            self.m8[f] = total[2 * f : 2 * f + 2]
        self.send(4)
        self.in4[p.f] = self.m8[p.f]

    def last(self):
        p = self.p
        self.arrived(self.in4, self.r4, p.cols)
        self.arrived(self.inb, self.rb, p.cols)
        for f in range(8):
            rows = self.in4[f]
            at = 864 * f
            while at < 864 * (f + 1):
                b = at // D
                end = min(864 * (f + 1), D * (b + 1))
                for s in range(2):
                    self.mods[b, s, :, at - D * b : end - D * b] = rows[s : s + 1, at - 864 * f : end - 864 * f]
                at = end
        for f in range(8):
            row = self.inb[f]
            for i, lo in enumerate((0, 144, 288, 1008)):
                self.bias[i, :, 144 * f : 144 * f + 144] = row[:, lo : lo + 144]
            half = 576 * (f % 2)
            self.wide[f // 2, :, half : half + 576] = row[:, 432:1008]
        line = jnp.concatenate([self.bias[0], jnp.zeros((1, D), F32), self.bias[1]], axis=1)
        for k in range(4):
            self.qkvb[k] = line[:, 864 * k : 864 * k + 864]

    def drain(self):
        for step in (1, 2, "b", 3, 4):
            for c in self.copies(step):
                c.wait_send()


def layer_stats(x):
    mean = jnp.mean(x, axis=-1, keepdims=True)
    centered = x - mean
    inv = lax.rsqrt(jnp.mean(centered * centered, axis=-1, keepdims=True) + 1e-6)
    return centered * inv, inv


def by_rows(body):
    def step(i, carry):
        body(pl.ds(pl.multiple_of(i * 128, 128), 128), i // 2)
        return carry

    lax.fori_loop(0, 3, step, 0)


def transpose_into(src, dst):
    for i in range(3):
        for k in range(9):
            t = src[128 * i : 128 * i + 128, 128 * k : 128 * k + 128].astype(F32).T.astype(B16)
            at = 128 * k
            while at < 128 * (k + 1):
                b = at // 144
                end = min(128 * (k + 1), 144 * (b + 1))
                dst[b, at - 144 * b : end - 144 * b, 128 * i : 128 * i + 128] = t[at - 128 * k : end - 128 * k]
                at = end


def pair_rows(p, mine, land, send, recv, loc):
    to_sib = [remote(mine.at[2 * k + (1 - p.c)], land.at[k, :, pl.ds(384, 384)], send.at[k], recv.at[k], p.s_dev) for k in range(4)]
    to_own = [pltpu.make_async_copy(mine.at[2 * k + p.c], land.at[k, :, pl.ds(0, 384)], loc.at[k]) for k in range(4)]
    return to_sib + to_own


class Bag:
    pass


def forward_steps(p, i, o, v, con):
    saves = []

    def save(pair):
        n = len(saves)
        saves.append(lambda: pltpu.make_async_copy(*pair(), v.ow.at[n]))
        saves[n]().start()

    waits = []

    def pairs(k, mine, land):
        waits.append(lambda: pair_rows(p, mine(), land, v.pt.at[k], v.pr.at[k], v.pl_.at[k]))
        for c in waits[-1]():
            c.start()

    loads = {}

    def load(name, k, slot, src, dst, sem):
        c = pltpu.make_async_copy(src, dst, sem)
        c.start()
        loads[name, k] = c

    def get_tokens():
        for n, (key, src, dst) in enumerate((("full", i.full, cut(v.tok, 0, SEQ)), ("masked", i.masked, v.masked), ("cot0", i.cot_full, cut(v.cot, 0, SEQ)), ("cot1", i.cot_masked, cut(v.cot, SEQ, KEEP)))):
            loads[key] = pltpu.make_async_copy(src.at[0], dst, v.lt.at[n])
            loads[key].start()

    def tokens():
        for key in ("full", "masked", "cot0", "cot1"):
            loads[key].wait()
        spread = (lax.broadcasted_iota(jnp.int32, (SEQ, KEEP), 0) == i.keep[...]).astype(B16)
        v.tok[SEQ:TOK] = tn(spread, v.masked[...]).astype(B16)
        save(lambda: (v.tok, o.tok))

    def norm1():
        def body(r, s):
            n, _ = layer_stats(v.tok[r, :].astype(F32))
            v.hid[r, :] = (n * (1.0 + con.mods[1, s]) + con.mods[0, s]).astype(B16)

        by_rows(body)

    def grads_in():
        v.gb[0:SEQ] = (con.mods[5, 0] * v.cot[0:SEQ].astype(F32)).astype(B16)
        v.gb[SEQ:TOK] = (con.mods[5, 1] * v.cot[SEQ:TOK].astype(F32)).astype(B16)
        save(lambda: (v.gb, o.gb))
        transpose_into(v.gb, v.gbt)
        pairs(0, lambda: v.gbt, o.gbp)

    def turn1():
        transpose_into(v.hid, v.h1t)
        pairs(1, lambda: v.h1t, o.h1p)

    def load_q(k):
        load("q", k, k % 2, o.t0.at[k], v.wq.at[k % 2], v.lq.at[k % 2])

    def qkv(k):
        loads["q", k].wait()
        y = (nn(v.hid[...], v.wq[k % 2, :, :, :, 0:864].reshape(D, 864)) + con.qkvb[k]).astype(B16)
        for h in range(12):
            v.qkv[12 * k + h] = y[:, 72 * h : 72 * h + 72]
        if k + 2 < 4:
            load_q(k + 2)
        if k == 3:
            pltpu.make_async_copy(v.qkv, o.qkv, v.oq.at[0]).start()

    def end_qkv():
        pltpu.make_async_copy(v.qkv, o.qkv, v.oq.at[0]).wait()

    def f_end():
        for s in saves:
            s().wait()
        for w in waits:
            for c in w():
                c.wait()

    def heads(k, n):
        def step(g, carry):
            parts = [(4 * g + u, lo, hi) for u in range(4) for lo, hi in ((0, SEQ), (SEQ, TOK))]
            scores = [nt(v.qkv[h, lo:hi], v.qkv[16 + h, lo:hi]) * SCALE for h, lo, hi in parts]
            exps = [jnp.exp(x - jnp.max(x, axis=-1, keepdims=True)) for x in scores]
            probs = [(e * (1.0 / jnp.sum(e, axis=-1, keepdims=True))).astype(B16) for e in exps]
            for (h, lo, hi), pr in zip(parts, probs):
                v.mixh[h, lo:hi] = nn(pr, v.qkv[32 + h, lo:hi]).astype(B16)
            return carry

        lax.fori_loop(k // 4, (k + n) // 4, step, 0)

    def mix():
        for h in range(HEADS):
            v.mixed[:, 72 * h : 72 * h + 72] = v.mixh[h]
        transpose_into(v.mixed, v.mxt)
        pairs(3, lambda: v.mxt, o.mxp)

    def load_o():
        for k in range(4):
            load("o", k, k, o.t0.at[k, :, :, :, pl.ds(768, 384)], v.wo.at[k], v.lo.at[k])

    def attend():
        for k in range(4):
            loads["o", k].wait()
            cols = slice(288 * k, 288 * k + 288)
            v.attn[:, cols] = nn(v.mixed[...], v.wo[k, :, :, :, 96:384].reshape(D, 288)) + con.bias[2, :, cols]

        def body(r, s):
            resid = v.tok[r, :].astype(F32) + con.mods[2, s] * v.attn[r, :]
            n, _ = layer_stats(resid)
            v.hid2[r, :] = (n * (1.0 + con.mods[4, s]) + con.mods[3, s]).astype(B16)

        by_rows(body)
        save(lambda: (v.attn, o.attn))

    def turn2():
        transpose_into(v.hid2, v.h2t)
        pairs(2, lambda: v.h2t, o.h2p)

    def load_1(k):
        load("1", k, k % 2, o.t2.at[k], v.w1.at[k % 2], v.l1.at[k % 2])

    def fc1(k):
        loads["1", k].wait()

        def tile(t, carry):
            lanes = pl.ds(pl.multiple_of(t * 384, 128), 384)
            u = nn(v.hid2[...], v.w1[k % 2, :, :, :, lanes].reshape(D, 384)) + con.wide[k, :, lanes]
            w = u * u
            th = jnp.tanh(GELU_A * u * (1.0 + GELU_B * w))
            v.act[k, :, lanes] = (0.5 * u * (1.0 + th)).astype(B16)
            v.dact[k, :, lanes] = (0.5 * (1.0 + th) + 0.5 * u * (1.0 - th * th) * (GELU_A * (1.0 + 3.0 * GELU_B * w))).astype(B16)
            return carry

        lax.fori_loop(0, 3, tile, 0)
        if k + 2 < 4:
            load_1(k + 2)
        save(lambda: (v.act.at[k], o.act.at[k, pl.ds(0, TOK)]))
        save(lambda: (v.dact.at[k], o.dact.at[k]))
        waits.append(lambda: [remote(v.act.at[k], o.act.at[k, pl.ds(TOK, TOK)], v.as_.at[k], v.ar.at[k], p.s_dev)])
        waits[-1]()[0].start()

    return dict(get_tokens=get_tokens, tokens=tokens, norm1=norm1, grads_in=grads_in, turn1=turn1, load_q=load_q, qkv=qkv, heads=heads, mix=mix, load_o=load_o,
                attend=attend, turn2=turn2, load_1=load_1, fc1=fc1, end_qkv=end_qkv, f_end=f_end)


LANES = (1152, 1152, 1152)
B_ROWS = (32, 32, 32)


class Scatter:
    SEMS = dict(sd=(4, 4, 2), rd=(4, 4, 2), sx=(4, 4), rx=(4, 4), sy=(4, 4), ry=(4, 4), sz=(4, 4), rz=(4, 5),
                cz=(4, 4), bz=(4, 5), cd=(4, 2), bd=(4, 2), cx=(4,), bx=(4,), cy=(4,), by=(4,))

    @classmethod
    def scratch(cls):
        out = []
        for m in range(3):
            b, n = B_ROWS[m], LANES[m]
            a = 144 - b
            out += [pltpu.VMEM(s, B16) for s in ((4, a, n), (4, a, n), (4, a, n), (5, a, n))]
            if b:
                out += [pltpu.VMEM(s, B16) for s in ((5, 4, b, n), (b, n), (b, n), (b, n))]
        return out + [pltpu.SemaphoreType.DMA(s) for s in cls.SEMS.values()]

    @classmethod
    def count(cls):
        return sum(8 if b else 4 for b in B_ROWS) + len(cls.SEMS)

    def __init__(self, p, r, refs):
        self.p, self.r = p, r
        refs = list(refs)
        self.ld, self.lx, self.ly, self.lz = [], [], [], []
        self.lbz, self.lbx, self.lby, self.lbd = {}, {}, {}, {}
        for m in range(3):
            for part in (self.ld, self.lx, self.ly, self.lz):
                part.append(refs.pop(0))
            if B_ROWS[m]:
                for part in (self.lbz, self.lbx, self.lby, self.lbd):
                    part[m] = refs.pop(0)
        for name in self.SEMS:
            setattr(self, name, refs.pop(0))

    def blk(self, m, dp, zs, lo, n):
        return self.r[m].at[dp, zs, pl.ds(lo, n), pl.ds(0, LANES[m])]

    def a(self, m):
        return 144 - B_ROWS[m]

    def half(self, m, j):
        a = self.a(m)
        h = (a // 32) * 16
        return a - h if j % 2 == 0 else h

    def got(self, ref, sem):
        remote(ref, ref, self.sd.at[0, 0, 0], sem, self.p.x_dev).wait_recv()

    def add(self, dst, *lands):
        y = dst[...].astype(F32)
        for land in lands:
            y = y + land[...].astype(F32)
        dst[...] = y.astype(B16)

    def c1(self, m, j):
        p, zs, a, h = self.p, self.p.order[j], self.a(m), self.half(m, j)
        one = remote(self.blk(m, p.dg, zs, 0, h), self.ld[m].at[zs, pl.ds(0, h)], self.sd.at[m, zs, 0], self.rd.at[m, zs, 0], p.x_dev)
        two = remote(self.blk(m, p.dg, zs, h, a - h), self.ld[m].at[zs, pl.ds(h, a - h)], self.sd.at[m, zs, 1], self.rd.at[m, zs, 1], p.y_dev)
        return one, two

    def c2(self, m, j):
        p, zs, a = self.p, self.p.order[j], self.a(m)
        y = remote(self.blk(m, p.yn, zs, 0, a), self.ly[m].at[zs], self.sy.at[m, zs], self.ry.at[m, zs], p.y_dev)
        x = remote(self.blk(m, p.xn, zs, 0, a), self.lx[m].at[zs], self.sx.at[m, zs], self.rx.at[m, zs], p.x_dev)
        return y, x

    def cz_(self, m, j):
        p, zs, a = self.p, self.p.order[j], self.a(m)
        up = zs > p.z
        slot = jnp.where(up, zs, jnp.where(zs == p.z - 1, 4, zs))
        return remote(self.blk(m, p.dp, zs, 0, a), self.lz[m].at[slot], self.sz.at[m, zs], self.rz.at[m, slot], (p.dp, p.f + jnp.where(up, 2, -2)))

    def cb(self, m, j):
        p, zs, a, b = self.p, self.p.order[j], self.a(m), B_ROWS[m]
        up = zs > p.z
        slot = jnp.where(up, zs, jnp.where(zs == p.z - 1, 4, zs))
        src = self.r[m].at[:, zs, pl.ds(a, b), pl.ds(0, LANES[m])]
        return remote(src, self.lbz[m].at[slot], self.cz.at[m, zs], self.bz.at[m, slot], (p.dp, p.f + jnp.where(up, 2, -2)))

    def cb2(self, m):
        p, a, b = self.p, self.a(m), B_ROWS[m]
        h = 16 * ((b // 16 + 1) // 2)
        one = remote(self.blk(m, p.dg, p.z, a, h), self.lbd[m].at[pl.ds(0, h)], self.cd.at[m, 0], self.bd.at[m, 0], p.x_dev)
        two = remote(self.blk(m, p.dg, p.z, a + h, b - h), self.lbd[m].at[pl.ds(h, b - h)], self.cd.at[m, 1], self.bd.at[m, 1], p.y_dev)
        return one, two

    def cb3(self, m):
        p, a, b = self.p, self.a(m), B_ROWS[m]
        y = remote(self.blk(m, p.yn, p.z, a, b), self.lby[m], self.cy.at[m], self.by.at[m], p.y_dev)
        x = remote(self.blk(m, p.xn, p.z, a, b), self.lbx[m], self.cx.at[m], self.bx.at[m], p.x_dev)
        return y, x

    def s1(self, m, j):
        for c in self.c1(m, j):
            c.start()

    def s2(self, m, j):
        p, zs, a, h = self.p, self.p.order[j], self.a(m), self.half(m, j)
        y, x = self.c2(m, j)
        land = self.ld[m].at[zs, pl.ds(0, h)]
        self.got(land, self.rd.at[m, zs, 0])
        self.add(self.blk(m, p.yn, zs, 0, h), land)
        y.start()
        land = self.ld[m].at[zs, pl.ds(h, a - h)]
        self.got(land, self.rd.at[m, zs, 1])
        self.add(self.blk(m, p.xn, zs, h, a - h), land)
        x.start()

    def s3(self, m, j):
        p, zs, a = self.p, self.p.order[j], self.a(m)
        self.got(self.lx[m].at[zs], self.rx.at[m, zs])
        self.got(self.ly[m].at[zs], self.ry.at[m, zs])
        self.add(self.blk(m, p.dp, zs, 0, a), self.lx[m].at[zs], self.ly[m].at[zs])

    def zt(self, m, j):
        p, zs, a = self.p, self.p.order[j], self.a(m)

        @pl.when(p.middle)
        def _():
            land = self.lz[m].at[zs]
            self.got(land, self.rz.at[m, zs])
            self.add(self.blk(m, p.dp, zs, 0, a), land)

        self.cz_(m, j).start()

    def both(self, act):
        @pl.when(self.p.z > 0)
        def _():
            act(self.p.z)

        @pl.when(self.p.z < 3)
        def _():
            act(4)

    def zf(self, m):
        p = self.p

        def take(slot):
            land = self.lz[m].at[slot]
            self.got(land, self.rz.at[m, slot])
            self.add(self.blk(m, p.dp, p.z, 0, self.a(m)), land)

        self.both(take)

    def b1(self, m, j):
        p, zs, a, b = self.p, self.p.order[j], self.a(m), B_ROWS[m]

        @pl.when(p.middle)
        def _():
            self.got(self.lbz[m].at[zs], self.bz.at[m, zs])
            for d in range(4):
                self.add(self.blk(m, d, zs, a, b), self.lbz[m].at[zs, d])

        self.cb(m, j).start()

    def bf(self, m):
        p, a, b = self.p, self.a(m), B_ROWS[m]

        def take(slot):
            self.got(self.lbz[m].at[slot], self.bz.at[m, slot])
            for d in range(4):
                self.add(self.blk(m, d, p.z, a, b), self.lbz[m].at[slot, d])

        self.both(take)
        for c in self.cb2(m):
            c.start()

    def b3(self, m):
        p, a, b = self.p, self.a(m), B_ROWS[m]
        h = 16 * ((b // 16 + 1) // 2)
        y, x = self.cb3(m)
        land = self.lbd[m].at[pl.ds(0, h)]
        self.got(land, self.bd.at[m, 0])
        self.add(self.blk(m, p.yn, p.z, a, h), land)
        y.start()
        land = self.lbd[m].at[pl.ds(h, b - h)]
        self.got(land, self.bd.at[m, 1])
        self.add(self.blk(m, p.xn, p.z, a + h, b - h), land)
        x.start()

    def b4(self, m):
        p, a, b = self.p, self.a(m), B_ROWS[m]
        self.got(self.lbx[m], self.bx.at[m])
        self.got(self.lby[m], self.by.at[m])
        self.add(self.blk(m, p.dp, p.z, a, b), self.lbx[m], self.lby[m])

    def sent(self, m):
        for j in range(4):
            for c in self.c1(m, j) + self.c2(m, j):
                c.wait_send()
            if j:
                self.cz_(m, j).wait_send()
                if B_ROWS[m]:
                    self.cb(m, j).wait_send()
        if B_ROWS[m]:
            for c in self.cb2(m) + self.cb3(m):
                c.wait_send()


class Back:
    SEMS = dict(r1=(8,), s1=(8,), r2=(4,), s2=(4,), rb=(4,), sb=(4,), r3=(8,), s3=(8,), r4=(4,), s4=(4,))
    SHAPES = dict(msg=(8, 4, D), in1=(8, 4, D), gm=(16, 864), in2=(4, 16, 864), bs=(1, D), inb=(4, 1, D), sil=(8, 8, 288), silr=(64, 288),
                  gmr=(64, 864), b8=(8, 8, 288), in3=(8, 8, 288), b4=(4, 2, 288), in4=(4, 2, 288))

    @classmethod
    def scratch(cls):
        return [pltpu.VMEM(s, F32) for s in cls.SHAPES.values()] + [pltpu.SemaphoreType.DMA(s) for s in cls.SEMS.values()]

    def __init__(self, p, gmods, gbias, w_ada, scratch):
        self.p, self.gmods, self.gbias, self.w_ada = p, gmods, gbias, w_ada
        for name, ref in zip(list(self.SHAPES) + list(self.SEMS), scratch, strict=True):
            setattr(self, name, ref)

    def over_dp(self, src_of, land, sem_s, sem_r):
        p = self.p
        return [remote(src_of(r), land.at[p.dp], sem_s.at[r], sem_r.at[p.dp], (r, p.f)) for r in p.rows]

    def over_f(self, src_of, land, sem_s, sem_r):
        p = self.p
        return [remote(src_of(c), land.at[p.f], sem_s.at[c], sem_r.at[p.f], (p.dp, c)) for c in p.cols]

    def copies(self, step):
        return {
            1: lambda: self.over_f(lambda c: self.msg.at[c], self.in1, self.s1, self.r1),
            2: lambda: self.over_dp(lambda r: self.gm, self.in2, self.s2, self.r2),
            "b": lambda: self.over_dp(lambda r: self.bs, self.inb, self.sb, self.rb),
            3: lambda: self.over_f(lambda c: self.b8.at[c], self.in3, self.s3, self.r3),
            4: lambda: self.over_dp(lambda r: self.b4.at[r], self.in4, self.s4, self.r4),
        }[step]()

    def send(self, step):
        for c in self.copies(step):
            c.start()

    def arrived(self, land, sem, peers):
        for q in peers:
            remote(land.at[q], land.at[q], self.s1.at[0], sem.at[q], self.p.x_dev).wait_recv()

    def begin(self):
        p = self.p
        for s in range(2):
            for f in range(8):
                at = 864 * f
                while at < 864 * (f + 1):
                    b = at // D
                    end = min(864 * (f + 1), D * (b + 1))
                    self.msg[f, s : s + 1, at - 864 * f : end - 864 * f] = self.gmods[b, s, :, at - D * b : end - D * b].astype(B16).astype(F32)
                    at = end
                self.msg[f, s : s + 1, 864:D] = jnp.zeros((1, D - 864), F32)
        for f in range(8):
            for i, lo in enumerate((0, 144, 288, 1008)):
                self.msg[f, 2:3, lo : lo + 144] = self.gbias[i, :, 144 * f : 144 * f + 144]
            half = 576 * (f % 2)
            self.msg[f, 2:3, 432:1008] = self.gbias[4 + f // 2, :, half : half + 576]
            self.msg[f, 3:4, :] = jnp.zeros((1, D), F32)
        self.send(1)
        self.in1[p.f] = self.msg[p.f]

    def second(self, sil):
        p = self.p
        self.arrived(self.in1, self.r1, p.cols)
        total = jnp.zeros((1, D), F32)
        for f in range(8):
            rows = self.in1[f]
            self.gm[2 * f : 2 * f + 2, :] = rows[0:2, 0:864]
            total = total + rows[2:3]
        self.bs[...] = total
        self.send(2)
        self.send("b")
        self.in2[p.dp] = self.gm[...]
        self.inb[p.dp] = self.bs[...]
        for f in range(8):
            for d in range(4):
                self.silr[16 * d + 2 * f : 16 * d + 2 * f + 2, :] = sil[f, 2 * d : 2 * d + 2]

    def third(self, out_w, out_b, out_biases):
        p = self.p
        self.arrived(self.in2, self.r2, p.rows)
        self.arrived(self.inb, self.rb, p.rows)
        gm = self.in2[...].reshape(64, 864)
        low = gm.astype(B16)
        back = nt(low, self.w_ada[...])
        for f in range(8):
            for d in range(4):
                self.b8[f, 2 * d : 2 * d + 2, :] = back[16 * d + 2 * f : 16 * d + 2 * f + 2]
        self.send(3)
        self.in3[p.f] = self.b8[p.f]
        out_b[...] = jnp.sum(gm, axis=0, keepdims=True)
        out_w[...] = tn(self.silr[...].astype(B16), low)
        row = self.inb[0] + self.inb[1] + self.inb[2] + self.inb[3]
        for ref, lo in zip(out_biases, (0, 144, 288, 432, 1008), strict=True):
            ref[...] = row[:, lo : lo + ref.shape[1]]

    def fourth(self):
        p = self.p
        self.arrived(self.in3, self.r3, p.cols)
        total = self.in3[0]
        for f in range(1, 8):
            total = total + self.in3[f]
        for d in range(4):
            self.b4[d] = total[2 * d : 2 * d + 2]
        self.send(4)
        self.in4[p.dp] = self.b4[p.dp]

    def last(self, conds, outs):
        p = self.p
        self.arrived(self.in4, self.r4, p.rows)
        for s in range(2):
            x = conds[s][...].astype(F32)
            sig = 1.0 / (1.0 + jnp.exp(-x))
            slope = sig * (1.0 + x * (1.0 - sig))
            for d in range(4):
                outs[s][:, 288 * d : 288 * d + 288] = self.in4[d, s : s + 1, :] * slope[:, 288 * d : 288 * d + 288]

    def drain(self):
        for step in (1, 2, "b", 3, 4):
            for c in self.copies(step):
                c.wait_send()


def backward_steps(p, i, o, v, con, back):
    loads, ends = {}, []
    count = dict(ld=0, ws=0)

    def load(key, src, dst):
        c = pltpu.make_async_copy(src, dst, v.ld.at[count["ld"]])
        count["ld"] += 1
        c.start()
        loads[key] = c

    def save(src, dst):
        c = pltpu.make_async_copy(src, dst, v.ws.at[count["ws"]])
        count["ws"] += 1
        c.start()
        return c

    pending = {}

    by_dp = (p.dg, p.yn, p.xn, p.dp)
    by_z = p.order[::-1]

    def load_gbp():
        load("gbp", o.gbp, v.gbp)

    def load_act(n):
        load(("actp", n), o.act.at[by_dp[n]], v.actp.at[n % 2])

    def grad_fc2(n):
        if n == 0:
            loads["gbp"].wait()
        loads["actp", n].wait()
        dp = by_dp[n]

        y = nn(v.gbp[...].reshape(576, 768), v.actp[n % 2]).astype(B16)
        for z in range(4):
            v.r_big[dp, z] = y[144 * z : 144 * z + 144]
        if n + 2 < 4:
            load_act(n + 2)

    def load_mlp(k):
        s = k % 2
        if k == 0:
            load("gb", o.gb, v.gb)
        load(("w2", k), o.t3.at[k], v.w2.at[s])
        if k == 0:
            load_w1(k)
        load(("dact", k), o.dact.at[k], v.dact.at[s])

    def load_w1(k):
        load(("w1", k), o.t2.at[k], v.w1.at[0])

    def mlp(k):
        s = k % 2
        if k == 0:
            loads["gb"].wait()
        loads["w2", k].wait()
        loads["dact", k].wait()
        if k >= 2:
            c, w = pending.pop(("gup", k - 2))
            c.wait_send()
            w.wait()

        gu = (nn(v.gb[...], v.w2[s].reshape(D, D)) * v.dact[s].astype(F32)).astype(B16)
        v.gup[s] = gu
        v.gbias[4 + k] = jnp.sum(gu.astype(F32), axis=0, keepdims=True)
        c = remote(v.gup.at[s], o.gupp.at[k, pl.ds(TOK, TOK)], v.gs.at[k], v.gr.at[k], p.s_dev)
        c.start()
        pending["gup", k] = (c, save(v.gup.at[s], o.gupp.at[k, pl.ds(0, TOK)]))
        loads["w1", k].wait()

        two = nt(v.gup[s], v.w1[0].reshape(D, D))
        v.gh2[...] = two if k == 0 else v.gh2[...] + two
        if k + 1 < 4:
            load_w1(k + 1)
        if k + 2 < 4:
            load_mlp(k + 2)

    def end_mlp():
        for k in (2, 3):
            c, w = pending.pop(("gup", k))
            c.wait_send()
            w.wait()

    def load_g():
        load("h2p", o.h2p, v.h2p)
        for n in range(2):
            load_gup(n)

    def load_gup(n):
        if n == 0:
            for k in range(4):
                sib = o.gupp.at[k, pl.ds(TOK, TOK)]
                remote(sib, sib, v.gs.at[k], v.gr.at[k], p.s_dev).wait_recv()
        load(("gupv", n), o.gupp.at[by_z[n]], v.gupv.at[n % 2])

    def grad_fc1(n):
        if n == 0:
            loads["h2p"].wait()
        loads["gupv", n].wait()
        z = by_z[n]

        y = nn(v.h2p[...].reshape(576, 768), v.gupv[n % 2]).astype(B16)
        for d in range(4):
            v.r_fc1[d, z] = y[144 * d : 144 * d + 144]
        if n + 2 < 4:
            load_gup(n + 2)

    def load_x():
        for n in range(2):
            load_branch(n)
        load_n()

    def load_branch(k):
        load(("w2", k), o.t3.at[k], v.w2.at[k % 2])
        load(("act", k), o.act.at[k, pl.ds(0, TOK)], v.acto.at[k % 2])

    def branch(k):
        loads["w2", k].wait()
        loads["act", k].wait()
        one = nt(v.acto[k % 2], v.w2[k % 2].reshape(D, D))
        v.branch[...] = one if k == 0 else v.branch[...] + one
        if k + 2 < 4:
            load_branch(k + 2)

    def result():
        for key in ("tok", "attn", "cot0", "cot1"):
            loads[key].wait()

        def body(r, s):
            branch = v.branch[r, :] + con.bias[3]
            v.res[r, :] = (v.tok[r, :].astype(F32) + con.mods[2, s] * v.attn[r, :] + con.mods[5, s] * branch).astype(B16)
            v.gmods[5, s] += jnp.sum(v.cot[r, :].astype(F32) * branch, axis=0, keepdims=True)

        by_rows(body)
        pltpu.make_async_copy(v.res, o.result, v.fs.at[0]).start()

    def end_result():
        pltpu.make_async_copy(v.res, o.result, v.fs.at[0]).wait()

    def load_n():
        load("cot0", i.cot_full.at[0], cut(v.cot, 0, SEQ))
        load("cot1", i.cot_masked.at[0], cut(v.cot, SEQ, KEEP))
        load("tok", o.tok, v.tok)
        load("attn", o.attn, v.attn)

    def norm2():
        for key in ("tok", "attn", "cot0", "cot1"):
            loads[key].wait()
        zero = jnp.zeros((1, D), F32)
        for b in range(6):
            for s in range(2):
                v.gmods[b, s] = zero
        v.gbias[2] = zero
        v.gbias[3] = zero

        def body(r, s):
            tok = v.tok[r, :].astype(F32)
            attn = v.attn[r, :]
            resid = tok + con.mods[2, s] * attn
            n, inv = layer_stats(resid)
            cot = v.cot[r, :].astype(F32)
            gh = v.gh2[r, :]
            v.gmods[4, s] += jnp.sum(gh * n, axis=0, keepdims=True)
            v.gmods[3, s] += jnp.sum(gh, axis=0, keepdims=True)
            u = gh * (1.0 + con.mods[4, s])
            gres = cot + inv * (u - jnp.mean(u, axis=-1, keepdims=True) - n * jnp.mean(u * n, axis=-1, keepdims=True))
            v.gres[r, :] = gres
            v.gmods[2, s] += jnp.sum(gres * attn, axis=0, keepdims=True)
            ga = (con.mods[2, s] * gres).astype(B16)
            v.ga[r, :] = ga
            v.gbias[2] += jnp.sum(ga.astype(F32), axis=0, keepdims=True)
            v.gbias[3] += jnp.sum(v.gb[r, :].astype(F32), axis=0, keepdims=True)

        by_rows(body)

    def load_o():
        for k in range(4):
            load(("wo", k), o.t0.at[k, :, :, :, pl.ds(768, 384)], v.wo.at[k])

    def give_a():
        remote(v.ga, cut(o.gap, TOK, TOK), v.ps.at[0], v.gpr.at[0], p.s_dev).start()
        pltpu.make_async_copy(v.ga, cut(o.gap, 0, TOK), v.pb.at[0]).start()

    def load_m():
        load("mxp", o.mxp, v.mxp)
        remote(v.ga, cut(o.gap, TOK, TOK), v.ps.at[0], v.gpr.at[0], p.s_dev).wait()
        pltpu.make_async_copy(v.ga, cut(o.gap, 0, TOK), v.pb.at[0]).wait()
        load("gap", o.gap, v.gapv)

    def grad_mixed():
        y = jnp.zeros((TOK, D), F32)
        for k in range(4):
            loads["wo", k].wait()
            y = y + nt(v.ga[:, 288 * k : 288 * k + 288], v.wo[k, :, :, :, 96:384].reshape(D, 288))
        y = y.astype(B16)
        for h in range(HEADS):
            v.gmh[h] = y[:, 72 * h : 72 * h + 72]

    def grad_out():
        loads["mxp"].wait()
        loads["gap"].wait()
        y = nn(v.mxp[...].reshape(576, 768), v.gapv[...]).astype(B16)
        for d in range(4):
            for z in range(4):
                v.r_big[d, z, :, 864:1152] = y[144 * d : 144 * d + 144, 288 * z : 288 * z + 288]

    def load_q():
        load("qkv", o.qkv, v.qkv)
        load("tok", o.tok, v.tok)
        load("h1p", o.h1p, v.h1p)
        for k in range(2):
            load_wq(k)

    def load_wq(k):
        load(("wq", k), o.t0.at[by_z[k]], v.wq.at[k % 2])

    def heads(k, n):
        if k == 0:
            loads["qkv"].wait()

        def step(g, carry):
            parts = [(4 * g + u, lo, hi) for u in range(4) for lo, hi in ((0, SEQ), (SEQ, TOK))]
            qs, ks, vs = ([v.qkv[16 * n + h, lo:hi] for h, lo, hi in parts] for n in range(3))
            gs = [v.gmh[h, lo:hi] for h, lo, hi in parts]
            scores = [nt(key, q) * SCALE for q, key in zip(qs, ks)]
            gps = [nt(val, gm) for val, gm in zip(vs, gs)]
            exps = [jnp.exp(x - jnp.max(x, axis=0, keepdims=True)) for x in scores]
            probs = [e * (1.0 / jnp.sum(e, axis=0, keepdims=True)) for e in exps]
            gsc = [(pr * (gp - jnp.sum(pr * gp, axis=0, keepdims=True))).astype(B16) for pr, gp in zip(probs, gps)]
            for (h, lo, hi), pr, gc, q, key, gm in zip(parts, probs, gsc, qs, ks, gs):
                v.qkv[32 + h, lo:hi] = nn(pr.astype(B16), gm).astype(B16)
                v.qkv[h, lo:hi] = (tn(gc, key) * SCALE).astype(B16)
                v.qkv[16 + h, lo:hi] = (nn(gc, q) * SCALE).astype(B16)
            return carry

        lax.fori_loop(k // 4, (k + n) // 4, step, 0)

    def grad_h1(n):
        s = n % 2
        z = by_z[n]
        for h in range(12):
            v.gq[s, :, 72 * h : 72 * h + 72] = v.qkv[12 * z + h]
        c = remote(v.gq.at[s], o.gqp.at[z, pl.ds(TOK, TOK)], v.qs.at[z], v.qr.at[z], p.s_dev)
        c.start()
        pending["gq", n] = (c, save(v.gq.at[s], o.gqp.at[z, pl.ds(0, TOK)]))
        v.gsum[z] = jnp.sum(v.gq[s].astype(F32), axis=0, keepdims=True)
        loads["wq", n].wait()
        y = nt(v.gq[s], v.wq[s, :, :, :, 0:864].reshape(D, 864))
        v.gh1[...] = y if n == 0 else v.gh1[...] + y
        if n + 2 < 4:
            load_wq(n + 2)

    def sums():
        v.gbias[0, :, 0:864] = v.gsum[0]
        v.gbias[0, :, 864:D] = v.gsum[1, :, 0:288]
        v.gbias[1, :, 0:288] = v.gsum[2, :, 576:864]
        v.gbias[1, :, 288:D] = v.gsum[3]

    def load_gq(n):
        z = by_z[n]
        sib = o.gqp.at[z, pl.ds(TOK, TOK)]
        remote(sib, sib, v.qs.at[z], v.qr.at[z], p.s_dev).wait_recv()
        c, w = pending.pop(("gq", n))
        c.wait_send()
        w.wait()
        load(("gqv", n), o.gqp.at[z], v.gqv.at[n % 2])

    def grad_qkv(n):
        if n == 0:
            loads["h1p"].wait()
        loads["gqv", n].wait()
        y = nn(v.h1p[...].reshape(576, 768), v.gqv[n % 2]).astype(B16)
        for d in range(4):
            v.r_big[d, by_z[n], :, 0:864] = y[144 * d : 144 * d + 144]

    def norm1():
        loads["tok"].wait()

        def body(r, s):
            n, inv = layer_stats(v.tok[r, :].astype(F32))
            gh = v.gh1[r, :]
            v.gmods[1, s] += jnp.sum(gh * n, axis=0, keepdims=True)
            v.gmods[0, s] += jnp.sum(gh, axis=0, keepdims=True)
            u = gh * (1.0 + con.mods[1, s])
            v.gres[r, :] += inv * (u - jnp.mean(u, axis=-1, keepdims=True) - n * jnp.mean(u * n, axis=-1, keepdims=True))

        by_rows(body)

    def put_full():
        pltpu.make_async_copy(cut(v.gres, 0, SEQ), o.gfull, v.fs.at[3]).start()

    def end_full():
        pltpu.make_async_copy(cut(v.gres, 0, SEQ), o.gfull, v.fs.at[3]).wait()

    def spread():
        hot = (lax.broadcasted_iota(jnp.int32, (SEQ, KEEP), 0) == i.keep[...]).astype(F32)
        v.spr[...] = lax.dot_general(hot, v.gres[SEQ:TOK], (((1,), (0,)), ((), ())), precision=lax.Precision.HIGHEST, preferred_element_type=F32)
        pltpu.make_async_copy(v.spr, o.gmasked, v.fs.at[1]).start()

    def end_spread():
        pltpu.make_async_copy(v.spr, o.gmasked, v.fs.at[1]).wait()

    def put(n, src, dst):
        return pltpu.make_async_copy(src, dst, v.fo.at[n])

    def finals(n):
        return put(n, v.part[n].at[0], (o.gw_fc1, o.gw_qkv, o.gw_out)[n].at[p.c])

    def swaps(n):
        return remote(v.part[n].at[1], (o.gw_fc1, o.gw_qkv, o.gw_out)[n].at[p.c], v.xs.at[n], v.xr.at[n], p.s_dev)

    def swap(block, width, n):
        first = p.c == 0
        lo, hi = block[:, 0:width], block[:, width : 2 * width]
        v.part[n][1] = jnp.where(first, hi, lo)
        v.part[n][0] = jnp.where(first, lo, hi)
        finals(n).start()
        swaps(n).start()

    def end_swap(n):
        finals(n).wait()
        swaps(n).wait_send()
        land = (o.gw_fc1, o.gw_qkv, o.gw_out)[n].at[1 - p.c]
        remote(land, land, v.xs.at[n], v.xr.at[n], p.s_dev).wait_recv()

    def out_fc2():
        put(3, v.r_big.at[p.dp, p.z], o.gw_fc2).start()

    def end_fc2():
        put(3, v.r_big.at[p.dp, p.z], o.gw_fc2).wait()

    def out_fc1():
        swap(v.r_fc1[p.dp, p.z], 576, 0)

    def out_qo():
        swap(v.r_big[p.dp, p.z, :, 0:864], 432, 1)
        swap(v.r_big[p.dp, p.z, :, 864:1152], 144, 2)

    def end_fc1():
        end_swap(0)

    def end_qo():
        end_swap(1)
        end_swap(2)

    def back_second():
        back.second(con.in2)

    def back_third():
        back.third(v.gwa, o.gb_ada, (o.gb_q, o.gb_v, o.gb_out, o.gb_fc1, o.gb_fc2))

        pltpu.make_async_copy(v.gwa, o.gw_ada, v.fs.at[2]).start()

    def end_ada():
        pltpu.make_async_copy(v.gwa, o.gw_ada, v.fs.at[2]).wait()

    def back_last():
        back.last((i.cond_full, i.cond_masked), (o.gc_full, o.gc_masked))

    table = {n: f for n, f in locals().items() if callable(f)}
    table.update(back_begin=back.begin, back_fourth=back.fourth)
    return table


STAGE = dict(got_q=((144, 432), B16), got_1=((144, 576), B16), got_o=((144, 144), B16), w_out=((288, 144), B16), bq=((144, 1152), B16), b1=((144, 1152), B16),
             gmods=((6, 2, 1, D), F32), gbias=((8, 1, D), F32), part1=((2, 144, 576), B16), partq=((2, 144, 432), B16), parto=((2, 144, 144), B16))
SIGNALS = dict(st=(3,), rt=(3,), lq=(2,), lo=(4,), l1=(2,), lt=(4,), pt=(4, 4), pr=(4, 4), pl_=(4, 4), as_=(4,), ar=(4,), ow=(16,), oq=(1,),
               ld=(80,), ws=(24,), gs=(4,), gr=(4,), qs=(4,), qr=(4,), ps=(4,), pb=(4,), gpr=(4,), xs=(3,), xr=(3,), fs=(4,), fo=(4,))
SCOPE_P = dict(hid=((TOK, D), B16), hid2=((TOK, D), B16), tok=((TOK, D), B16), h1t=((8, 144, TOK), B16), h2t=((8, 144, TOK), B16), gbt=((8, 144, TOK), B16), mxt=((8, 144, TOK), B16),
           gb=((TOK, D), B16), mixed=((TOK, D), B16), attn=((TOK, D), F32), act=((4, TOK, D), B16), dact=((4, TOK, D), B16))
SCOPE_I = dict(masked=((SEQ, D), B16), cot=((TOK, D), B16))
SCOPE_H = dict(qkv=((48, TOK, HEAD_DIM), B16), mixh=((HEADS, TOK, HEAD_DIM), B16), wq=((2, 4, 2, 144, D), B16))
SCOPE_U = dict(wo=((4, 4, 2, 144, 384), B16), w1=((2, 4, 2, 144, D), B16))
SCOPE_R = dict(r_big=((4, 4, 144, D), B16), r_fc1=((4, 4, 144, D), B16), gmh=((HEADS, TOK, HEAD_DIM), B16), gres=((TOK, D), F32), ga=((TOK, D), B16))
SCOPE_M = dict(gb=((TOK, D), B16), gh2=((TOK, D), F32))
SCOPE_W = dict(gbp=((4, 144, 768), B16), actp=((2, 2 * TOK, D), B16), w2=((2, 4, 2, 144, D), B16), w1=((1, 4, 2, 144, D), B16),
           dact=((2, TOK, D), B16), gup=((2, TOK, D), B16))
SCOPE_G = dict(h2p=((4, 144, 768), B16), gupv=((2, 2 * TOK, D), B16))
SCOPE_N = dict(tok=((TOK, D), B16), attn=((TOK, D), F32), cot=((TOK, D), B16))
SCOPE_X = dict(w2=((2, 4, 2, 144, D), B16), acto=((2, TOK, D), B16), branch=((TOK, D), F32), tok=((TOK, D), B16), attn=((TOK, D), F32), cot=((TOK, D), B16), res=((TOK, D), B16))
SCOPE_S = dict(spr=((SEQ, D), F32), gwa=((288, 864), F32))
SCOPE_B = dict(wo=((4, 4, 2, 144, 384), B16))
SCOPE_O = dict(gapv=((2 * TOK, D), B16), mxp=((4, 144, 768), B16))
SCOPE_Q = dict(qkv=((48, TOK, HEAD_DIM), B16), wq=((2, 4, 2, 144, D), B16), gq=((2, TOK, 864), B16),
           gsum=((4, 1, 864), F32), gqv=((2, 2 * TOK, 864), B16), h1p=((4, 144, 768), B16), gh1=((TOK, D), F32), tok=((TOK, D), B16))
INS_V = dict(keep=0, cond_full=0, cond_masked=0, w_ada=0, b_ada=0, b_q=0, b_v=0, b_out=0, b_fc1=0, b_fc2=0, w_qkv=0, w_out=0, w_fc1=0, w_fc2=0)
INS_A = dict(full=0, masked=0, cot_full=0, cot_masked=0)
OUT_V = dict(gc_full=((1, D), F32), gc_masked=((1, D), F32), gb_ada=((1, 864), F32), gb_q=((1, 144), F32), gb_v=((1, 144), F32),
             gb_out=((1, 144), F32), gb_fc1=((1, 576), F32), gb_fc2=((1, 144), F32))
OUT_A = dict(
    result=((TOK, D), B16), gfull=((SEQ, D), F32), gmasked=((SEQ, D), F32), gw_ada=((288, 864), F32), gw_qkv=((2, 144, 432), B16),
    gw_out=((2, 144, 144), B16), gw_fc1=((2, 144, 576), B16), gw_fc2=((144, D), B16),
    t0=((4, 4, 2, 144, D), B16), t2=((4, 4, 2, 144, D), B16), t3=((4, 4, 2, 144, D), B16),
    tok=((TOK, D), B16), qkv=((48, TOK, HEAD_DIM), B16), attn=((TOK, D), F32),
    mxp=((4, 144, 768), B16), h1p=((4, 144, 768), B16), h2p=((4, 144, 768), B16), gbp=((4, 144, 768), B16), act=((4, 2 * TOK, D), B16), dact=((4, TOK, D), B16), gb=((TOK, D), B16),
    gupp=((4, 2 * TOK, D), B16), gqp=((4, 2 * TOK, 864), B16), gap=((2 * TOK, D), B16),
)


def block_kernel(events, *refs):
    i, o, v = Bag(), Bag(), Bag()
    refs = list(refs)
    for bag, names in ((i, INS_V), (i, INS_A), (o, OUT_V), (o, OUT_A), (v, STAGE), (v, SIGNALS)):
        for n in names:
            setattr(bag, n, refs.pop(0))
    v.part = (v.part1, v.partq, v.parto)
    p = Place()
    con_refs = [refs.pop(0) for _ in range(len(Conditions.SHAPES) + len(Conditions.SEMS))]
    back_refs = [refs.pop(0) for _ in range(len(Back.SHAPES) + len(Back.SEMS))]
    sc_refs = [refs.pop(0) for _ in range(Scatter.count())]
    con = Conditions(p, (i.cond_full, i.cond_masked), i.w_ada, i.b_ada, (i.b_q, i.b_v, i.b_out, i.b_fc1, i.b_fc2), con_refs)
    back = Back(p, v.gmods, v.gbias, i.w_ada, back_refs)
    sc = Scatter(p, None, sc_refs)
    g = Gather(p, (o.t0, o.t2, o.t3), (v.bq, v.b1, i.w_fc2), refs)
    f_table = forward_steps(p, i, o, v, con)
    table = backward_steps(p, i, o, v, con, back)
    f_table.update(second=con.second, third=con.third, fourth=con.fourth, last=con.last, begin=con.begin)
    table.update({"f_" + n.removeprefix("f_"): f for n, f in f_table.items()})
    table.update(own=g.own, bown=g.bown, arr=g.arr, cross=g.cross, bcross=g.bcross, bz=g.bz_, barr=g.barr, fin=g.fin, have=g.have)
    table.update(s1=sc.s1, s2=sc.s2, s3=sc.s3, zt=sc.zt, zf=sc.zf, b1=sc.b1, bf=sc.bf, b3=sc.b3, b4=sc.b4, sent=sc.sent)

    def stages(n):
        return stage(p, (i.w_qkv, v.w_out, i.w_fc1)[n], (v.got_q, v.got_o, v.got_1)[n], v.st.at[n], v.rt.at[n])

    def join_q():
        stages(0).wait_recv()
        join(p, i.w_qkv, v.got_q, v.bq)
        stages(1).wait_recv()
        join(p, v.w_out, v.got_o, v.bq, 864)

    def join_1():
        stages(2).wait_recv()
        join(p, i.w_fc1, v.got_1, v.b1)

    table.update(join_q=join_q, join_1=join_1)

    def run(queue):
        for name, args in queue:
            if args and isinstance(args[0], dict):
                spec = args[0]

                def scope(*inner, spec=spec):
                    for n, ref in zip(spec, inner, strict=True):
                        setattr(v, n, ref)
                    if spec is SCOPE_R:
                        sc.r = (v.r_big, v.r_fc1, v.r_big)
                    run(queue)

                pl.run_scoped(scope, *[pltpu.VMEM(s, d) for s, d in spec.values()])
            elif name not in table:
                return
            else:
                table[name](*args)

    v.w_out[...] = i.w_out[...].astype(F32).T.astype(B16)
    p.barrier()
    for n in range(3):
        stages(n).start()
    run(iter(events))
    for n in range(3):
        stages(n).wait_send()
    con.drain()
    back.drain()
    g.drain()


def block_events():
    e = Script()
    e.bown(FC2)
    e.join_q()
    e.bown(QO)
    e.own(QO)
    e.bcross(QO)
    e.join_1()
    e.own(FC1)
    e.bown(FC1)
    e.open(SCOPE_P)
    e.arr(QO, 2)
    e.open(SCOPE_I)
    e.arr(QO, 1)
    e.f_get_tokens()
    e.bcross(FC1)
    e.bz(QO)
    e.cross(QO, 2)
    e.arr(QO, 3)
    e.barr(QO, 2)
    e.f_begin()
    e.barr(QO, 1)
    e.cross(QO, 0)
    e.f_second()
    e.cross(QO, 1)
    e.arr(FC1, 1)
    e.bz(FC1)
    e.cross(QO, 3)
    e.barr(QO, 3)
    e.f_tokens()
    e.f_third()
    e.f_fourth()
    e.fin(QO, 2)
    e.cross(FC1, 0)
    e.fin(QO, 0)
    e.fin(QO, 1)
    e.f_last()
    e.arr(FC1, 2)
    e.cross(FC1, 1)
    e.arr(FC1, 3)
    e.fin(QO, 3)
    e.f_norm1()
    e.own(FC2)
    e.f_grads_in()
    e.have(QO)
    e.close()
    e.f_turn1()
    e.open(SCOPE_H)
    e.barr(FC1, 1)
    e.f_load_q(0)
    e.f_load_q(1)
    e.f_qkv(0)
    e.f_qkv(1)
    e.fin(FC1, 0)
    e.f_qkv(2)
    e.cross(FC1, 2)
    e.fin(FC1, 1)
    e.f_qkv(3)
    e.barr(FC1, 2)
    e.f_heads(0, 4)
    e.f_heads(4, 4)
    e.f_heads(8, 4)
    e.f_heads(12, 4)
    e.f_mix()
    e.f_end_qkv()
    e.close()
    e.open(SCOPE_U)
    e.barr(FC1, 3)
    e.f_load_o()
    e.cross(FC1, 3)
    e.bcross(FC2)
    e.f_attend()
    e.cross(FC2, 0)
    e.fin(FC1, 2)
    e.f_turn2()
    e.arr(FC2, 2)
    e.arr(FC2, 1)
    e.fin(FC1, 3)
    e.bz(FC2)
    e.have(FC1)
    e.f_load_1(0)
    e.f_load_1(1)
    e.f_fc1(0)
    e.f_fc1(1)
    e.arr(FC2, 3)
    e.f_fc1(2)
    e.cross(FC2, 2)
    e.f_fc1(3)
    e.close()
    e.f_end()
    e.cross(FC2, 1)
    e.close()
    e.open(SCOPE_R)
    e.open(SCOPE_M)
    e.open(SCOPE_N)
    e.load_n()
    e.open(SCOPE_W)
    e.barr(FC2, 1)
    e.cross(FC2, 3)
    e.load_gbp()
    e.load_act(0)
    e.load_act(1)
    e.fin(FC2, 0)
    e.barr(FC2, 2)
    e.grad_fc2(0)
    e.s1(FC2, 1)
    e.grad_fc2(1)
    e.grad_fc2(2)
    e.s1(FC2, 3)
    e.fin(FC2, 1)
    e.grad_fc2(3)
    e.barr(FC2, 3)
    e.b1(FC2, 3)
    e.s1(FC2, 2)
    e.fin(FC2, 3)
    e.fin(FC2, 2)
    e.b1(FC2, 2)
    e.s1(FC2, 0)
    e.have(FC2)
    e.load_mlp(0)
    e.s2(FC2, 3)
    e.s2(FC2, 1)
    e.load_mlp(1)
    e.s2(FC2, 2)
    e.mlp(0)
    e.b1(FC2, 1)
    e.mlp(1)
    e.s3(FC2, 3)
    e.zt(FC2, 3)
    e.s2(FC2, 0)
    e.mlp(2)
    e.mlp(3)
    e.s3(FC2, 1)
    e.zt(FC2, 1)
    e.end_mlp()
    e.close()
    e.open(SCOPE_G)
    e.open(SCOPE_B)
    e.load_o()
    e.load_g()
    e.norm2()
    e.s3(FC2, 2)
    e.zt(FC2, 2)
    e.bf(FC2)
    e.give_a()
    e.grad_fc1(0)
    e.s1(FC1, 3)
    e.grad_fc1(1)
    e.b3(FC2)
    e.s1(FC1, 2)
    e.b1(FC1, 3)
    e.grad_fc1(2)
    e.grad_fc1(3)
    e.s2(FC1, 3)
    e.grad_mixed()
    e.s3(FC2, 0)
    e.b4(FC2)
    e.b1(FC1, 2)
    e.s1(FC1, 1)
    e.s2(FC1, 2)
    e.s1(FC1, 0)
    e.zf(FC2)
    e.close()
    e.sent(FC2)
    e.close()
    e.close()
    e.close()
    e.out_fc2()
    e.open(SCOPE_Q)
    e.load_q()
    e.end_fc2()
    e.open(SCOPE_O)
    e.load_m()
    e.grad_out()
    e.close()
    e.b1(FC1, 1)
    e.heads(0, 4)
    e.heads(4, 4)
    e.s2(FC1, 1)
    e.heads(8, 4)
    e.heads(12, 4)
    e.grad_h1(0)
    e.grad_h1(1)
    e.s3(FC1, 2)
    e.s3(FC1, 3)
    e.zt(FC1, 3)
    e.s2(FC1, 0)
    e.load_gq(0)
    e.grad_h1(2)
    e.load_gq(1)
    e.zt(FC1, 2)
    e.grad_qkv(0)
    e.grad_h1(3)
    e.bf(FC1)
    e.grad_qkv(1)
    e.s1(QO, 3)
    e.b1(QO, 3)
    e.load_gq(2)
    e.s3(FC1, 0)
    e.s3(FC1, 1)
    e.s1(QO, 2)
    e.load_gq(3)
    e.grad_qkv(2)
    e.grad_qkv(3)
    e.sums()
    e.s1(QO, 1)
    e.norm1()
    e.b3(FC1)
    e.b1(QO, 2)
    e.put_full()
    e.close()
    e.open(SCOPE_X)
    e.s2(QO, 3)
    e.s1(QO, 0)
    e.load_x()
    e.branch(0)
    e.branch(1)
    e.b1(QO, 1)
    e.b4(FC1)
    e.s2(QO, 1)
    e.branch(2)
    e.branch(3)
    e.s2(QO, 2)
    e.s3(QO, 3)
    e.zt(QO, 3)
    e.result()
    e.end_result()
    e.zt(FC1, 1)
    e.s2(QO, 0)
    e.close()
    e.open(SCOPE_S)
    e.back_begin()
    e.back_second()
    e.back_third()
    e.s3(QO, 2)
    e.bf(QO)
    e.s3(QO, 1)
    e.zt(QO, 2)
    e.zf(FC1)
    e.zt(QO, 1)
    e.back_fourth()
    e.spread()
    e.s3(QO, 0)
    e.b3(QO)
    e.back_last()
    e.end_full()
    e.zf(QO)
    e.b4(QO)
    e.out_qo()
    e.out_fc1()
    e.sent(FC1)
    e.end_qo()
    e.sent(QO)
    e.end_spread()
    e.end_ada()
    e.end_fc1()
    e.close()
    e.close()
    return e.steps


def block(events, args):
    V, A = pl.BlockSpec(memory_space=pltpu.VMEM), pl.BlockSpec(memory_space=pl.ANY)
    outs = {**OUT_V, **OUT_A}
    got = pl.pallas_call(
        functools.partial(block_kernel, events),
        out_shape=[jax.ShapeDtypeStruct(s, d) for s, d in outs.values()],
        in_specs=[V] * len(INS_V) + [A] * len(INS_A),
        out_specs=[V] * len(OUT_V) + [A] * len(OUT_A),
        scratch_shapes=[pltpu.VMEM(s, d) for s, d in STAGE.values()] + [pltpu.SemaphoreType.DMA(s) for s in SIGNALS.values()]
        + Conditions.scratch() + Back.scratch() + Scatter.scratch() + Gather.scratch(),
        compiler_params=pltpu.CompilerParams(collective_id=0, has_side_effects=True, vmem_limit_bytes=62 * 2**20),
        name="block",
    )(*args)
    return dict(zip(outs, got, strict=True))


FINAL_A = dict(result=((TOK, D), B16), gfull=((SEQ, D), F32), gmasked=((SEQ, D), F32), gw_ada=((288, 864), F32))
FINAL_V = dict(gw_qkv=(2, 144, 432), gw_out=(2, 144, 144), gw_fc1=(2, 144, 576), gw_fc2=(144, D))


def final_kernel(result, gfull, gmasked, gw_ada, *refs):
    blocks, refs = refs[:4], refs[4:]
    small, refs = refs[:8], refs[8:]
    outs, sem = refs[:-1], refs[-1]
    moves = ((cut(result, 0, SEQ), outs[0].at[0]), (cut(result, SEQ, KEEP), outs[1].at[0]), (gfull, outs[2].at[0]), (gmasked, outs[3].at[0]), (gw_ada, outs[4]))
    copies = [pltpu.make_async_copy(src, dst, sem.at[n]) for n, (src, dst) in enumerate(moves)]
    for c in copies:
        c.start()
    for n, (src, dst) in enumerate(zip(blocks, outs[5:9], strict=True)):
        y = src[...].astype(F32)
        dst[...] = y.reshape(288, 144).T if n == 1 else y
    for src, dst in zip(small, outs[9:], strict=True):
        dst[...] = src[...].reshape(dst.shape)
    for c in copies:
        c.wait()


def whole(full_input, masked_input, keep_index, cond_full, cond_masked, w_ada, b_ada, w_qkv, b_q, b_v, w_out, b_out, w_fc1, b_fc1, w_fc2, b_fc2, cot_full, cot_masked):
    g = block(block_events(), (keep_index, cond_full, cond_masked, w_ada, b_ada, b_q, b_v, b_out, b_fc1, b_fc2, w_qkv, w_out.T, w_fc1, w_fc2.T, full_input, masked_input, cot_full, cot_masked))
    V, A = pl.BlockSpec(memory_space=pltpu.VMEM), pl.BlockSpec(memory_space=pl.ANY)
    shapes = [((1, SEQ, D), B16), ((1, KEEP, D), B16), ((1, SEQ, D), F32), ((1, SEQ, D), F32), ((288, 864), F32)]
    shapes += [((144, 288) if n == 1 else s, F32) for n, s in enumerate(FINAL_V.values())]
    shapes += [((1, D), F32)] * 2 + [(s, F32) for s in ((864,), (144,), (144,), (144,), (576,), (144,))]
    out = pl.pallas_call(
        final_kernel,
        out_shape=[jax.ShapeDtypeStruct(s, d) for s, d in shapes],
        in_specs=[V] * 16,
        out_specs=[A] * 5 + [V] * (len(shapes) - 5),
        scratch_shapes=[pltpu.SemaphoreType.DMA((5,))],
        name="results",
    )(*[g[n] for n in FINAL_A], *[g[n] for n in FINAL_V], *[g[n] for n in OUT_V])
    out_full, out_masked, gfull, gmasked, gw_ada, gw_qkv, gw_out, gw_fc1, gw_fc2, gc_full, gc_masked, gb_ada, gb_q, gb_v, gb_out, gb_fc1, gb_fc2 = out
    return (
        out_full, out_masked, gfull, gmasked, gc_full, gc_masked, gw_ada, gb_ada, gw_qkv.reshape(288, 432), gb_q, gb_v, gw_out.T, gb_out,
        gw_fc1.reshape(288, 576), gb_fc1, gw_fc2.T, gb_fc2,
    )


def plain_layer_stats(values):
    centered = values - jnp.mean(values, axis=-1, keepdims=True)
    inverse = lax.rsqrt(jnp.mean(centered * centered, axis=-1, keepdims=True) + 1e-06)
    return (centered * inverse, inverse)


def plain_layer_back(upstream, normed, inverse):
    return inverse * (
        upstream
        - jnp.mean(upstream, axis=-1, keepdims=True)
        - normed * jnp.mean(upstream * normed, axis=-1, keepdims=True)
    )


def plain_gelu_tanh(values):
    return jax.nn.gelu(values, approximate=True)


def plain_expand_mods(piece, full_length, kept_length):
    head_part = jnp.broadcast_to(piece[:, 0:1], (piece.shape[0], full_length, piece.shape[2]))
    tail_part = jnp.broadcast_to(piece[:, 1:2], (piece.shape[0], kept_length, piece.shape[2]))
    return jnp.concatenate([head_part, tail_part], axis=1)


def plain_image_sums(values, full_length):
    return jnp.stack(
        [jnp.sum(values[:, :full_length], axis=1), jnp.sum(values[:, full_length:], axis=1)], axis=1
    )


def plain_forward_pass(tokens, mods, weights, biases, full_length):
    images, length, features = tokens.shape
    head_count = features // HEAD_DIM
    pieces = [
        plain_expand_mods(
            mods[:, :, column * features : (column + 1) * features],
            full_length,
            length - full_length,
        )
        for column in range(6)
    ]
    norm_one, inverse_one = plain_layer_stats(tokens)
    hidden_one = (norm_one * (1.0 + pieces[1]) + pieces[0]).astype(jnp.bfloat16)
    bias_all = jnp.concatenate([biases[1], jnp.zeros((features,), jnp.bfloat16), biases[2]]).astype(
        jnp.float32
    )
    projected = (
        jnp.einsum("itd,de->ite", hidden_one, weights[1], preferred_element_type=jnp.float32)
        + bias_all
    )
    projected = projected.astype(jnp.bfloat16).reshape(images, length, 3, head_count, HEAD_DIM)
    query_rows = projected[:, :, 0]
    key_rows = projected[:, :, 1]
    value_rows = projected[:, :, 2]
    scale_factor = 1.0 / math.sqrt(HEAD_DIM)
    scores = (
        jnp.einsum("iqhc,ikhc->ihqk", query_rows, key_rows, preferred_element_type=jnp.float32)
        * scale_factor
    )
    marker = jnp.arange(length) >= full_length
    same_image = marker[:, None] == marker[None, :]
    scores = jnp.where(same_image, scores, -1e30)
    row_max = jnp.max(scores, axis=-1, keepdims=True)
    exponent = jnp.exp(scores - row_max)
    attention = exponent / jnp.sum(exponent, axis=-1, keepdims=True)
    attention_low = attention.astype(jnp.bfloat16)
    mixed = jnp.einsum(
        "ihqk,ikhc->iqhc", attention_low, value_rows, preferred_element_type=jnp.float32
    )
    mixed = mixed.astype(jnp.bfloat16).reshape(images, length, features)
    attn_out = jnp.einsum(
        "itd,de->ite", mixed, weights[2], preferred_element_type=jnp.float32
    ) + biases[3].astype(jnp.float32)
    residual = tokens + pieces[2] * attn_out
    norm_two, inverse_two = plain_layer_stats(residual)
    hidden_two = (norm_two * (1.0 + pieces[4]) + pieces[3]).astype(jnp.bfloat16)
    upper = jnp.einsum(
        "itd,df->itf", hidden_two, weights[3], preferred_element_type=jnp.float32
    ) + biases[4].astype(jnp.float32)
    activated = plain_gelu_tanh(upper).astype(jnp.bfloat16)
    branch = jnp.einsum(
        "itf,fd->itd", activated, weights[4], preferred_element_type=jnp.float32
    ) + biases[5].astype(jnp.float32)
    result = residual + pieces[5] * branch
    return (
        result,
        pieces,
        norm_one,
        inverse_one,
        hidden_one,
        query_rows,
        key_rows,
        value_rows,
        attention,
        attention_low,
        mixed,
        attn_out,
        norm_two,
        inverse_two,
        hidden_two,
        upper,
        activated,
        branch,
    )


def general(
    full_input,
    masked_input,
    keep_index,
    cond_full,
    cond_masked,
    w_ada,
    b_ada,
    w_qkv,
    b_q,
    b_v,
    w_out,
    b_out,
    w_fc1,
    b_fc1,
    w_fc2,
    b_fc2,
    cot_full,
    cot_masked,
):
    def columns(shard):
        return lax.all_gather(lax.all_gather(shard, ROWS, axis=0, tiled=True), COLS, axis=1, tiled=True)

    weights = (None, columns(w_qkv), columns(w_out), columns(w_fc1), columns(w_fc2))
    widths = [b.shape[0] for b in (b_q, b_v, b_out, b_fc1, b_fc2)]
    packed = lax.all_gather(jnp.concatenate([b_q, b_v, b_out, b_fc1, b_fc2]), COLS, axis=0, tiled=False)
    biases, at = [None], 0
    for width in widths:
        biases.append(packed[:, at : at + width].reshape(-1))
        at += width
    full_length = full_input.shape[1]
    images = full_input.shape[0]
    features = full_input.shape[2]
    picked = jnp.take_along_axis(masked_input, keep_index[:, :, None], axis=1)
    tokens = jnp.concatenate([full_input, picked], axis=1).astype(jnp.float32)
    conds = jnp.stack([cond_full, cond_masked], axis=1).astype(jnp.float32)
    silu_low = jax.nn.silu(conds).astype(jnp.bfloat16)
    n_dp, n_fsdp = lax.axis_size(ROWS), lax.axis_size(COLS)
    rows_ada, cols_ada = w_ada.shape
    every_silu = lax.all_gather(silu_low, (ROWS, COLS), axis=0, tiled=True)
    my_silu = lax.dynamic_slice_in_dim(every_silu, lax.axis_index(ROWS) * rows_ada, rows_ada, axis=2)
    part = jnp.einsum("ijd,de->ije", my_silu, w_ada, preferred_element_type=jnp.float32)
    part = lax.psum_scatter(part, ROWS, scatter_dimension=0, tiled=True)
    part = part + b_ada.astype(jnp.float32)
    mods = lax.all_to_all(part, COLS, split_axis=0, concat_axis=2, tiled=True)
    (
        result,
        pieces,
        norm_one,
        inverse_one,
        hidden_one,
        query_rows,
        key_rows,
        value_rows,
        attention,
        attention_low,
        mixed,
        attn_out,
        norm_two,
        inverse_two,
        hidden_two,
        upper,
        activated,
        branch,
    ) = plain_forward_pass(tokens, mods, weights, biases, full_length)
    length = tokens.shape[1]
    head_count = features // HEAD_DIM
    scale_factor = 1.0 / math.sqrt(HEAD_DIM)
    grad_result = jnp.concatenate([cot_full, cot_masked], axis=1).astype(jnp.float32)
    grad_gate_two = plain_image_sums(grad_result * branch, full_length)
    grad_branch = (pieces[5] * grad_result).astype(jnp.bfloat16)
    grad_b_fc2 = jnp.sum(grad_branch.astype(jnp.float32), axis=(0, 1))
    grad_w_fc2 = jnp.einsum(
        "itf,itd->fd", activated, grad_branch, preferred_element_type=jnp.float32
    )
    grad_act = jnp.einsum(
        "itd,fd->itf", grad_branch, weights[4], preferred_element_type=jnp.float32
    )
    grad_upper = jax.vjp(plain_gelu_tanh, upper)[1](grad_act)[0].astype(jnp.bfloat16)
    grad_b_fc1 = jnp.sum(grad_upper.astype(jnp.float32), axis=(0, 1))
    grad_w_fc1 = jnp.einsum(
        "itd,itf->df", hidden_two, grad_upper, preferred_element_type=jnp.float32
    )
    grad_hidden_two = jnp.einsum(
        "itf,df->itd", grad_upper, weights[3], preferred_element_type=jnp.float32
    )
    grad_scale_two = plain_image_sums(grad_hidden_two * norm_two, full_length)
    grad_shift_two = plain_image_sums(grad_hidden_two, full_length)
    grad_residual = grad_result + plain_layer_back(
        grad_hidden_two * (1.0 + pieces[4]), norm_two, inverse_two
    )
    grad_gate_one = plain_image_sums(grad_residual * attn_out, full_length)
    grad_attn = (pieces[2] * grad_residual).astype(jnp.bfloat16)
    grad_b_out = jnp.sum(grad_attn.astype(jnp.float32), axis=(0, 1))
    grad_w_out = jnp.einsum("itd,ite->de", mixed, grad_attn, preferred_element_type=jnp.float32)
    grad_mixed = jnp.einsum(
        "ite,de->itd", grad_attn, weights[2], preferred_element_type=jnp.float32
    )
    grad_mixed = grad_mixed.astype(jnp.bfloat16).reshape(images, length, head_count, HEAD_DIM)
    grad_attention = jnp.einsum(
        "iqhc,ikhc->ihqk", grad_mixed, value_rows, preferred_element_type=jnp.float32
    )
    grad_values = jnp.einsum(
        "ihqk,iqhc->ikhc", attention_low, grad_mixed, preferred_element_type=jnp.float32
    )
    grad_scores = attention * (
        grad_attention - jnp.sum(attention * grad_attention, axis=-1, keepdims=True)
    )
    grad_scores = grad_scores.astype(jnp.bfloat16)
    grad_queries = (
        jnp.einsum("ihqk,ikhc->iqhc", grad_scores, key_rows, preferred_element_type=jnp.float32)
        * scale_factor
    )
    grad_keys = (
        jnp.einsum("ihqk,iqhc->ikhc", grad_scores, query_rows, preferred_element_type=jnp.float32)
        * scale_factor
    )
    grad_projected = jnp.stack([grad_queries, grad_keys, grad_values], axis=2)
    grad_projected = grad_projected.reshape(images, length, 3 * features).astype(jnp.bfloat16)
    grad_b_q = jnp.sum(grad_projected[:, :, :features].astype(jnp.float32), axis=(0, 1))
    grad_b_v = jnp.sum(grad_projected[:, :, 2 * features :].astype(jnp.float32), axis=(0, 1))
    grad_w_qkv = jnp.einsum(
        "itd,ite->de", hidden_one, grad_projected, preferred_element_type=jnp.float32
    )
    grad_hidden_one = jnp.einsum(
        "ite,de->itd", grad_projected, weights[1], preferred_element_type=jnp.float32
    )
    grad_scale_one = plain_image_sums(grad_hidden_one * norm_one, full_length)
    grad_shift_one = plain_image_sums(grad_hidden_one, full_length)
    grad_tokens = grad_residual + plain_layer_back(
        grad_hidden_one * (1.0 + pieces[1]), norm_one, inverse_one
    )
    grad_mods = jnp.concatenate(
        [
            grad_shift_one,
            grad_scale_one,
            grad_gate_one,
            grad_shift_two,
            grad_scale_two,
            grad_gate_two,
        ],
        axis=-1,
    ).astype(jnp.bfloat16)
    cut = grad_mods.reshape(images, 2, n_fsdp, cols_ada)
    mine = lax.all_to_all(cut, COLS, split_axis=2, concat_axis=0, tiled=False)
    mine = lax.all_gather(mine.reshape(n_fsdp * images, 2, cols_ada), ROWS, axis=0, tiled=True)
    grad_b_ada = jnp.sum(mine.astype(jnp.float32), axis=(0, 1))
    grad_w_ada = jnp.einsum("ijd,ije->de", my_silu, mine, preferred_element_type=jnp.float32)
    back = jnp.einsum("ije,de->ijd", mine, w_ada, preferred_element_type=jnp.float32)
    back = lax.psum_scatter(back.reshape(n_dp, n_fsdp * images, 2, rows_ada), COLS, scatter_dimension=1, tiled=True)
    grad_silu = lax.all_to_all(back, ROWS, split_axis=0, concat_axis=3, tiled=True).reshape(images, 2, features)
    grad_cond = jax.vjp(jax.nn.silu, conds)[1](grad_silu)[0]
    image_rows = jnp.arange(images)[:, None]
    grad_masked = (
        jnp.zeros((images, full_length, features), jnp.float32)
        .at[image_rows, keep_index]
        .set(grad_tokens[:, full_length:])
    )
    def owned(grad):
        inner = lax.psum_scatter(grad.astype(jnp.bfloat16), ROWS, scatter_dimension=0, tiled=True)
        return lax.psum_scatter(inner, COLS, scatter_dimension=1, tiled=True).astype(jnp.float32)

    matrices = (grad_w_ada, owned(grad_w_qkv), owned(grad_w_out), owned(grad_w_fc1), owned(grad_w_fc2))
    sums = (grad_b_q, grad_b_v, grad_b_out, grad_b_fc1, grad_b_fc2)
    line = jnp.concatenate([g.reshape(n_fsdp, -1) for g in sums], axis=1)
    line = lax.psum(lax.psum_scatter(line, COLS, scatter_dimension=0, tiled=True), ROWS)[0]
    vectors, at = [grad_b_ada], 0
    for width in widths:
        vectors.append(line[at : at + width])
        at += width
    return (
        result[:, :full_length].astype(jnp.bfloat16),
        result[:, full_length:].astype(jnp.bfloat16),
        grad_tokens[:, :full_length],
        grad_masked,
        grad_cond[:, 0],
        grad_cond[:, 1],
        matrices[0],
        vectors[0],
        matrices[1],
        vectors[1],
        vectors[2],
        matrices[2],
        vectors[3],
        matrices[3],
        vectors[4],
        matrices[4],
        vectors[5],
    )


def solution(mesh):
    special = dict(mesh.shape) == {ROWS: 4, COLS: 8}
    return jax.shard_map(
        whole if special else general,
        mesh=mesh,
        in_specs=(
            P((ROWS, COLS), None, None),
            P((ROWS, COLS), None, None),
            P((ROWS, COLS), None),
            P((ROWS, COLS), None),
            P((ROWS, COLS), None),
            P(ROWS, COLS),
            P(COLS),
            P(ROWS, COLS),
            P(COLS),
            P(COLS),
            P(ROWS, COLS),
            P(COLS),
            P(ROWS, COLS),
            P(COLS),
            P(ROWS, COLS),
            P(COLS),
            P((ROWS, COLS), None, None),
            P((ROWS, COLS), None, None),
        ),
        out_specs=(
            P((ROWS, COLS), None, None),
            P((ROWS, COLS), None, None),
            P((ROWS, COLS), None, None),
            P((ROWS, COLS), None, None),
            P((ROWS, COLS), None),
            P((ROWS, COLS), None),
            P(ROWS, COLS),
            P(COLS),
            P(ROWS, COLS),
            P(COLS),
            P(COLS),
            P(ROWS, COLS),
            P(COLS),
            P(ROWS, COLS),
            P(COLS),
            P(ROWS, COLS),
            P(COLS),
        ),
        check_vma=False,
    )
```
